256 devices in a mesh: dp: 8 (over z), seq: 32 (over x, y, core).
Axes of the slice: x: 4, y: 4, z: 8, core: 2. Of those that a mesh axis runs over, the one named last changes fastest.
Arguments:
- query: bfloat16 [32768, 1024], P(('dp', 'seq')), may hold values from -6 to 6
- key: bfloat16 [32768, 1024], P(('dp', 'seq')), may hold values from -6 to 6
- value: bfloat16 [32768, 1024], P(('dp', 'seq')), may hold values from -6 to 6
- gate_u: bfloat16 [32768, 1024], P(('dp', 'seq')), may hold values from -6 to 6
- out_weight: bfloat16 [1024, 1024], replicated, may hold values from -0.1875 to 0.1875
- cotangent: bfloat16 [32768, 1024], P(('dp', 'seq')), may hold values from -6 to 6
- hist_lengths: int32 [8, 4], P('dp'), may hold values from 1 to 2048, 4096 in all within a row
Outputs:
- d_query: bfloat16 [32768, 1024], P(('dp', 'seq'))
- d_key: bfloat16 [32768, 1024], P(('dp', 'seq'))
- d_value: bfloat16 [32768, 1024], P(('dp', 'seq'))
- d_gate: bfloat16 [32768, 1024], P(('dp', 'seq'))
- d_weight: float32 [1024, 1024], P(('dp', 'seq'))
The draws below stay inside these ranges and needn't reach their ends.
Inputs may be any that keep to these rules, and one draw needn't show every extreme that they name: `hist_lengths`: row r lists the lengths of the histories packed in order into the 4096 tokens of group r; each row sums to 4096 and its longest history has exactly 2048 tokens.
All inputs are finite; a program needn't handle non-finite values.
Results may differ from the reference program's by a relative error of at most 0.018.
Values may be sent and summed in bfloat16 or wider, within the bound.
No kernel may reach another device: no remote copies, remote signals or barrier semaphores. Data moves between devices by JAX's collectives and lax.ppermute only.
A program may use at most 128 MiB of HBM per device.

```python
import math
import jax
import jax.numpy as jnp
import numpy as np
from jax import lax

HEADS = 16
HEAD_DIM = 64
D = 1024
USERS = 4
GROUP_TOK = 4096
TOKENS = 32768
N_DP = 8


def level_of(rng, dims, pieces, least, top_value):
    factor_of, own = 1.0, jax.random.fold_in(rng, 6)
    for axis_at, parts in pieces:
        steps = jnp.exp(jax.random.uniform(jax.random.fold_in(own, axis_at), (parts,), jnp.float32, least / len(pieces), top_value / len(pieces)))
        factor_of = factor_of * jnp.repeat(steps, dims[axis_at] // parts).reshape([-1 if axis == axis_at else 1 for axis in range(len(dims))])
    return factor_of


def profile(amount, total, limit, lean):
    loads = [(1 << 20) // math.isqrt(rank ** lean) + 1 for rank in range(2, amount + 1)]
    spare, given = total - limit - (amount - 1), [1] * (amount - 1)
    while spare > 0:
        free = [i for i in range(amount - 1) if given[i] < limit]
        pool, budget = sum([loads[i] for i in free]), spare
        for i in free:
            extra = min(limit - given[i], max(1, budget * loads[i] // pool), spare)
            given[i] = given[i] + extra
            spare = spare - extra
    return np.array([limit] + given)


def uneven(key, number_of, total, bound, skew):
    if number_of == 2:
        one = jax.random.randint(key, (), max(1, total - bound), min(bound, total - 1) + 1)
        return jnp.stack([one, total - one])
    lengths = jnp.asarray(profile(number_of, total, bound, skew), jnp.int32)
    pairs = (number_of - 1) // 2
    giver, sink = lengths[1:1 + 2 * pairs:2], lengths[2:2 + 2 * pairs:2]
    room = jnp.minimum(giver - 1, bound - sink)
    shifted = jax.random.randint(jax.random.fold_in(key, 1), (pairs,), 0, 1 << 20) % (room + 1)
    lengths = lengths.at[1:1 + 2 * pairs:2].set(giver - shifted).at[2:2 + 2 * pairs:2].set(sink + shifted)
    return lengths[jax.random.permutation(jax.random.fold_in(key, 2), number_of)]


def centred(own_key, shape, scale, reach, cuts=(), held_as=jnp.bfloat16):
    entries = scale * jax.random.normal(own_key, shape, jnp.float32)
    if cuts:
        entries = entries * level_of(own_key, shape, cuts, -0.22, 0.18)
    return jnp.clip(entries, -reach, reach).astype(held_as)


def setup_inputs(seed: int = 0) -> dict:
    seeds = jax.random.split(jax.random.key(seed), 8)
    return {
        "query": centred(seeds[0], (TOKENS, D), 1.0, 6.0, ((0, 256),)),
        "key": centred(seeds[1], (TOKENS, D), 1.0, 6.0, ((0, 256),)),
        "value": centred(seeds[2], (TOKENS, D), 1.0, 6.0, ((0, 256),)),
        "gate_u": centred(seeds[3], (TOKENS, D), 1.0, 6.0, ((0, 256),)),
        "out_weight": centred(seeds[4], (D, D), D ** -0.5, 0.1875),
        "cotangent": centred(seeds[5], (TOKENS, D), 1.0, 6.0, ((0, 256),)),
        "hist_lengths": jax.vmap(lambda own: uneven(own, USERS, GROUP_TOK, GROUP_TOK // 2, 2))(jax.random.split(seeds[6], N_DP)).reshape((N_DP, USERS)).astype(jnp.int32),
    }


def history_starts(lengths_row, all_tokens):
    ends = jnp.cumsum(lengths_row).astype(jnp.int32)
    positions = jnp.arange(all_tokens, dtype=jnp.int32)
    passed = ends[None, :] <= positions[:, None]
    return lax.optimization_barrier(jnp.sum(jnp.where(passed, lengths_row[None, :], 0), axis=1)).astype(jnp.int32)

def live_mask(query_pos, query_start, key_first, key_count):
    key_pos = key_first + jnp.arange(key_count, dtype=jnp.int32)
    return (key_pos[None, :] >= query_start[:, None]) & (key_pos[None, :] <= query_pos[:, None])

def forward_group(query_g, key_g, value_g, lengths_row):
    all_tokens = query_g.shape[0]
    queries = query_g.reshape(all_tokens, HEADS, HEAD_DIM).astype(jnp.float32)
    keys = key_g.reshape(all_tokens, HEADS, HEAD_DIM).astype(jnp.float32)
    values = value_g.reshape(all_tokens, HEADS, HEAD_DIM).astype(jnp.float32)
    starts = history_starts(lengths_row, all_tokens)
    q_block = min(512, all_tokens)
    k_block = min(512, all_tokens)
    factor = 1.0 / math.sqrt(HEAD_DIM)

    def one_block(block_id, result):
        q_here = lax.dynamic_slice_in_dim(queries, block_id * q_block, q_block, 0)
        pos_here = (block_id * q_block + jnp.arange(q_block, dtype=jnp.int32)).astype(jnp.int32)
        start_here = starts[pos_here]
        first_tile = start_here[0] // k_block
        end_tile = pos_here[q_block - 1] // k_block + 1

        def one_tile(tile_id, running):
            k_here = lax.dynamic_slice_in_dim(keys, tile_id * k_block, k_block, 0)
            v_here = lax.dynamic_slice_in_dim(values, tile_id * k_block, k_block, 0)
            live = live_mask(pos_here, start_here, tile_id * k_block, k_block)
            scores = jnp.einsum('qhd,khd->hqk', q_here, k_here) * factor
            weights = jnp.where(live[None], jax.nn.silu(scores), 0.0).astype(jnp.bfloat16).astype(jnp.float32)
            return running + jnp.einsum('hqk,khd->qhd', weights, v_here)
        summed = lax.fori_loop(first_tile, end_tile, one_tile, jnp.zeros((q_block, HEADS, HEAD_DIM), jnp.float32))
        return lax.dynamic_update_slice_in_dim(result, summed.reshape(q_block, HEADS * HEAD_DIM).astype(jnp.bfloat16), block_id * q_block, 0)
    return lax.fori_loop(0, all_tokens // q_block, one_block, jnp.zeros((all_tokens, HEADS * HEAD_DIM), jnp.bfloat16))

def backward_group(query_g, key_g, value_g, grad_g, lengths_row):
    all_tokens = query_g.shape[0]
    queries = query_g.reshape(all_tokens, HEADS, HEAD_DIM).astype(jnp.float32)
    keys = key_g.reshape(all_tokens, HEADS, HEAD_DIM).astype(jnp.float32)
    values = value_g.reshape(all_tokens, HEADS, HEAD_DIM).astype(jnp.float32)
    grads = grad_g.reshape(all_tokens, HEADS, HEAD_DIM).astype(jnp.float32)
    starts = history_starts(lengths_row, all_tokens)
    q_block = min(512, all_tokens)
    k_block = min(512, all_tokens)
    factor = 1.0 / math.sqrt(HEAD_DIM)

    def one_block(block_id, carry):
        dq_all, dk_all, dv_all = carry
        q_here = lax.dynamic_slice_in_dim(queries, block_id * q_block, q_block, 0)
        g_here = lax.dynamic_slice_in_dim(grads, block_id * q_block, q_block, 0)
        pos_here = (block_id * q_block + jnp.arange(q_block, dtype=jnp.int32)).astype(jnp.int32)
        start_here = starts[pos_here]
        first_tile = start_here[0] // k_block
        end_tile = pos_here[q_block - 1] // k_block + 1

        def one_tile(tile_id, state):
            dq_here, dk_run, dv_run = state
            k_here = lax.dynamic_slice_in_dim(keys, tile_id * k_block, k_block, 0)
            v_here = lax.dynamic_slice_in_dim(values, tile_id * k_block, k_block, 0)
            live = live_mask(pos_here, start_here, tile_id * k_block, k_block)[None]
            scores = jnp.einsum('qhd,khd->hqk', q_here, k_here) * factor
            sigma = jax.nn.sigmoid(scores)
            weights = jnp.where(live, jax.nn.silu(scores), 0.0).astype(jnp.bfloat16).astype(jnp.float32)
            d_probs = jnp.einsum('qhd,khd->hqk', g_here, v_here)
            d_scores = jnp.where(live, d_probs * sigma * (1.0 + scores * (1.0 - sigma)), 0.0) * factor
            d_scores = d_scores.astype(jnp.bfloat16).astype(jnp.float32)
            dv_tile = jnp.einsum('hqk,qhd->khd', weights, g_here)
            dk_tile = jnp.einsum('hqk,qhd->khd', d_scores, q_here)
            dq_here = dq_here + jnp.einsum('hqk,khd->qhd', d_scores, k_here)
            old_k = lax.dynamic_slice_in_dim(dk_run, tile_id * k_block, k_block, 0)
            old_v = lax.dynamic_slice_in_dim(dv_run, tile_id * k_block, k_block, 0)
            dk_run = lax.dynamic_update_slice_in_dim(dk_run, old_k + dk_tile, tile_id * k_block, 0)
            dv_run = lax.dynamic_update_slice_in_dim(dv_run, old_v + dv_tile, tile_id * k_block, 0)
            return (dq_here, dk_run, dv_run)
        start_state = (jnp.zeros((q_block, HEADS, HEAD_DIM), jnp.float32), dk_all, dv_all)
        dq_here, dk_all, dv_all = lax.fori_loop(first_tile, end_tile, one_tile, start_state)
        dq_all = lax.dynamic_update_slice_in_dim(dq_all, dq_here, block_id * q_block, 0)
        return (dq_all, dk_all, dv_all)
    empty = jnp.zeros((all_tokens, HEADS, HEAD_DIM), jnp.float32)
    dq_all, dk_all, dv_all = lax.fori_loop(0, all_tokens // q_block, one_block, (empty, empty, empty))
    width = HEADS * HEAD_DIM
    return (dq_all.reshape(all_tokens, width), dk_all.reshape(all_tokens, width), dv_all.reshape(all_tokens, width))

def reference(query, key, value, gate_u, out_weight, cotangent, hist_lengths):
    width = HEADS * HEAD_DIM
    grouped = lambda array: array.reshape(N_DP, GROUP_TOK, width)
    attn = lax.map(lambda items: forward_group(*items), (grouped(query), grouped(key), grouped(value), hist_lengths))
    attn = attn.reshape(TOKENS, width).astype(jnp.float32)
    center = attn - lax.optimization_barrier(jnp.mean(attn, axis=1, keepdims=True))
    rstd = lax.rsqrt(lax.optimization_barrier(jnp.mean(center * center, axis=1, keepdims=True)) + 1e-05)
    normed = center * rstd
    gated = (normed * gate_u.astype(jnp.float32)).astype(jnp.bfloat16)
    d_gated = jnp.dot(cotangent, out_weight.T, preferred_element_type=jnp.float32)
    d_weight = jnp.dot(gated.T, cotangent, preferred_element_type=jnp.float32) * (1.0 / math.sqrt(TOKENS))
    d_gate = (d_gated * normed).astype(jnp.bfloat16)
    grad_in = d_gated * gate_u.astype(jnp.float32)
    d_attn = rstd * (grad_in - lax.optimization_barrier(jnp.mean(grad_in, axis=1, keepdims=True)) - normed * lax.optimization_barrier(jnp.mean(grad_in * normed, axis=1, keepdims=True)))
    d_attn = d_attn.astype(jnp.bfloat16)
    d_query, d_key, d_value = lax.map(lambda items: backward_group(*items), (grouped(query), grouped(key), grouped(value), grouped(d_attn), hist_lengths))
    d_query = d_query.reshape(TOKENS, width).astype(jnp.bfloat16)
    d_key = d_key.reshape(TOKENS, width).astype(jnp.bfloat16)
    d_value = d_value.reshape(TOKENS, width).astype(jnp.bfloat16)
    return (d_query, d_key, d_value, d_gate, d_weight)
```

```python
import functools
import math

import jax
import jax.numpy as jnp
from jax import lax
from jax.experimental import pallas as pl
from jax.experimental.pallas import tpu as pltpu
from jax.sharding import Mesh, PartitionSpec as P

HEADS = 16
HEAD_DIM = 64
N_BLOCKS = 16
BLOCK = 128
HALF = 2048
TILE = 256
N_TILES = HALF // TILE
STATS = 6
CHIP = ("x", "y")
SWAP = ((0, 1), (1, 0))
BF16 = jnp.bfloat16
F32 = jnp.float32


def dot(a, b):
    return lax.dot_general(a, b, (((1,), (0,)), ((), ())), preferred_element_type=F32)


def dot_nt(a, b):
    return lax.dot_general(a, b, (((1,), (1,)), ((), ())), preferred_element_type=F32)


def start_of(slot, end1, end2):
    return jnp.where(slot < end1, 0, jnp.where(slot < end2, end1, end2))


def tile_range(tile, turn, end1, end2):
    turn_tile = turn // TILE
    split = (turn % TILE) > 0
    cyclic = lax.rem(tile - turn_tile + N_TILES, N_TILES) + 1
    cyclic = jnp.where((tile == turn_tile) & split, N_TILES, cyclic)
    first = start_of(tile * TILE, end1, end2) // TILE
    turned = turn > 0
    return jnp.where(turned, turn_tile, first), jnp.where(turned, cyclic, tile - first + 1)


def live_of(q_tile, k_tile, turn, end1, end2):
    q_slot = q_tile * TILE + lax.broadcasted_iota(jnp.int32, (1, TILE), 1)
    k_slot = k_tile * TILE + lax.broadcasted_iota(jnp.int32, (TILE, 1), 0)
    q_order = (q_slot - turn) & (HALF - 1)
    k_order = (k_slot - turn) & (HALF - 1)
    return (k_order <= q_order) & (k_order >= start_of(q_slot, end1, end2))


def sigmoid(s):
    return pl.reciprocal(1.0 + jnp.exp(-s), approx=True)


def forward_kernel(meta_ref, own_ref, other_ref, x_ref, attn_ref, stat_ref, k_ref):
    core, turn, end1, end2 = (meta_ref[i] for i in range(4))
    for b in range(N_BLOCKS):
        mine, theirs = own_ref[b // 2], other_ref[b // 2]
        here = jnp.where(core == b % 2, mine, theirs)
        x_ref[:, b * BLOCK : (b + 1) * BLOCK] = here
        k_ref[b * BLOCK : (b + 1) * BLOCK, :] = here[64:128, :].T

    def one_tile(tile, _):
        q_cols = pl.ds(pl.multiple_of(tile * TILE, TILE), TILE)
        q_t = x_ref[0:64, q_cols] * BF16(0.125)
        first, count = tile_range(tile, turn, end1, end2)

        def step(at, acc):
            k_tile = lax.rem(first + at, N_TILES)
            k_cols = pl.ds(pl.multiple_of(k_tile * TILE, TILE), TILE)
            s = dot(k_ref[k_cols, :], q_t)
            live = live_of(tile, k_tile, turn, end1, end2)
            w = jnp.where(live, s * sigmoid(s), 0.0).astype(BF16)
            return acc + dot(x_ref[128:192, k_cols], w)

        acc = lax.fori_loop(0, count, step, jnp.zeros((HEAD_DIM, TILE), F32))
        attn = acc.astype(BF16)
        attn_f = attn.astype(F32)
        g = x_ref[192:256, q_cols].astype(F32)
        mean = jnp.mean(attn_f, axis=0, keepdims=True)
        centre = attn_f - mean
        rows = (
            mean,
            jnp.sum(centre * g, axis=0, keepdims=True),
            jnp.sum(centre * centre, axis=0, keepdims=True),
            jnp.sum(g, axis=0, keepdims=True),
        )
        for b in range(TILE // BLOCK):
            block = tile * (TILE // BLOCK) + b
            cols = slice(b * BLOCK, (b + 1) * BLOCK)
            attn_ref[block] = attn[:, cols]
            for i, row in enumerate(rows):
                stat_ref[i, pl.ds(block, 1), :] = row[:, cols]
        return 0

    lax.fori_loop(0, N_TILES, one_tile, 0)


def backward_kernel(
    meta_ref, x_ref, attn_ref, stat_ref, out_ref, qn_ref, kn_ref, vn_ref, dn_ref, dt_ref, dk_ref, dv_ref
):
    turn, end1, end2 = (meta_ref[i] for i in range(1, 4))
    stat = stat_ref[...].astype(F32)
    mean_h = stat[:, 0] + stat[:, 1]
    mean = jnp.mean(mean_h, axis=0)
    off = mean_h - mean[None]
    square = jnp.sum(stat[:, 4] + HEAD_DIM * off * off, axis=0)
    rstd = lax.rsqrt(square * (1.0 / 1024) + 1e-05)
    g_sum = stat[:, 5]
    g_mean = jnp.sum(g_sum, axis=0) * (1.0 / 1024)
    both = jnp.sum(stat[:, 2] + stat[:, 3] + off * g_sum, axis=0) * rstd * (1.0 / 1024)
    for b in range(N_BLOCKS):
        cols = slice(b * BLOCK, (b + 1) * BLOCK)
        here = x_ref[:, cols]
        r = rstd[b : b + 1]
        normed = (attn_ref[b].astype(F32) - mean[b : b + 1]) * r
        d = (r * (here[192:256].astype(F32) - g_mean[b : b + 1] - normed * both[b : b + 1])).astype(BF16)
        dt_ref[:, cols] = d
        dn_ref[cols, :] = d.T
        qn_ref[cols, :] = here[0:64].T * BF16(0.125)
        kn_ref[cols, :] = here[64:128].T
        vn_ref[cols, :] = here[128:192].T
    dk_ref[...] = jnp.zeros_like(dk_ref)
    dv_ref[...] = jnp.zeros_like(dv_ref)

    def one_tile(tile, _):
        q_cols = pl.ds(pl.multiple_of(tile * TILE, TILE), TILE)
        q_t = x_ref[0:64, q_cols] * BF16(0.125)
        d_t = dt_ref[:, q_cols]
        q_n = qn_ref[q_cols, :]
        d_n = dn_ref[q_cols, :]
        first, count = tile_range(tile, turn, end1, end2)

        def step(at, acc):
            k_tile = lax.rem(first + at, N_TILES)
            k_cols = pl.ds(pl.multiple_of(k_tile * TILE, TILE), TILE)
            s = dot(kn_ref[k_cols, :], q_t)
            d_p = dot(vn_ref[k_cols, :], d_t)
            live = live_of(tile, k_tile, turn, end1, end2)
            sigma = jnp.where(live, sigmoid(s), 0.0)
            silu = s * sigma
            w = silu.astype(BF16)
            d_s = (d_p * (sigma + silu * (1.0 - sigma))).astype(BF16)
            dv_ref[k_cols, :] += dot(w, d_n)
            dk_ref[k_cols, :] += dot(d_s, q_n)
            return acc + dot(x_ref[64:128, k_cols], d_s)

        acc = lax.fori_loop(0, count, step, jnp.zeros((HEAD_DIM, TILE), F32))
        dq = (acc * 0.125).astype(BF16)
        for b in range(TILE // BLOCK):
            out_ref[tile * (TILE // BLOCK) + b, 0:64, :] = dq[:, b * BLOCK : (b + 1) * BLOCK]
        return 0

    lax.fori_loop(0, N_TILES, one_tile, 0)
    for b in range(N_BLOCKS):
        cols = slice(b * BLOCK, (b + 1) * BLOCK)
        out_ref[b, 64:128, :] = dk_ref[cols, :].T.astype(BF16)
        out_ref[b, 128:192, :] = dv_ref[cols, :].T.astype(BF16)


def vmem(n=1):
    return [pl.BlockSpec(memory_space=pltpu.VMEM)] * n


PARAMS = pltpu.CompilerParams(vmem_limit_bytes=48 * 1024 * 1024)


def attend_forward(meta, own, other):
    return pl.pallas_call(
        forward_kernel,
        out_shape=(
            jax.ShapeDtypeStruct((256, HALF), BF16),
            jax.ShapeDtypeStruct((N_BLOCKS, HEAD_DIM, BLOCK), BF16),
            jax.ShapeDtypeStruct((4, N_BLOCKS, BLOCK), F32),
        ),
        in_specs=[pl.BlockSpec(memory_space=pltpu.SMEM)] + vmem(2),
        out_specs=tuple(vmem(3)),
        scratch_shapes=[pltpu.VMEM((HALF, HEAD_DIM), BF16)],
        compiler_params=PARAMS,
        name="attend_forward",
    )(meta, own, other)


def attend_backward(meta, x, attn, stat):
    return pl.pallas_call(
        backward_kernel,
        out_shape=jax.ShapeDtypeStruct((N_BLOCKS, 192, BLOCK), BF16),
        in_specs=[pl.BlockSpec(memory_space=pltpu.SMEM)] + vmem(3),
        out_specs=vmem()[0],
        scratch_shapes=[pltpu.VMEM((HALF, HEAD_DIM), BF16)] * 4
        + [pltpu.VMEM((HEAD_DIM, HALF), BF16)]
        + [pltpu.VMEM((HALF, HEAD_DIM), F32)] * 2,
        compiler_params=PARAMS,
        name="attend_backward",
    )(meta, x, attn, stat)


def split_two(x):
    high = x.astype(BF16)
    return high, (x - high.astype(F32)).astype(BF16)


def on_device(query, key, value, gate_u, out_weight, cotangent, hist_lengths):
    core = lax.axis_index("core")
    lengths = hist_lengths[0]

    ends = jnp.cumsum(lengths)
    long_at = jnp.argmax(lengths)
    begin = ends[long_at] - HALF
    at = jnp.arange(3, dtype=jnp.int32)
    other_ends = jnp.cumsum(lengths[at + (at >= long_at)])
    turn = jnp.where(core == 0, begin & (HALF - 1), 0)
    end1 = jnp.where(core == 0, HALF, other_ends[0])
    end2 = jnp.where(core == 0, HALF, other_ends[1])
    meta = jnp.stack([core, turn, end1, end2]).astype(jnp.int32)

    slots = (2 * jnp.arange(8, dtype=jnp.int32)[:, None] + core) * BLOCK + jnp.arange(BLOCK, dtype=jnp.int32)
    low_mine = ((slots >= begin) == (core == 0))[:, None, :]

    def swap(x):
        return lax.ppermute(x, "core", SWAP)

    def chips(x):
        return lax.all_to_all(x, CHIP, 0, 0, tiled=True)

    d_gated_t = dot_nt(out_weight, cotangent)
    gate_t = gate_u.T.astype(F32)
    g_t = (d_gated_t * gate_t).astype(BF16)
    send = jnp.stack([query.T, key.T, value.T, g_t]).reshape(4, HEADS, HEAD_DIM, BLOCK)
    send = send.transpose(1, 0, 2, 3).reshape(HEADS, 256, BLOCK)
    got = chips(send)
    low, high = got[:8], got[8:]
    own = jnp.where(low_mine, low, high)
    other = swap(jnp.where(low_mine, high, low))
    x, attn, stat = attend_forward(meta, own, other)

    mean_hi, mean_lo = split_two(stat[0])
    both_hi, both_lo = split_two(stat[1])
    stat = jnp.stack([mean_hi, mean_lo, both_hi, both_lo, stat[2].astype(BF16), stat[3].astype(BF16)])

    def to_owners(blocks):
        pairs = blocks.reshape((8, 2) + blocks.shape[1:])
        mine = lax.dynamic_index_in_dim(pairs, core, 1, keepdims=False)
        theirs = swap(lax.dynamic_index_in_dim(pairs, 1 - core, 1, keepdims=False))
        return jnp.concatenate([jnp.where(low_mine, mine, theirs), jnp.where(low_mine, theirs, mine)], axis=0)

    stat = jnp.broadcast_to(stat.reshape(1, STATS * N_BLOCKS, BLOCK), (HEADS, STATS * N_BLOCKS, BLOCK))
    got = chips(jnp.concatenate([to_owners(attn), stat], axis=1))
    stat = got[:, 64:].reshape(HEADS, STATS, N_BLOCKS, BLOCK)
    grads = attend_backward(meta, x, attn, stat)

    attn_t = got[:, :64].reshape(1024, BLOCK).astype(F32)
    center = attn_t - jnp.mean(attn_t, axis=0, keepdims=True)
    rstd = lax.rsqrt(jnp.mean(center * center, axis=0, keepdims=True) + 1e-05)
    normed = center * rstd
    gated_t = (normed * gate_t).astype(BF16)
    d_gate = (d_gated_t * normed).astype(BF16).T

    all_cot = lax.all_gather(cotangent, "dp", axis=0, tiled=True)
    got_gated = lax.all_to_all(gated_t, "dp", 0, 0, tiled=True).reshape(8, BLOCK, BLOCK)
    gated_all = got_gated.transpose(1, 0, 2).reshape(BLOCK, 8 * BLOCK)
    part = dot(gated_all, all_cot) * (1.0 / math.sqrt(32768))
    part = part.reshape(HEADS, 2, 4, 1024)
    part = lax.dynamic_index_in_dim(part, core, 1, keepdims=False) + swap(
        lax.dynamic_index_in_dim(part, 1 - core, 1, keepdims=False)
    )
    hi, lo = split_two(part)
    parts = jnp.concatenate([hi.reshape(HEADS, 32, BLOCK), lo.reshape(HEADS, 32, BLOCK)], axis=1)

    got = chips(jnp.concatenate([to_owners(grads), parts], axis=1))

    def tokens(rows):
        return rows.reshape(1024, BLOCK).T

    d_query, d_key, d_value = (tokens(got[:, 64 * i : 64 * (i + 1)]) for i in range(3))
    d_weight = jnp.sum(got[:, 192:224].astype(F32) + got[:, 224:256].astype(F32), axis=0).reshape(4, 1024)
    return d_query, d_key, d_value, d_gate, d_weight


def solution(mesh):
    axes = ("dp", "x", "y", "core")
    inner = Mesh(mesh.devices.reshape(8, 4, 4, 2), axes)
    rows = P(axes, None)
    return jax.shard_map(
        on_device,
        mesh=inner,
        in_specs=(rows, rows, rows, rows, P(), rows, P("dp", None)),
        out_specs=(rows, rows, rows, rows, rows),
        check_vma=False,
    )
```

```python
import math

import jax
import jax.numpy as jnp
from jax import lax
from jax.experimental import pallas as pl
from jax.experimental.pallas import tpu as pltpu
from jax.sharding import Mesh, PartitionSpec as P

HEADS = 16
HEAD_DIM = 64
WIDTH = HEADS * HEAD_DIM
N_BLOCKS = 16
BLOCK = 128
HALF = N_BLOCKS * BLOCK
SUB = 256
F_TILE = 2048
B_TILE = 1024
STATS = 5
CHIP = ("x", "y")
SWAP = ((0, 1), (1, 0))
BF16 = jnp.bfloat16
F32 = jnp.float32


def dot(a, b):
    return lax.dot_general(a, b, (((1,), (0,)), ((), ())), preferred_element_type=F32)


def dot_nt(a, b):
    return lax.dot_general(a, b, (((1,), (1,)), ((), ())), preferred_element_type=F32)


def sigmoid(s):
    return pltpu.reciprocal(1.0 + jnp.exp(-s), approx=True)


def lanes():
    return lax.broadcasted_iota(jnp.int32, (1, BLOCK), 1)


def place_of(place_ref):
    first, second, third = (place_ref[i] for i in range(3))
    core = place_ref[4]
    is_first, is_second = first == HALF, second == HALF
    begin = jnp.where(is_first, 0, jnp.where(is_second, first, first + second + jnp.where(third == HALF, 0, third)))
    end1 = jnp.where(is_first, second, first)
    end2 = end1 + jnp.where(is_first | is_second, third, second)
    turn = jnp.where(core == 0, begin & (HALF - 1), 0)
    return core, begin, turn, jnp.where(core == 0, HALF, end1), jnp.where(core == 0, HALF, end2)


def low_is_mine(j, core, begin):
    return ((2 * j + core) * BLOCK + lanes() >= begin) == (core == 0)


def live_of(q_at, k_at, end1, end2, diagonal):
    q_place = q_at + lax.broadcasted_iota(jnp.int32, (1, SUB), 1)
    k_place = k_at + lax.broadcasted_iota(jnp.int32, (SUB, 1), 0)
    start = jnp.where(q_place < end1, 0, jnp.where(q_place < end2, end1, end2))
    live = k_place >= start
    return live & (k_place <= q_place) if diagonal else live


def below(n_tiles, tile):
    n_sub = tile // SUB
    for i in range(n_tiles):
        for j in range(i + 1):
            subs = [(q, k) for q in range(n_sub) for k in range(n_sub) if j < i or k <= q]
            yield i * tile, j * tile, subs


def forward_kernel(
    place_ref, got_ref, other_ref, x_ref, attn_ref, mine_ref, theirs_ref, stat_ref, k_ref, slot_ref, stats_ref
):
    core, begin, turn, end1, end2 = place_of(place_ref)
    whole, rest = turn // BLOCK, turn % BLOCK
    lane = lanes()
    for b in range(N_BLOCKS):
        j = b // 2
        mine = jnp.where(low_is_mine(j, core, begin), got_ref[j], got_ref[8 + j])
        here = jnp.where(core == b % 2, mine, other_ref[j])
        slot_ref[b] = pltpu.roll(here.astype(F32), lax.rem(BLOCK - rest, BLOCK), 1)
    for b in range(N_BLOCKS):
        first, second = slot_ref[lax.rem(b + whole, N_BLOCKS)], slot_ref[lax.rem(b + whole + 1, N_BLOCKS)]
        here = jnp.where(lane < BLOCK - rest, first, second)
        x_ref[0:64, b * BLOCK : (b + 1) * BLOCK] = (here[0:64] * 0.125).astype(BF16)
        x_ref[64:256, b * BLOCK : (b + 1) * BLOCK] = here[64:256].astype(BF16)
        k_ref[b * BLOCK : (b + 1) * BLOCK, :] = here[64:128].astype(BF16).T

    for q_at, k_at, subs in below(HALF // F_TILE, F_TILE):
        weights = {}
        for q, k in subs:
            q_sub, k_sub = q_at + q * SUB, k_at + k * SUB
            s = dot(k_ref[k_sub : k_sub + SUB, :], x_ref[0:64, q_sub : q_sub + SUB])
            live = live_of(q_sub, k_sub, end1, end2, q_sub == k_sub)
            weights[q, k] = jnp.where(live, s * sigmoid(s), 0.0).astype(BF16)
        for q in range(F_TILE // SUB):
            q_sub = q_at + q * SUB
            acc = jnp.zeros((HEAD_DIM, SUB), F32)
            for k in range(F_TILE // SUB):
                if (q, k) in weights:
                    k_sub = k_at + k * SUB
                    acc += dot(x_ref[128:192, k_sub : k_sub + SUB], weights[q, k])
            attn_ref[:, q_sub : q_sub + SUB] = acc.astype(BF16)

    turned = []
    for b in range(N_BLOCKS):
        cols = slice(b * BLOCK, (b + 1) * BLOCK)
        attn = attn_ref[:, cols].astype(F32)
        g = x_ref[192:256, cols].astype(F32)
        mean = jnp.mean(attn, axis=0, keepdims=True)
        centre = attn - mean
        both = jnp.sum(centre * g, axis=0, keepdims=True)
        mean_hi = mean.astype(BF16).astype(F32)
        square = jnp.sum(centre * centre, axis=0, keepdims=True)
        total = jnp.sum(g, axis=0, keepdims=True)
        for i, row in enumerate((mean_hi, mean - mean_hi, both, square, total)):
            stats_ref[i * N_BLOCKS + b : i * N_BLOCKS + b + 1, :] = row
        turned.append(attn)
    stat_ref[...] = stats_ref[...].astype(BF16)
    turn_out(turned, turn, core, slot_ref, mine_ref, theirs_ref)


def turn_out(blocks, turn, core, slot_ref, mine_ref, theirs_ref):
    whole, rest = turn // BLOCK, turn % BLOCK
    rows = blocks[0].shape[0]
    for b, block in enumerate(blocks):
        slot_ref[b, 0:rows, :] = pltpu.roll(block, rest, 1)
    from_this = lanes() >= rest
    for j in range(8):
        pair = []
        for b in (2 * j, 2 * j + 1):
            this = slot_ref[lax.rem(b - whole + N_BLOCKS, N_BLOCKS), 0:rows, :]
            last = slot_ref[lax.rem(b - whole + N_BLOCKS - 1, N_BLOCKS), 0:rows, :]
            pair.append(jnp.where(from_this, this, last).astype(BF16))
        mine_ref[j] = jnp.where(core == 0, pair[0], pair[1])
        theirs_ref[j] = jnp.where(core == 0, pair[1], pair[0])


def backward_kernel(
    place_ref, x_ref, attn_ref, got_ref, mine_ref, theirs_ref,
    qn_ref, kn_ref, vn_ref, dn_ref, dt_ref, dq_ref, dk_ref, dv_ref, slot_ref,
):
    core, _, turn, end1, end2 = place_of(place_ref)
    stat = got_ref[:, 64 : 64 + STATS * N_BLOCKS, :].astype(F32).reshape(HEADS, STATS, N_BLOCKS, BLOCK)
    mean_h = stat[:, 0] + stat[:, 1]
    mean = jnp.mean(mean_h, axis=0)
    off = mean_h - mean[None]
    square = jnp.sum(stat[:, 3] + HEAD_DIM * off * off, axis=0)
    rstd = lax.rsqrt(square * (1.0 / WIDTH) + 1e-05)
    g_sum = stat[:, 4]
    g_mean = jnp.sum(g_sum, axis=0) * (1.0 / WIDTH)
    both = jnp.sum(stat[:, 2] + off * g_sum, axis=0) * rstd * (1.0 / WIDTH)
    for b in range(N_BLOCKS):
        cols = slice(b * BLOCK, (b + 1) * BLOCK)
        here = x_ref[:, cols]
        r = rstd[b : b + 1]
        normed = (attn_ref[:, cols].astype(F32) - mean[b : b + 1]) * r
        d = (r * (here[192:256].astype(F32) - g_mean[b : b + 1] - normed * both[b : b + 1])).astype(BF16)
        dt_ref[:, cols] = d
        dn_ref[cols, :] = d.T
        qn_ref[cols, :] = here[0:64].T
        kn_ref[cols, :] = here[64:128].T
        vn_ref[cols, :] = here[128:192].T

    for q_at, k_at, subs in below(HALF // B_TILE, B_TILE):
        made = {}
        for q, k in subs:
            q_cols = slice(q_at + q * SUB, q_at + (q + 1) * SUB)
            k_cols = slice(k_at + k * SUB, k_at + (k + 1) * SUB)
            s = dot(kn_ref[k_cols, :], x_ref[0:64, q_cols])
            d_p = dot(vn_ref[k_cols, :], dt_ref[:, q_cols])
            live = live_of(q_cols.start, k_cols.start, end1, end2, q_cols.start == k_cols.start)
            sigma = jnp.where(live, sigmoid(s), 0.0)
            silu = s * sigma
            made[q, k] = silu.astype(BF16), (d_p * (sigma + silu * (1.0 - sigma))).astype(BF16)
        for k in range(B_TILE // SUB):
            k_cols = slice(k_at + k * SUB, k_at + (k + 1) * SUB)
            d_v, d_k = [], []
            for q in range(B_TILE // SUB):
                if (q, k) in made:
                    q_cols = slice(q_at + q * SUB, q_at + (q + 1) * SUB)
                    d_v.append(dot(made[q, k][0], dn_ref[q_cols, :]))
                    d_k.append(dot(made[q, k][1], qn_ref[q_cols, :]))
            if q_at == k_at:
                dv_ref[k_cols, :], dk_ref[k_cols, :] = sum(d_v), sum(d_k)
            else:
                dv_ref[k_cols, :] += sum(d_v)
                dk_ref[k_cols, :] += sum(d_k)
        for q in range(B_TILE // SUB):
            q_cols = slice(q_at + q * SUB, q_at + (q + 1) * SUB)
            d_q = []
            for k in range(B_TILE // SUB):
                if (q, k) in made:
                    d_q.append(dot(x_ref[64:128, k_at + k * SUB : k_at + (k + 1) * SUB], made[q, k][1]))
            if k_at == 0:
                dq_ref[:, q_cols] = sum(d_q)
            else:
                dq_ref[:, q_cols] += sum(d_q)

    turned = []
    for b in range(N_BLOCKS):
        cols = slice(b * BLOCK, (b + 1) * BLOCK)
        turned.append(jnp.concatenate([dq_ref[:, cols] * 0.125, dk_ref[cols, :].T, dv_ref[cols, :].T], axis=0))
    turn_out(turned, turn, core, slot_ref, mine_ref, theirs_ref)


def prepare_kernel(q_ref, k_ref, v_ref, u_ref, cot_ref, w_ref, send_ref, ut_ref, dg_ref):
    d_gated = dot_nt(w_ref[...], cot_ref[...])
    u_t = u_ref[...].T
    dg_ref[...] = d_gated
    ut_ref[...] = u_t
    g_t = (d_gated * u_t.astype(F32)).astype(BF16)
    for i, rows in enumerate((q_ref[...].T, k_ref[...].T, v_ref[...].T, g_t)):
        for h in range(4):
            send_ref[h, i * 64 : (i + 1) * 64, :] = rows[h * 64 : (h + 1) * 64]


def other_half_kernel(place_ref, got_ref, out_ref):
    core, begin = place_of(place_ref)[:2]
    for j in range(8):
        out_ref[j] = jnp.where(low_is_mine(j, core, begin), got_ref[8 + j], got_ref[j])


def to_owners_kernel(place_ref, mine_ref, theirs_ref, out_ref):
    core, begin = place_of(place_ref)[:2]
    for j in range(8):
        low_mine = low_is_mine(j, core, begin)
        mine, theirs = mine_ref[j], theirs_ref[j]
        out_ref[j] = jnp.where(low_mine, mine, theirs)
        out_ref[8 + j] = jnp.where(low_mine, theirs, mine)


def attn_to_owners_kernel(place_ref, mine_ref, theirs_ref, stat_ref, out_ref):
    to_owners_kernel(place_ref, mine_ref, theirs_ref, out_ref.at[:, 0:64, :])
    for j in range(HEADS):
        out_ref[j, 64:, :] = stat_ref[...]


def normalised(got_ref):
    attn = got_ref[:, 0:64, :].astype(F32).reshape(WIDTH, BLOCK)
    centre = attn - jnp.mean(attn, axis=0, keepdims=True)
    return centre * lax.rsqrt(jnp.mean(centre * centre, axis=0, keepdims=True) + 1e-05)


def gated_kernel(place_ref, got_ref, ut_ref, mine_ref, theirs_ref, zero_ref, one_ref):
    core = place_ref[4]
    gated = normalised(got_ref) * ut_ref[...].astype(F32)
    for z in range(0, 8, 2):
        for chip in range(HEADS):
            at = z * BLOCK + chip * 8
            one, two = gated[at : at + 8], gated[at + BLOCK : at + BLOCK + 8]
            rows = slice(chip * 32 + z * 4, chip * 32 + z * 4 + 8)
            zero_ref[rows, :] = jnp.concatenate([one[0:4], two[0:4]], axis=0)
            one_ref[rows, :] = jnp.concatenate([one[4:8], two[4:8]], axis=0)
    zero, one = zero_ref[...].astype(BF16), one_ref[...].astype(BF16)
    mine_ref[...] = jnp.where(core == 0, zero, one)
    theirs_ref[...] = jnp.where(core == 0, one, zero)


def d_gate_kernel(got_ref, dg_ref, after_ref, out_ref):
    d_gate = (dg_ref[...] * normalised(got_ref)).astype(BF16)
    for i in range(WIDTH // BLOCK):
        out_ref[:, i * BLOCK : (i + 1) * BLOCK] = d_gate[i * BLOCK : (i + 1) * BLOCK].T


def product_kernel(a_ref, b_ref, c_ref, d_ref, out_ref):
    for at in range(0, 512, 128):
        rows = slice(at, at + 128)
        out_ref[rows, :] = (dot(a_ref[rows, :], c_ref[...]) + dot(b_ref[rows, :], d_ref[...])).astype(BF16)


def finish_kernel(got_ref, dq_ref, dk_ref, dv_ref):
    for i, out_ref in enumerate((dq_ref, dk_ref, dv_ref)):
        for h in range(0, HEADS, 2):
            pair = got_ref[h : h + 2, i * 64 : (i + 1) * 64, :].reshape(BLOCK, BLOCK)
            out_ref[:, h * 64 : (h + 2) * 64] = pair.T


SMEM = pl.BlockSpec(memory_space=pltpu.SMEM)
VMEM = pl.BlockSpec(memory_space=pltpu.VMEM)


def call(kernel, name, out_shape, in_specs, args, scratch=(), flops=1 << 28, transcendentals=0):
    return pl.pallas_call(
        kernel,
        out_shape=out_shape,
        in_specs=in_specs,
        out_specs=jax.tree.map(lambda _: VMEM, out_shape),
        scratch_shapes=list(scratch),
        compiler_params=pltpu.CompilerParams(vmem_limit_bytes=56 * 1024 * 1024),
        cost_estimate=pl.CostEstimate(flops=flops, bytes_accessed=1 << 21, transcendentals=transcendentals),
        name=name,
    )(*args)


def shape(dims, dtype=BF16):
    return jax.ShapeDtypeStruct(dims, dtype)


def prepare(query, key, value, gate_u, cotangent, out_weight):
    cols = pl.BlockSpec((BLOCK, 256), lambda i: (0, i))
    return pl.pallas_call(
        prepare_kernel,
        grid=(4,),
        out_shape=(shape((HEADS, 256, BLOCK)), shape((WIDTH, BLOCK)), shape((WIDTH, BLOCK), F32)),
        in_specs=[cols] * 4
        + [pl.BlockSpec((BLOCK, WIDTH), lambda i: (0, 0)), pl.BlockSpec((256, WIDTH), lambda i: (i, 0))],
        out_specs=(
            pl.BlockSpec((4, 256, BLOCK), lambda i: (i, 0, 0)),
            pl.BlockSpec((256, BLOCK), lambda i: (i, 0)),
            pl.BlockSpec((256, BLOCK), lambda i: (i, 0)),
        ),
        name="prepare",
    )(query, key, value, gate_u, cotangent, out_weight)


def attend_forward(place, got, other):
    return call(
        forward_kernel,
        "attend_forward",
        (
            shape((256, HALF)),
            shape((HEAD_DIM, HALF)),
            shape((8, HEAD_DIM, BLOCK)),
            shape((8, HEAD_DIM, BLOCK)),
            shape((STATS * N_BLOCKS, BLOCK)),
        ),
        [SMEM, VMEM, VMEM],
        (place, got, other),
        [
            pltpu.VMEM((HALF, HEAD_DIM), BF16),
            pltpu.VMEM((N_BLOCKS, 256, BLOCK), F32),
            pltpu.VMEM((STATS * N_BLOCKS, BLOCK), F32),
        ],
        flops=1 << 30,
        transcendentals=1 << 22,
    )


def attend_backward(place, x, attn, got):
    return call(
        backward_kernel,
        "attend_backward",
        (shape((8, 192, BLOCK)), shape((8, 192, BLOCK))),
        [SMEM, VMEM, VMEM, VMEM],
        (place, x, attn, got),
        [pltpu.VMEM((HALF, HEAD_DIM), BF16)] * 4
        + [pltpu.VMEM((HEAD_DIM, HALF), BF16), pltpu.VMEM((HEAD_DIM, HALF), F32)]
        + [pltpu.VMEM((HALF, HEAD_DIM), F32)] * 2
        + [pltpu.VMEM((N_BLOCKS, 192, BLOCK), F32)],
        flops=1 << 33,
        transcendentals=1 << 24,
    )


def on_device(query, key, value, gate_u, out_weight, cotangent, hist_lengths):
    core = lax.axis_index("core")
    place = jnp.concatenate([hist_lengths[0], core[None]]).astype(jnp.int32)

    def swap(x):
        return lax.ppermute(x, "core", SWAP)

    def chips(x):
        return lax.all_to_all(x, CHIP, 0, 0, tiled=True)

    send, u_t, d_gated_t = prepare(query, key, value, gate_u, cotangent, out_weight)
    got = chips(send)
    theirs = call(other_half_kernel, "other_half", shape((8, 256, BLOCK)), [SMEM, VMEM], (place, got))
    x, attn, mine, theirs, stat = attend_forward(place, got, swap(theirs))

    rows = HEAD_DIM + STATS * N_BLOCKS
    send = call(
        attn_to_owners_kernel,
        "attn_to_owners",
        shape((HEADS, rows, BLOCK)),
        [SMEM] + [VMEM] * 3,
        (place, mine, swap(theirs), stat),
    )
    got_attn = chips(send)

    mine, theirs = call(
        gated_kernel,
        "gated",
        (shape((512, BLOCK)), shape((512, BLOCK))),
        [SMEM] + [VMEM] * 2,
        (place, got_attn, u_t),
        [pltpu.VMEM((512, BLOCK), F32)] * 2,
    )
    part = call(
        product_kernel,
        "product",
        shape((512, WIDTH)),
        [VMEM] * 4,
        (mine, swap(theirs), cotangent, swap(cotangent)),
    )
    parts = chips(part.reshape(HEADS, 32, WIDTH))

    mine, theirs = attend_backward(place, x, attn, got_attn)
    send = call(
        to_owners_kernel,
        "grads_to_owners",
        shape((HEADS, 192, BLOCK)),
        [SMEM] + [VMEM] * 2,
        (place, mine, swap(theirs)),
    )
    got = chips(send)

    part = jnp.sum(parts.astype(F32), axis=0).reshape(8, 4, WIDTH)
    z = lax.axis_index("dp")
    for step in (4, 2, 1):
        high = (z // step) % 2
        halves = part.reshape(2, step, 4, WIDTH)
        away = lax.dynamic_index_in_dim(halves, 1 - high, 0, keepdims=False)
        kept = lax.dynamic_index_in_dim(halves, high, 0, keepdims=False)
        part = kept + lax.ppermute(away, "dp", [(i, i ^ step) for i in range(8)])
    d_weight = part.reshape(4, WIDTH) * (1.0 / math.sqrt(32768))

    d_gate = call(
        d_gate_kernel,
        "d_gate",
        shape((BLOCK, WIDTH)),
        [VMEM, VMEM, pl.BlockSpec(memory_space=pl.ANY)],
        (got_attn, d_gated_t, send),
    )
    d_query, d_key, d_value = call(finish_kernel, "finish", (shape((BLOCK, WIDTH)),) * 3, [VMEM], (got,))
    return d_query, d_key, d_value, d_gate, d_weight


def solution(mesh):
    axes = ("dp", "x", "y", "core")
    inner = Mesh(mesh.devices.reshape(8, 4, 4, 2), axes)
    rows = P(axes, None)
    return jax.shard_map(
        on_device,
        mesh=inner,
        in_specs=(rows, rows, rows, rows, P(), rows, P("dp", None)),
        out_specs=(rows, rows, rows, rows, rows),
        check_vma=False,
    )
```

```python
import math

import jax
import jax.numpy as jnp
from jax import lax
from jax.experimental import pallas as pl
from jax.experimental.pallas import tpu as pltpu
from jax.sharding import Mesh, PartitionSpec as P

HEADS = 16
HEAD_DIM = 64
WIDTH = HEADS * HEAD_DIM
N_BLOCKS = 16
BLOCK = 128
HALF = N_BLOCKS * BLOCK
SUB = 256
F_TILE = 2048
B_TILE = 1024
STATS = 5
CHIP = ("x", "y")
SWAP = ((0, 1), (1, 0))
BF16 = jnp.bfloat16
F32 = jnp.float32


def dot(a, b):
    return lax.dot_general(a, b, (((1,), (0,)), ((), ())), preferred_element_type=F32)


def dot_nt(a, b):
    return lax.dot_general(a, b, (((1,), (1,)), ((), ())), preferred_element_type=F32)


def turned(x):
    n = x.shape[1]
    row, col = (lax.broadcasted_iota(jnp.int32, (n, n), i) for i in range(2))
    return dot_nt(jnp.where(row == col, 1.0, 0.0).astype(BF16), x).astype(BF16)


def sigmoid(s):
    return pltpu.reciprocal(1.0 + jnp.exp(-s), approx=True)


def lanes():
    return lax.broadcasted_iota(jnp.int32, (1, BLOCK), 1)


def place_of(place_ref):
    first, second, third = (place_ref[i] for i in range(3))
    core = place_ref[4]
    is_first, is_second = first == HALF, second == HALF
    begin = jnp.where(is_first, 0, jnp.where(is_second, first, first + second + jnp.where(third == HALF, 0, third)))
    end1 = jnp.where(is_first, second, first)
    end2 = end1 + jnp.where(is_first | is_second, third, second)
    turn = jnp.where(core == 0, begin & (HALF - 1), 0)
    return core, begin, turn, jnp.where(core == 0, HALF, end1), jnp.where(core == 0, HALF, end2)


def low_is_mine(j, core, begin):
    return ((2 * j + core) * BLOCK + lanes() >= begin) == (core == 0)


def live_of(q_at, k_at, end1, end2, diagonal):
    q_place = q_at + lax.broadcasted_iota(jnp.int32, (1, SUB), 1)
    k_place = k_at + lax.broadcasted_iota(jnp.int32, (SUB, 1), 0)
    start = jnp.where(q_place < end1, 0, jnp.where(q_place < end2, end1, end2))
    live = k_place >= start
    return live & (k_place <= q_place) if diagonal else live


def below(n_tiles, tile):
    n_sub = tile // SUB
    for i in range(n_tiles):
        for j in range(i + 1):
            subs = [(q, k) for q in range(n_sub) for k in range(n_sub) if j < i or k <= q]
            yield i * tile, j * tile, subs


def forward_kernel(
    place_ref, got_ref, other_ref, x_ref, attn_ref, mine_ref, theirs_ref, stat_ref, k_ref, slot_ref, stats_ref
):
    core, begin, turn, end1, end2 = place_of(place_ref)
    whole, rest = turn // BLOCK, turn % BLOCK
    lane = lanes()
    for b in range(N_BLOCKS):
        j = b // 2
        mine = jnp.where(low_is_mine(j, core, begin), got_ref[j], got_ref[8 + j])
        here = jnp.where(core == b % 2, mine, other_ref[j])
        slot_ref[b] = pltpu.roll(here.astype(F32), lax.rem(BLOCK - rest, BLOCK), 1)
    for b in range(N_BLOCKS):
        first, second = slot_ref[lax.rem(b + whole, N_BLOCKS)], slot_ref[lax.rem(b + whole + 1, N_BLOCKS)]
        here = jnp.where(lane < BLOCK - rest, first, second)
        x_ref[0:64, b * BLOCK : (b + 1) * BLOCK] = (here[0:64] * 0.125).astype(BF16)
        x_ref[64:256, b * BLOCK : (b + 1) * BLOCK] = here[64:256].astype(BF16)
        k_ref[b * BLOCK : (b + 1) * BLOCK, :] = here[64:128].astype(BF16).T

    for q_at, k_at, subs in below(HALF // F_TILE, F_TILE):
        weights = {}
        for q, k in subs:
            q_sub, k_sub = q_at + q * SUB, k_at + k * SUB
            s = dot(k_ref[k_sub : k_sub + SUB, :], x_ref[0:64, q_sub : q_sub + SUB])
            live = live_of(q_sub, k_sub, end1, end2, q_sub == k_sub)
            weights[q, k] = jnp.where(live, s * sigmoid(s), 0.0).astype(BF16)
        for q in range(F_TILE // SUB):
            q_sub = q_at + q * SUB
            acc = jnp.zeros((HEAD_DIM, SUB), F32)
            for k in range(F_TILE // SUB):
                if (q, k) in weights:
                    k_sub = k_at + k * SUB
                    acc += dot(x_ref[128:192, k_sub : k_sub + SUB], weights[q, k])
            attn_ref[:, q_sub : q_sub + SUB] = acc.astype(BF16)

    turned = []
    for b in range(N_BLOCKS):
        cols = slice(b * BLOCK, (b + 1) * BLOCK)
        attn = attn_ref[:, cols].astype(F32)
        g = x_ref[192:256, cols].astype(F32)
        mean = jnp.mean(attn, axis=0, keepdims=True)
        centre = attn - mean
        both = jnp.sum(centre * g, axis=0, keepdims=True)
        mean_hi = mean.astype(BF16).astype(F32)
        square = jnp.sum(centre * centre, axis=0, keepdims=True)
        total = jnp.sum(g, axis=0, keepdims=True)
        for i, row in enumerate((mean_hi, mean - mean_hi, both, square, total)):
            stats_ref[i * N_BLOCKS + b : i * N_BLOCKS + b + 1, :] = row
        turned.append(attn)
    stat_ref[...] = stats_ref[...].astype(BF16)
    turn_out(turned, turn, core, slot_ref, mine_ref, theirs_ref)


def turn_out(blocks, turn, core, slot_ref, mine_ref, theirs_ref):
    whole, rest = turn // BLOCK, turn % BLOCK
    rows = blocks[0].shape[0]
    for b, block in enumerate(blocks):
        slot_ref[b, 0:rows, :] = pltpu.roll(block, rest, 1)
    from_this = lanes() >= rest
    for j in range(8):
        pair = []
        for b in (2 * j, 2 * j + 1):
            this = slot_ref[lax.rem(b - whole + N_BLOCKS, N_BLOCKS), 0:rows, :]
            last = slot_ref[lax.rem(b - whole + N_BLOCKS - 1, N_BLOCKS), 0:rows, :]
            pair.append(jnp.where(from_this, this, last).astype(BF16))
        mine_ref[j] = jnp.where(core == 0, pair[0], pair[1])
        theirs_ref[j] = jnp.where(core == 0, pair[1], pair[0])


def backward_kernel(
    place_ref, x_ref, attn_ref, got_ref, mine_ref, theirs_ref,
    qn_ref, kn_ref, vn_ref, dn_ref, dt_ref, dq_ref, dk_ref, dv_ref, slot_ref,
):
    core, _, turn, end1, end2 = place_of(place_ref)
    stat = got_ref[:, 64 : 64 + STATS * N_BLOCKS, :].astype(F32).reshape(HEADS, STATS, N_BLOCKS, BLOCK)
    mean_h = stat[:, 0] + stat[:, 1]
    mean = jnp.mean(mean_h, axis=0)
    off = mean_h - mean[None]
    square = jnp.sum(stat[:, 3] + HEAD_DIM * off * off, axis=0)
    rstd = lax.rsqrt(square * (1.0 / WIDTH) + 1e-05)
    g_sum = stat[:, 4]
    g_mean = jnp.sum(g_sum, axis=0) * (1.0 / WIDTH)
    both = jnp.sum(stat[:, 2] + off * g_sum, axis=0) * rstd * (1.0 / WIDTH)
    for b in range(N_BLOCKS):
        cols = slice(b * BLOCK, (b + 1) * BLOCK)
        here = x_ref[:, cols]
        r = rstd[b : b + 1]
        normed = (attn_ref[:, cols].astype(F32) - mean[b : b + 1]) * r
        d = (r * (here[192:256].astype(F32) - g_mean[b : b + 1] - normed * both[b : b + 1])).astype(BF16)
        dt_ref[:, cols] = d
        dn_ref[cols, :] = d.T
        qn_ref[cols, :] = here[0:64].T
        kn_ref[cols, :] = here[64:128].T
        vn_ref[cols, :] = here[128:192].T

    for q_at, k_at, subs in below(HALF // B_TILE, B_TILE):
        made = {}
        for q, k in subs:
            q_cols = slice(q_at + q * SUB, q_at + (q + 1) * SUB)
            k_cols = slice(k_at + k * SUB, k_at + (k + 1) * SUB)
            s = dot(kn_ref[k_cols, :], x_ref[0:64, q_cols])
            d_p = dot(vn_ref[k_cols, :], dt_ref[:, q_cols])
            live = live_of(q_cols.start, k_cols.start, end1, end2, q_cols.start == k_cols.start)
            sigma = jnp.where(live, sigmoid(s), 0.0)
            silu = s * sigma
            made[q, k] = silu.astype(BF16), (d_p * (sigma + silu * (1.0 - sigma))).astype(BF16)
        for k in range(B_TILE // SUB):
            k_cols = slice(k_at + k * SUB, k_at + (k + 1) * SUB)
            d_v, d_k = [], []
            for q in range(B_TILE // SUB):
                if (q, k) in made:
                    q_cols = slice(q_at + q * SUB, q_at + (q + 1) * SUB)
                    d_v.append(dot(made[q, k][0], dn_ref[q_cols, :]))
                    d_k.append(dot(made[q, k][1], qn_ref[q_cols, :]))
            if q_at == k_at:
                dv_ref[k_cols, :], dk_ref[k_cols, :] = sum(d_v), sum(d_k)
            else:
                dv_ref[k_cols, :] += sum(d_v)
                dk_ref[k_cols, :] += sum(d_k)
        for q in range(B_TILE // SUB):
            q_cols = slice(q_at + q * SUB, q_at + (q + 1) * SUB)
            d_q = []
            for k in range(B_TILE // SUB):
                if (q, k) in made:
                    d_q.append(dot(x_ref[64:128, k_at + k * SUB : k_at + (k + 1) * SUB], made[q, k][1]))
            if k_at == 0:
                dq_ref[:, q_cols] = sum(d_q)
            else:
                dq_ref[:, q_cols] += sum(d_q)

    turned = []
    for b in range(N_BLOCKS):
        cols = slice(b * BLOCK, (b + 1) * BLOCK)
        turned.append(jnp.concatenate([dq_ref[:, cols] * 0.125, dk_ref[cols, :].T, dv_ref[cols, :].T], axis=0))
    turn_out(turned, turn, core, slot_ref, mine_ref, theirs_ref)


def prepare_kernel(q_ref, k_ref, v_ref, u_ref, cot_ref, w_ref, send_ref, ut_ref, dg_ref):
    d_gated = dot_nt(w_ref[...], cot_ref[...])
    u_t = turned(u_ref[...])
    dg_ref[...] = d_gated
    ut_ref[...] = u_t
    g_t = (d_gated * u_t.astype(F32)).astype(BF16)
    for i, rows in enumerate((turned(q_ref[...]), turned(k_ref[...]), turned(v_ref[...]), g_t)):
        for h in range(4):
            send_ref[h, i * 64 : (i + 1) * 64, :] = rows[h * 64 : (h + 1) * 64]


def other_half_kernel(place_ref, got_ref, out_ref):
    core, begin = place_of(place_ref)[:2]
    for j in range(8):
        out_ref[j] = jnp.where(low_is_mine(j, core, begin), got_ref[8 + j], got_ref[j])


def to_owners_kernel(place_ref, mine_ref, theirs_ref, out_ref):
    core, begin = place_of(place_ref)[:2]
    for j in range(8):
        low_mine = low_is_mine(j, core, begin)
        mine, theirs = mine_ref[j], theirs_ref[j]
        out_ref[j] = jnp.where(low_mine, mine, theirs)
        out_ref[8 + j] = jnp.where(low_mine, theirs, mine)


def attn_to_owners_kernel(place_ref, mine_ref, theirs_ref, stat_ref, out_ref):
    to_owners_kernel(place_ref, mine_ref, theirs_ref, out_ref.at[:, 0:64, :])
    for j in range(HEADS):
        out_ref[j, 64:, :] = stat_ref[...]


def normalised(got_ref):
    attn = got_ref[:, 0:64, :].astype(F32).reshape(WIDTH, BLOCK)
    centre = attn - jnp.mean(attn, axis=0, keepdims=True)
    return centre * lax.rsqrt(jnp.mean(centre * centre, axis=0, keepdims=True) + 1e-05)


def gated_kernel(place_ref, got_ref, ut_ref, mine_ref, theirs_ref, zero_ref, one_ref):
    core = place_ref[4]
    gated = normalised(got_ref) * ut_ref[...].astype(F32)
    for z in range(0, 8, 2):
        for chip in range(HEADS):
            at = z * BLOCK + chip * 8
            one, two = gated[at : at + 8], gated[at + BLOCK : at + BLOCK + 8]
            rows = slice(chip * 32 + z * 4, chip * 32 + z * 4 + 8)
            zero_ref[rows, :] = jnp.concatenate([one[0:4], two[0:4]], axis=0)
            one_ref[rows, :] = jnp.concatenate([one[4:8], two[4:8]], axis=0)
    zero, one = zero_ref[...].astype(BF16), one_ref[...].astype(BF16)
    mine_ref[...] = jnp.where(core == 0, zero, one)
    theirs_ref[...] = jnp.where(core == 0, one, zero)


def d_gate_kernel(got_ref, dg_ref, after_ref, out_ref):
    d_gate = (dg_ref[...] * normalised(got_ref)).astype(BF16)
    for i in range(WIDTH // BLOCK):
        out_ref[:, i * BLOCK : (i + 1) * BLOCK] = turned(d_gate[i * BLOCK : (i + 1) * BLOCK])


def product_kernel(a_ref, b_ref, c_ref, d_ref, out_ref):
    for at in range(0, 512, 128):
        rows = slice(at, at + 128)
        out_ref[rows, :] = (dot(a_ref[rows, :], c_ref[...]) + dot(b_ref[rows, :], d_ref[...])).astype(BF16)


def finish_kernel(got_ref, dq_ref, dk_ref, dv_ref):
    for i, out_ref in enumerate((dq_ref, dk_ref, dv_ref)):
        for h in range(0, HEADS, 4):
            heads = got_ref[h : h + 4, i * 64 : (i + 1) * 64, :].reshape(256, BLOCK)
            out_ref[:, h * 64 : (h + 4) * 64] = turned(heads)


SMEM = pl.BlockSpec(memory_space=pltpu.SMEM)
VMEM = pl.BlockSpec(memory_space=pltpu.VMEM)


def call(kernel, name, out_shape, in_specs, args, scratch=(), mib=8, flops=1 << 26, transcendentals=0):
    return pl.pallas_call(
        kernel,
        out_shape=out_shape,
        in_specs=in_specs,
        out_specs=jax.tree.map(lambda _: VMEM, out_shape),
        scratch_shapes=list(scratch),
        compiler_params=pltpu.CompilerParams(vmem_limit_bytes=mib * 1024 * 1024),
        cost_estimate=pl.CostEstimate(flops=flops, bytes_accessed=1 << 21, transcendentals=transcendentals),
        name=name,
    )(*args)


def shape(dims, dtype=BF16):
    return jax.ShapeDtypeStruct(dims, dtype)


def prepare(query, key, value, gate_u, cotangent, out_weight):
    cols = pl.BlockSpec((BLOCK, 256), lambda i: (0, i))
    return pl.pallas_call(
        prepare_kernel,
        grid=(4,),
        out_shape=(shape((HEADS, 256, BLOCK)), shape((WIDTH, BLOCK)), shape((WIDTH, BLOCK), F32)),
        in_specs=[cols] * 4
        + [pl.BlockSpec((BLOCK, WIDTH), lambda i: (0, 0)), pl.BlockSpec((256, WIDTH), lambda i: (i, 0))],
        out_specs=(
            pl.BlockSpec((4, 256, BLOCK), lambda i: (i, 0, 0)),
            pl.BlockSpec((256, BLOCK), lambda i: (i, 0)),
            pl.BlockSpec((256, BLOCK), lambda i: (i, 0)),
        ),
        name="prepare",
    )(query, key, value, gate_u, cotangent, out_weight)


def attend_forward(place, got, other):
    return call(
        forward_kernel,
        "attend_forward",
        (
            shape((256, HALF)),
            shape((HEAD_DIM, HALF)),
            shape((8, HEAD_DIM, BLOCK)),
            shape((8, HEAD_DIM, BLOCK)),
            shape((STATS * N_BLOCKS, BLOCK)),
        ),
        [SMEM, VMEM, VMEM],
        (place, got, other),
        [
            pltpu.VMEM((HALF, HEAD_DIM), BF16),
            pltpu.VMEM((N_BLOCKS, 256, BLOCK), F32),
            pltpu.VMEM((STATS * N_BLOCKS, BLOCK), F32),
        ],
        mib=20,
        flops=1 << 30,
        transcendentals=1 << 22,
    )


def attend_backward(place, x, attn, got):
    return call(
        backward_kernel,
        "attend_backward",
        (shape((8, 192, BLOCK)), shape((8, 192, BLOCK))),
        [SMEM, VMEM, VMEM, VMEM],
        (place, x, attn, got),
        [pltpu.VMEM((HALF, HEAD_DIM), BF16)] * 4
        + [pltpu.VMEM((HEAD_DIM, HALF), BF16), pltpu.VMEM((HEAD_DIM, HALF), F32)]
        + [pltpu.VMEM((HALF, HEAD_DIM), F32)] * 2
        + [pltpu.VMEM((N_BLOCKS, 192, BLOCK), F32)],
        mib=24,
        flops=1 << 33,
        transcendentals=1 << 24,
    )


def on_device(query, key, value, gate_u, out_weight, cotangent, hist_lengths):
    core = lax.axis_index("core")
    place = jnp.concatenate([hist_lengths[0], core[None]]).astype(jnp.int32)

    def swap(x):
        return lax.ppermute(x, "core", SWAP)

    def chips(x):
        return lax.all_to_all(x, CHIP, 0, 0, tiled=True)

    send, u_t, d_gated_t = prepare(query, key, value, gate_u, cotangent, out_weight)
    got = chips(send)
    theirs = call(other_half_kernel, "other_half", shape((8, 256, BLOCK)), [SMEM, VMEM], (place, got))
    x, attn, mine, theirs, stat = attend_forward(place, got, swap(theirs))

    rows = HEAD_DIM + STATS * N_BLOCKS
    send = call(
        attn_to_owners_kernel,
        "attn_to_owners",
        shape((HEADS, rows, BLOCK)),
        [SMEM] + [VMEM] * 3,
        (place, mine, swap(theirs), stat),
    )
    got_attn = chips(send)

    mine, theirs = call(
        gated_kernel,
        "gated",
        (shape((512, BLOCK)), shape((512, BLOCK))),
        [SMEM] + [VMEM] * 2,
        (place, got_attn, u_t),
        [pltpu.VMEM((512, BLOCK), F32)] * 2,
    )
    part = call(
        product_kernel,
        "product",
        shape((512, WIDTH)),
        [VMEM] * 4,
        (mine, swap(theirs), cotangent, swap(cotangent)),
    )
    parts = chips(part.reshape(HEADS, 32, WIDTH))

    mine, theirs = attend_backward(place, x, attn, got_attn)
    send = call(
        to_owners_kernel,
        "grads_to_owners",
        shape((HEADS, 192, BLOCK)),
        [SMEM] + [VMEM] * 2,
        (place, mine, swap(theirs)),
    )
    got = chips(send)
    d_gate = call(
        d_gate_kernel,
        "d_gate",
        shape((BLOCK, WIDTH)),
        [VMEM, VMEM, pl.BlockSpec(memory_space=pl.ANY)],
        (got_attn, d_gated_t, send),
        flops=1 << 20,
    )

    parts, d_gate = lax.optimization_barrier((parts, d_gate))
    part = jnp.sum(parts.astype(F32), axis=0).reshape(8, 4, WIDTH)
    z = lax.axis_index("dp")
    for step in (4, 2, 1):
        high = (z // step) % 2
        halves = part.reshape(2, step, 4, WIDTH)
        away = lax.dynamic_index_in_dim(halves, 1 - high, 0, keepdims=False)
        kept = lax.dynamic_index_in_dim(halves, high, 0, keepdims=False)
        part = kept + lax.ppermute(away, "dp", [(i, i ^ step) for i in range(8)])
    d_weight = part.reshape(4, WIDTH) * (1.0 / math.sqrt(32768))

    d_query, d_key, d_value = call(finish_kernel, "finish", (shape((BLOCK, WIDTH)),) * 3, [VMEM], (got,))
    return d_query, d_key, d_value, d_gate, d_weight


def solution(mesh):
    axes = ("dp", "x", "y", "core")
    inner = Mesh(mesh.devices.reshape(8, 4, 4, 2), axes)
    rows = P(axes, None)
    return jax.shard_map(
        on_device,
        mesh=inner,
        in_specs=(rows, rows, rows, rows, P(), rows, P("dp", None)),
        out_specs=(rows, rows, rows, rows, rows),
        check_vma=False,
    )
```

```python
import math

import jax
import jax.numpy as jnp
from jax import lax
from jax.experimental import pallas as pl
from jax.experimental.pallas import tpu as pltpu
from jax.sharding import Mesh, PartitionSpec as P

HEADS = 16
HEAD_DIM = 64
WIDTH = HEADS * HEAD_DIM
N_BLOCKS = 16
BLOCK = 128
HALF = N_BLOCKS * BLOCK
SUB = 256
F_TILE = 2048
B_TILE = 1024
STATS = 5
CHIP = ("x", "y")
SWAP = ((0, 1), (1, 0))
BF16 = jnp.bfloat16
F32 = jnp.float32


def dot(a, b):
    return lax.dot_general(a, b, (((1,), (0,)), ((), ())), preferred_element_type=F32)


def dot_nt(a, b):
    return lax.dot_general(a, b, (((1,), (1,)), ((), ())), preferred_element_type=F32)


def sigmoid(s):
    return pltpu.reciprocal(1.0 + jnp.exp(-s), approx=True)


def lanes():
    return lax.broadcasted_iota(jnp.int32, (1, BLOCK), 1)


def place_of(place_ref):
    first, second, third = (place_ref[i] for i in range(3))
    core = place_ref[4]
    is_first, is_second = first == HALF, second == HALF
    begin = jnp.where(is_first, 0, jnp.where(is_second, first, first + second + jnp.where(third == HALF, 0, third)))
    end1 = jnp.where(is_first, second, first)
    end2 = end1 + jnp.where(is_first | is_second, third, second)
    turn = jnp.where(core == 0, begin & (HALF - 1), 0)
    return core, begin, turn, jnp.where(core == 0, HALF, end1), jnp.where(core == 0, HALF, end2)


def low_is_mine(j, core, begin):
    return ((2 * j + core) * BLOCK + lanes() >= begin) == (core == 0)


def live_of(q_at, k_at, end1, end2, diagonal):
    q_place = q_at + lax.broadcasted_iota(jnp.int32, (1, SUB), 1)
    k_place = k_at + lax.broadcasted_iota(jnp.int32, (SUB, 1), 0)
    start = jnp.where(q_place < end1, 0, jnp.where(q_place < end2, end1, end2))
    live = k_place >= start
    return live & (k_place <= q_place) if diagonal else live


def below(n_tiles, tile):
    n_sub = tile // SUB
    for i in range(n_tiles):
        for j in range(i + 1):
            subs = [(q, k) for q in range(n_sub) for k in range(n_sub) if j < i or k <= q]
            yield i * tile, j * tile, subs


def forward_kernel(
    place_ref, got_ref, other_ref, x_ref, attn_ref, mine_ref, theirs_ref, stat_ref, k_ref, slot_ref, stats_ref
):
    core, begin, turn, end1, end2 = place_of(place_ref)
    whole, rest = turn // BLOCK, turn % BLOCK
    lane = lanes()
    for b in range(N_BLOCKS):
        j = b // 2
        mine = jnp.where(low_is_mine(j, core, begin), got_ref[j], got_ref[8 + j])
        here = jnp.where(core == b % 2, mine, other_ref[j])
        slot_ref[b] = pltpu.roll(here.astype(F32), lax.rem(BLOCK - rest, BLOCK), 1)
    for b in range(N_BLOCKS):
        first, second = slot_ref[lax.rem(b + whole, N_BLOCKS)], slot_ref[lax.rem(b + whole + 1, N_BLOCKS)]
        here = jnp.where(lane < BLOCK - rest, first, second)
        x_ref[0:64, b * BLOCK : (b + 1) * BLOCK] = (here[0:64] * 0.125).astype(BF16)
        x_ref[64:256, b * BLOCK : (b + 1) * BLOCK] = here[64:256].astype(BF16)
        k_ref[b * BLOCK : (b + 1) * BLOCK, :] = here[64:128].astype(BF16).T

    for q_at, k_at, subs in below(HALF // F_TILE, F_TILE):
        weights = {}
        for q, k in subs:
            q_sub, k_sub = q_at + q * SUB, k_at + k * SUB
            s = dot(k_ref[k_sub : k_sub + SUB, :], x_ref[0:64, q_sub : q_sub + SUB])
            live = live_of(q_sub, k_sub, end1, end2, q_sub == k_sub)
            weights[q, k] = jnp.where(live, s * sigmoid(s), 0.0).astype(BF16)
        for q in range(F_TILE // SUB):
            q_sub = q_at + q * SUB
            acc = jnp.zeros((HEAD_DIM, SUB), F32)
            for k in range(F_TILE // SUB):
                if (q, k) in weights:
                    k_sub = k_at + k * SUB
                    acc += dot(x_ref[128:192, k_sub : k_sub + SUB], weights[q, k])
            attn_ref[:, q_sub : q_sub + SUB] = acc.astype(BF16)

    turned = []
    for b in range(N_BLOCKS):
        cols = slice(b * BLOCK, (b + 1) * BLOCK)
        attn = attn_ref[:, cols].astype(F32)
        g = x_ref[192:256, cols].astype(F32)
        mean = jnp.mean(attn, axis=0, keepdims=True)
        centre = attn - mean
        both = jnp.sum(centre * g, axis=0, keepdims=True)
        mean_hi = mean.astype(BF16).astype(F32)
        square = jnp.sum(centre * centre, axis=0, keepdims=True)
        total = jnp.sum(g, axis=0, keepdims=True)
        for i, row in enumerate((mean_hi, mean - mean_hi, both, square, total)):
            stats_ref[i * N_BLOCKS + b : i * N_BLOCKS + b + 1, :] = row
        turned.append(attn)
    stat_ref[...] = stats_ref[...].astype(BF16)
    turn_out(turned, turn, core, slot_ref, mine_ref, theirs_ref)


def turn_out(blocks, turn, core, slot_ref, mine_ref, theirs_ref):
    whole, rest = turn // BLOCK, turn % BLOCK
    rows = blocks[0].shape[0]
    for b, block in enumerate(blocks):
        slot_ref[b, 0:rows, :] = pltpu.roll(block, rest, 1)
    from_this = lanes() >= rest
    for j in range(8):
        pair = []
        for b in (2 * j, 2 * j + 1):
            this = slot_ref[lax.rem(b - whole + N_BLOCKS, N_BLOCKS), 0:rows, :]
            last = slot_ref[lax.rem(b - whole + N_BLOCKS - 1, N_BLOCKS), 0:rows, :]
            pair.append(jnp.where(from_this, this, last).astype(BF16))
        mine_ref[j] = jnp.where(core == 0, pair[0], pair[1])
        theirs_ref[j] = jnp.where(core == 0, pair[1], pair[0])


PAIRS = [(q, k) for q in range(HALF // SUB) for k in range(q + 1)]
AT = {pair: i for i, pair in enumerate(PAIRS)}


def derive_kernel(place_ref, x_ref, silu_ref, slope_ref, qn_ref, kn_ref, vn_ref):
    end1, end2 = place_of(place_ref)[3:]
    for b in range(N_BLOCKS):
        cols = slice(b * BLOCK, (b + 1) * BLOCK)
        for i, out_ref in enumerate((qn_ref, kn_ref, vn_ref)):
            out_ref[cols, :] = x_ref[i * 64 : (i + 1) * 64, cols].T
    for q, k in PAIRS:
        q_cols, k_cols = slice(q * SUB, (q + 1) * SUB), slice(k * SUB, (k + 1) * SUB)
        s = dot(kn_ref[k_cols, :], x_ref[0:64, q_cols])
        sigma = jnp.where(live_of(q * SUB, k * SUB, end1, end2, q == k), sigmoid(s), 0.0)
        silu = s * sigma
        silu_ref[AT[q, k]] = silu.astype(BF16)
        slope_ref[AT[q, k]] = (sigma + silu * (1.0 - sigma)).astype(BF16)


def backward_kernel(
    place_ref, x_ref, attn_ref, got_ref, silu_ref, slope_ref, qn_ref, kn_ref, vn_ref, mine_ref, theirs_ref,
    dn_ref, dt_ref, dq_ref, dk_ref, dv_ref, slot_ref,
):
    core, _, turn, end1, end2 = place_of(place_ref)
    stat = got_ref[:, 64 : 64 + STATS * N_BLOCKS, :].astype(F32).reshape(HEADS, STATS, N_BLOCKS, BLOCK)
    mean_h = stat[:, 0] + stat[:, 1]
    mean = jnp.mean(mean_h, axis=0)
    off = mean_h - mean[None]
    square = jnp.sum(stat[:, 3] + HEAD_DIM * off * off, axis=0)
    rstd = lax.rsqrt(square * (1.0 / WIDTH) + 1e-05)
    g_sum = stat[:, 4]
    g_mean = jnp.sum(g_sum, axis=0) * (1.0 / WIDTH)
    both = jnp.sum(stat[:, 2] + off * g_sum, axis=0) * rstd * (1.0 / WIDTH)
    for b in range(N_BLOCKS):
        cols = slice(b * BLOCK, (b + 1) * BLOCK)
        r = rstd[b : b + 1]
        normed = (attn_ref[:, cols].astype(F32) - mean[b : b + 1]) * r
        d = (r * (x_ref[192:256, cols].astype(F32) - g_mean[b : b + 1] - normed * both[b : b + 1])).astype(BF16)
        dt_ref[:, cols] = d
        dn_ref[cols, :] = d.T

    for q_at, k_at, subs in below(HALF // B_TILE, B_TILE):
        n = B_TILE // SUB
        q_first, k_first = q_at // SUB, k_at // SUB
        made = {}
        for q, k in subs:
            q_cols = slice(q_at + q * SUB, q_at + (q + 1) * SUB)
            k_cols = slice(k_at + k * SUB, k_at + (k + 1) * SUB)
            d_p = dot(vn_ref[k_cols, :], dt_ref[:, q_cols])
            made[q, k] = (d_p * slope_ref[AT[q_first + q, k_first + k]].astype(F32)).astype(BF16)
        for k in range(n):
            k_cols = slice(k_at + k * SUB, k_at + (k + 1) * SUB)
            d_v, d_k = [], []
            for q in range(n):
                if (q, k) in made:
                    q_cols = slice(q_at + q * SUB, q_at + (q + 1) * SUB)
                    d_v.append(dot(silu_ref[AT[q_first + q, k_first + k]], dn_ref[q_cols, :]))
                    d_k.append(dot(made[q, k], qn_ref[q_cols, :]))
            if q_at == k_at:
                dv_ref[k_cols, :], dk_ref[k_cols, :] = sum(d_v), sum(d_k)
            else:
                dv_ref[k_cols, :] += sum(d_v)
                dk_ref[k_cols, :] += sum(d_k)
        for q in range(n):
            q_cols = slice(q_at + q * SUB, q_at + (q + 1) * SUB)
            d_q = []
            for k in range(n):
                if (q, k) in made:
                    d_q.append(dot(x_ref[64:128, k_at + k * SUB : k_at + (k + 1) * SUB], made[q, k]))
            if k_at == 0:
                dq_ref[:, q_cols] = sum(d_q)
            else:
                dq_ref[:, q_cols] += sum(d_q)

    turned = []
    for b in range(N_BLOCKS):
        cols = slice(b * BLOCK, (b + 1) * BLOCK)
        turned.append(jnp.concatenate([dq_ref[:, cols] * 0.125, dk_ref[cols, :].T, dv_ref[cols, :].T], axis=0))
    turn_out(turned, turn, core, slot_ref, mine_ref, theirs_ref)


def prepare_kernel(q_ref, k_ref, v_ref, u_ref, cot_ref, w_ref, send_ref, ut_ref, dg_ref):
    for at in range(0, WIDTH, 256):
        cols = slice(at, at + 256)
        d_gated = dot_nt(w_ref[cols, :], cot_ref[...])
        u_t = u_ref[:, cols].T
        dg_ref[cols, :] = d_gated
        ut_ref[cols, :] = u_t
        g_t = (d_gated * u_t.astype(F32)).astype(BF16)
        for i, rows in enumerate((q_ref[:, cols].T, k_ref[:, cols].T, v_ref[:, cols].T, g_t)):
            for h in range(4):
                send_ref[at // 64 + h, i * 64 : (i + 1) * 64, :] = rows[h * 64 : (h + 1) * 64]


def other_half_kernel(place_ref, got_ref, out_ref):
    core, begin = place_of(place_ref)[:2]
    for j in range(8):
        out_ref[j] = jnp.where(low_is_mine(j, core, begin), got_ref[8 + j], got_ref[j])


def to_owners_kernel(place_ref, mine_ref, theirs_ref, out_ref):
    core, begin = place_of(place_ref)[:2]
    for j in range(8):
        low_mine = low_is_mine(j, core, begin)
        mine, theirs = mine_ref[j], theirs_ref[j]
        out_ref[j] = jnp.where(low_mine, mine, theirs)
        out_ref[8 + j] = jnp.where(low_mine, theirs, mine)


def attn_to_owners_kernel(place_ref, mine_ref, theirs_ref, stat_ref, out_ref):
    to_owners_kernel(place_ref, mine_ref, theirs_ref, out_ref.at[:, 0:64, :])
    for j in range(HEADS):
        out_ref[j, 64:, :] = stat_ref[...]


def normalised(got_ref):
    attn = got_ref[:, 0:64, :].astype(F32).reshape(WIDTH, BLOCK)
    centre = attn - jnp.mean(attn, axis=0, keepdims=True)
    return centre * lax.rsqrt(jnp.mean(centre * centre, axis=0, keepdims=True) + 1e-05)


def gated_kernel(place_ref, got_ref, ut_ref, mine_ref, theirs_ref, zero_ref, one_ref):
    core = place_ref[4]
    gated = normalised(got_ref) * ut_ref[...].astype(F32)
    for z in range(0, 8, 2):
        for chip in range(HEADS):
            at = z * BLOCK + chip * 8
            one, two = gated[at : at + 8], gated[at + BLOCK : at + BLOCK + 8]
            rows = slice(chip * 32 + z * 4, chip * 32 + z * 4 + 8)
            zero_ref[rows, :] = jnp.concatenate([one[0:4], two[0:4]], axis=0)
            one_ref[rows, :] = jnp.concatenate([one[4:8], two[4:8]], axis=0)
    zero, one = zero_ref[...].astype(BF16), one_ref[...].astype(BF16)
    mine_ref[...] = jnp.where(core == 0, zero, one)
    theirs_ref[...] = jnp.where(core == 0, one, zero)


def d_gate_kernel(got_ref, dg_ref, after_ref, out_ref):
    d_gate = (dg_ref[...] * normalised(got_ref)).astype(BF16)
    for i in range(WIDTH // BLOCK):
        out_ref[:, i * BLOCK : (i + 1) * BLOCK] = d_gate[i * BLOCK : (i + 1) * BLOCK].T


def product_kernel(a_ref, b_ref, c_ref, d_ref, out_ref):
    for at in range(0, 512, 128):
        rows = slice(at, at + 128)
        out_ref[rows, :] = (dot(a_ref[rows, :], c_ref[...]) + dot(b_ref[rows, :], d_ref[...])).astype(BF16)


def finish_kernel(got_ref, dq_ref, dk_ref, dv_ref):
    for i, out_ref in enumerate((dq_ref, dk_ref, dv_ref)):
        for h in range(0, HEADS, 4):
            heads = got_ref[h : h + 4, i * 64 : (i + 1) * 64, :].reshape(256, BLOCK)
            out_ref[:, h * 64 : (h + 4) * 64] = heads.T


SMEM = pl.BlockSpec(memory_space=pltpu.SMEM)
VMEM = pl.BlockSpec(memory_space=pltpu.VMEM)


def call(kernel, name, out_shape, in_specs, args, scratch=(), mib=8, flops=1 << 26, transcendentals=0):
    return pl.pallas_call(
        kernel,
        out_shape=out_shape,
        in_specs=in_specs,
        out_specs=jax.tree.map(lambda _: VMEM, out_shape),
        scratch_shapes=list(scratch),
        compiler_params=pltpu.CompilerParams(vmem_limit_bytes=mib * 1024 * 1024),
        cost_estimate=pl.CostEstimate(flops=flops, bytes_accessed=1 << 21, transcendentals=transcendentals),
        name=name,
    )(*args)


def shape(dims, dtype=BF16):
    return jax.ShapeDtypeStruct(dims, dtype)


def prepare(*args):
    shapes = shape((HEADS, 256, BLOCK)), shape((WIDTH, BLOCK)), shape((WIDTH, BLOCK), F32)
    return call(prepare_kernel, "prepare", shapes, [VMEM] * 6, args, mib=12)


def attend_forward(place, got, other):
    return call(
        forward_kernel,
        "attend_forward",
        (
            shape((256, HALF)),
            shape((HEAD_DIM, HALF)),
            shape((8, HEAD_DIM, BLOCK)),
            shape((8, HEAD_DIM, BLOCK)),
            shape((STATS * N_BLOCKS, BLOCK)),
        ),
        [SMEM, VMEM, VMEM],
        (place, got, other),
        [
            pltpu.VMEM((HALF, HEAD_DIM), BF16),
            pltpu.VMEM((N_BLOCKS, 256, BLOCK), F32),
            pltpu.VMEM((STATS * N_BLOCKS, BLOCK), F32),
        ],
        mib=20,
        flops=1 << 30,
        transcendentals=1 << 22,
    )


def derive(place, x):
    tiles = shape((len(PAIRS), SUB, SUB))
    return call(
        derive_kernel,
        "derive",
        (tiles, tiles) + (shape((HALF, HEAD_DIM)),) * 3,
        [SMEM, VMEM],
        (place, x),
        mib=16,
        flops=1 << 31,
        transcendentals=1 << 22,
    )


def attend_backward(place, x, attn, got, derived):
    return call(
        backward_kernel,
        "attend_backward",
        (shape((8, 192, BLOCK)), shape((8, 192, BLOCK))),
        [SMEM] + [VMEM] * 8,
        (place, x, attn, got) + derived,
        [
            pltpu.VMEM((HALF, HEAD_DIM), BF16),
            pltpu.VMEM((HEAD_DIM, HALF), BF16),
            pltpu.VMEM((HEAD_DIM, HALF), F32),
            pltpu.VMEM((HALF, HEAD_DIM), F32),
            pltpu.VMEM((HALF, HEAD_DIM), F32),
            pltpu.VMEM((N_BLOCKS, 192, BLOCK), F32),
        ],
        mib=20,
        flops=1 << 33,
    )


def on_device(query, key, value, gate_u, out_weight, cotangent, hist_lengths):
    core = lax.axis_index("core")
    place = jnp.concatenate([hist_lengths[0], core[None]]).astype(jnp.int32)

    def swap(x):
        return lax.ppermute(x, "core", SWAP)

    def chips(x):
        return lax.all_to_all(x, CHIP, 0, 0, tiled=True)

    send, u_t, d_gated_t = prepare(query, key, value, gate_u, cotangent, out_weight)
    got = chips(send)
    theirs = call(other_half_kernel, "other_half", shape((8, 256, BLOCK)), [SMEM, VMEM], (place, got))
    x, attn, mine, theirs, stat = attend_forward(place, got, swap(theirs))

    rows = HEAD_DIM + STATS * N_BLOCKS
    send = call(
        attn_to_owners_kernel,
        "attn_to_owners",
        shape((HEADS, rows, BLOCK)),
        [SMEM] + [VMEM] * 3,
        (place, mine, swap(theirs), stat),
    )
    got_attn = chips(send)
    derived = derive(place, x)

    mine, theirs = call(
        gated_kernel,
        "gated",
        (shape((512, BLOCK)), shape((512, BLOCK))),
        [SMEM] + [VMEM] * 2,
        (place, got_attn, u_t),
        [pltpu.VMEM((512, BLOCK), F32)] * 2,
    )
    part = call(
        product_kernel,
        "product",
        shape((512, WIDTH)),
        [VMEM] * 4,
        (mine, swap(theirs), cotangent, swap(cotangent)),
    )
    parts = chips(part.reshape(HEADS, 32, WIDTH))

    mine, theirs = attend_backward(place, x, attn, got_attn, derived)
    send = call(
        to_owners_kernel,
        "grads_to_owners",
        shape((HEADS, 192, BLOCK)),
        [SMEM] + [VMEM] * 2,
        (place, mine, swap(theirs)),
    )
    got = chips(send)
    d_gate = call(
        d_gate_kernel,
        "d_gate",
        shape((BLOCK, WIDTH)),
        [VMEM, VMEM, pl.BlockSpec(memory_space=pl.ANY)],
        (got_attn, d_gated_t, send),
        flops=1 << 20,
    )

    parts, d_gate = lax.optimization_barrier((parts, d_gate))
    part = jnp.sum(parts.astype(F32), axis=0).reshape(4, 2, 4, WIDTH)
    z = lax.axis_index("dp")

    def exchange(x, step):
        return lax.ppermute(x, "dp", [(i, i ^ step) for i in range(8)])

    away = lax.dynamic_index_in_dim(part, 1 - z % 2, 1, keepdims=False)
    part = lax.dynamic_index_in_dim(part, z % 2, 1, keepdims=False) + exchange(away, 1)
    d_weight = lax.dynamic_index_in_dim(part, z // 2, 0, keepdims=False)
    for step in (1, 2, 3):
        away = lax.dynamic_index_in_dim(part, (z // 2) ^ step, 0, keepdims=False)
        d_weight = d_weight + exchange(away, 2 * step)
    d_weight = d_weight * (1.0 / math.sqrt(32768))

    d_query, d_key, d_value = call(finish_kernel, "finish", (shape((BLOCK, WIDTH)),) * 3, [VMEM], (got,))
    return d_query, d_key, d_value, d_gate, d_weight


def solution(mesh):
    axes = ("dp", "x", "y", "core")
    inner = Mesh(mesh.devices.reshape(8, 4, 4, 2), axes)
    rows = P(axes, None)
    return jax.shard_map(
        on_device,
        mesh=inner,
        in_specs=(rows, rows, rows, rows, P(), rows, P("dp", None)),
        out_specs=(rows, rows, rows, rows, rows),
        check_vma=False,
    )
```

```python
import math

import jax
import jax.numpy as jnp
from jax import lax
from jax.experimental import pallas as pl
from jax.experimental.pallas import tpu as pltpu
from jax.sharding import Mesh, PartitionSpec as P

HEADS = 16
HEAD_DIM = 64
WIDTH = HEADS * HEAD_DIM
N_BLOCKS = 16
BLOCK = 128
HALF = N_BLOCKS * BLOCK
SUB = 256
F_TILE = 2048
B_TILE = 1024
STATS = 5
CHIP = ("x", "y")
SWAP = ((0, 1), (1, 0))
BF16 = jnp.bfloat16
F32 = jnp.float32


def dot(a, b):
    return lax.dot_general(a, b, (((1,), (0,)), ((), ())), preferred_element_type=F32)


def dot_nt(a, b):
    return lax.dot_general(a, b, (((1,), (1,)), ((), ())), preferred_element_type=F32)


def sigmoid(s):
    return pltpu.reciprocal(1.0 + jnp.exp(-s), approx=True)


def lanes():
    return lax.broadcasted_iota(jnp.int32, (1, BLOCK), 1)


def place_of(place_ref):
    first, second, third = (place_ref[i] for i in range(3))
    core = place_ref[4]
    is_first, is_second = first == HALF, second == HALF
    begin = jnp.where(is_first, 0, jnp.where(is_second, first, first + second + jnp.where(third == HALF, 0, third)))
    end1 = jnp.where(is_first, second, first)
    end2 = end1 + jnp.where(is_first | is_second, third, second)
    turn = jnp.where(core == 0, begin & (HALF - 1), 0)
    return core, begin, turn, jnp.where(core == 0, HALF, end1), jnp.where(core == 0, HALF, end2)


def low_is_mine(j, core, begin):
    return ((2 * j + core) * BLOCK + lanes() >= begin) == (core == 0)


def live_of(q_at, k_at, end1, end2, diagonal):
    q_place = q_at + lax.broadcasted_iota(jnp.int32, (1, SUB), 1)
    k_place = k_at + lax.broadcasted_iota(jnp.int32, (SUB, 1), 0)
    start = jnp.where(q_place < end1, 0, jnp.where(q_place < end2, end1, end2))
    live = k_place >= start
    return live & (k_place <= q_place) if diagonal else live


def below(n_tiles, tile):
    n_sub = tile // SUB
    for i in range(n_tiles):
        for j in range(i + 1):
            subs = [(q, k) for q in range(n_sub) for k in range(n_sub) if j < i or k <= q]
            yield i * tile, j * tile, subs


def forward_kernel(
    place_ref, got_ref, other_ref, x_ref, attn_ref, mine_ref, theirs_ref, stat_ref, k_ref, slot_ref, stats_ref
):
    core, begin, turn, end1, end2 = place_of(place_ref)
    whole, rest = turn // BLOCK, turn % BLOCK
    lane = lanes()
    for b in range(N_BLOCKS):
        j = b // 2
        mine = jnp.where(low_is_mine(j, core, begin), got_ref[j], got_ref[8 + j])
        here = jnp.where(core == b % 2, mine, other_ref[j])
        slot_ref[b] = pltpu.roll(here.astype(F32), lax.rem(BLOCK - rest, BLOCK), 1)
    for b in range(N_BLOCKS):
        first, second = slot_ref[lax.rem(b + whole, N_BLOCKS)], slot_ref[lax.rem(b + whole + 1, N_BLOCKS)]
        here = jnp.where(lane < BLOCK - rest, first, second)
        x_ref[0:64, b * BLOCK : (b + 1) * BLOCK] = (here[0:64] * 0.125).astype(BF16)
        x_ref[64:256, b * BLOCK : (b + 1) * BLOCK] = here[64:256].astype(BF16)
        k_ref[b * BLOCK : (b + 1) * BLOCK, :] = here[64:128].astype(BF16).T

    for q_at, k_at, subs in below(HALF // F_TILE, F_TILE):
        weights = {}
        for q, k in subs:
            q_sub, k_sub = q_at + q * SUB, k_at + k * SUB
            s = dot(k_ref[k_sub : k_sub + SUB, :], x_ref[0:64, q_sub : q_sub + SUB])
            live = live_of(q_sub, k_sub, end1, end2, q_sub == k_sub)
            weights[q, k] = jnp.where(live, s * sigmoid(s), 0.0).astype(BF16)
        for q in range(F_TILE // SUB):
            q_sub = q_at + q * SUB
            acc = jnp.zeros((HEAD_DIM, SUB), F32)
            for k in range(F_TILE // SUB):
                if (q, k) in weights:
                    k_sub = k_at + k * SUB
                    acc += dot(x_ref[128:192, k_sub : k_sub + SUB], weights[q, k])
            attn_ref[:, q_sub : q_sub + SUB] = acc.astype(BF16)

    turned = []
    for b in range(N_BLOCKS):
        cols = slice(b * BLOCK, (b + 1) * BLOCK)
        attn = attn_ref[:, cols].astype(F32)
        g = x_ref[192:256, cols].astype(F32)
        mean = jnp.mean(attn, axis=0, keepdims=True)
        centre = attn - mean
        both = jnp.sum(centre * g, axis=0, keepdims=True)
        mean_hi = mean.astype(BF16).astype(F32)
        square = jnp.sum(centre * centre, axis=0, keepdims=True)
        total = jnp.sum(g, axis=0, keepdims=True)
        for i, row in enumerate((mean_hi, mean - mean_hi, both, square, total)):
            stats_ref[i * N_BLOCKS + b : i * N_BLOCKS + b + 1, :] = row
        turned.append(attn)
    stat_ref[...] = stats_ref[...].astype(BF16)
    turn_out(turned, turn, core, slot_ref, mine_ref, theirs_ref)


def turn_out(blocks, turn, core, slot_ref, mine_ref, theirs_ref):
    whole, rest = turn // BLOCK, turn % BLOCK
    rows = blocks[0].shape[0]
    for b, block in enumerate(blocks):
        slot_ref[b, 0:rows, :] = pltpu.roll(block, rest, 1)
    from_this = lanes() >= rest
    for j in range(8):
        pair = []
        for b in (2 * j, 2 * j + 1):
            this = slot_ref[lax.rem(b - whole + N_BLOCKS, N_BLOCKS), 0:rows, :]
            last = slot_ref[lax.rem(b - whole + N_BLOCKS - 1, N_BLOCKS), 0:rows, :]
            pair.append(jnp.where(from_this, this, last).astype(BF16))
        mine_ref[j] = jnp.where(core == 0, pair[0], pair[1])
        theirs_ref[j] = jnp.where(core == 0, pair[1], pair[0])


GROUPS = [[(q_at // SUB + q, k_at // SUB + k) for q, k in subs] for q_at, k_at, subs in below(HALF // B_TILE, B_TILE)]
PAIRS = [pair for group in GROUPS for pair in group]
AT = {pair: i for i, pair in enumerate(PAIRS)}


def group_copies(from_ref, to_ref, sems):
    copies, at = [], 0
    for i, group in enumerate(GROUPS):
        part = pl.ds(at, len(group))
        copies.append(pltpu.make_async_copy(from_ref.at[part], to_ref.at[part], sems.at[i]))
        at += len(group)
    return copies


def derive_kernel(
    place_ref, x_ref, silu_out, slope_out, q_out, v_out,
    silu_ref, slope_ref, qn_ref, kn_ref, vn_ref, silu_sems, slope_sems, sems,
):
    end1, end2 = place_of(place_ref)[3:]
    for b in range(N_BLOCKS):
        cols = slice(b * BLOCK, (b + 1) * BLOCK)
        for i, out_ref in enumerate((qn_ref, kn_ref, vn_ref)):
            out_ref[cols, :] = x_ref[i * 64 : (i + 1) * 64, cols].T
    copies = [
        pltpu.make_async_copy(qn_ref, q_out, sems.at[0]),
        pltpu.make_async_copy(vn_ref, v_out, sems.at[1]),
    ]
    for copy in copies:
        copy.start()
    silu_copies = group_copies(silu_ref, silu_out, silu_sems)
    slope_copies = group_copies(slope_ref, slope_out, slope_sems)
    for i, group in enumerate(GROUPS):
        for q, k in group:
            q_cols, k_cols = slice(q * SUB, (q + 1) * SUB), slice(k * SUB, (k + 1) * SUB)
            s = dot(kn_ref[k_cols, :], x_ref[0:64, q_cols])
            sigma = jnp.where(live_of(q * SUB, k * SUB, end1, end2, q == k), sigmoid(s), 0.0)
            silu = s * sigma
            silu_ref[AT[q, k]] = silu.astype(BF16)
            slope_ref[AT[q, k]] = (sigma + silu * (1.0 - sigma)).astype(BF16)
        silu_copies[i].start()
        slope_copies[i].start()
    for copy in copies + silu_copies + slope_copies:
        copy.wait()


def backward_kernel(
    place_ref, x_ref, attn_ref, got_ref, silu_in, slope_in, q_in, v_in, mine_ref, theirs_ref,
    silu_ref, slope_ref, qn_ref, vn_ref, dn_ref, dt_ref, dq_ref, dk_ref, dv_ref, slot_ref,
    silu_sems, slope_sems, sems,
):
    v_copy = pltpu.make_async_copy(v_in, vn_ref, sems.at[1])
    q_copy = pltpu.make_async_copy(q_in, qn_ref, sems.at[0])
    silu_copies = group_copies(silu_in, silu_ref, silu_sems)
    slope_copies = group_copies(slope_in, slope_ref, slope_sems)
    v_copy.start()
    slope_copies[0].start()
    silu_copies[0].start()
    q_copy.start()
    for i in range(1, len(GROUPS)):
        slope_copies[i].start()
        silu_copies[i].start()
    core, _, turn, end1, end2 = place_of(place_ref)
    stat = got_ref[:, 64 : 64 + STATS * N_BLOCKS, :].astype(F32).reshape(HEADS, STATS, N_BLOCKS, BLOCK)
    mean_h = stat[:, 0] + stat[:, 1]
    mean = jnp.mean(mean_h, axis=0)
    off = mean_h - mean[None]
    square = jnp.sum(stat[:, 3] + HEAD_DIM * off * off, axis=0)
    rstd = lax.rsqrt(square * (1.0 / WIDTH) + 1e-05)
    g_sum = stat[:, 4]
    g_mean = jnp.sum(g_sum, axis=0) * (1.0 / WIDTH)
    both = jnp.sum(stat[:, 2] + off * g_sum, axis=0) * rstd * (1.0 / WIDTH)
    for b in range(N_BLOCKS):
        cols = slice(b * BLOCK, (b + 1) * BLOCK)
        r = rstd[b : b + 1]
        normed = (attn_ref[:, cols].astype(F32) - mean[b : b + 1]) * r
        d = (r * (x_ref[192:256, cols].astype(F32) - g_mean[b : b + 1] - normed * both[b : b + 1])).astype(BF16)
        dt_ref[:, cols] = d
        dn_ref[cols, :] = d.T

    v_copy.wait()
    for i, (q_at, k_at, subs) in enumerate(below(HALF // B_TILE, B_TILE)):
        slope_copies[i].wait()
        n = B_TILE // SUB
        q_first, k_first = q_at // SUB, k_at // SUB
        made = {}
        for q, k in subs:
            q_cols = slice(q_at + q * SUB, q_at + (q + 1) * SUB)
            k_cols = slice(k_at + k * SUB, k_at + (k + 1) * SUB)
            d_p = dot(vn_ref[k_cols, :], dt_ref[:, q_cols])
            made[q, k] = (d_p * slope_ref[AT[q_first + q, k_first + k]].astype(F32)).astype(BF16)
        silu_copies[i].wait()
        if i == 0:
            q_copy.wait()
        for k in range(n):
            k_cols = slice(k_at + k * SUB, k_at + (k + 1) * SUB)
            d_v, d_k = [], []
            for q in range(n):
                if (q, k) in made:
                    q_cols = slice(q_at + q * SUB, q_at + (q + 1) * SUB)
                    d_v.append(dot(silu_ref[AT[q_first + q, k_first + k]], dn_ref[q_cols, :]))
                    d_k.append(dot(made[q, k], qn_ref[q_cols, :]))
            if q_at == k_at:
                dv_ref[k_cols, :], dk_ref[k_cols, :] = sum(d_v), sum(d_k)
            else:
                dv_ref[k_cols, :] += sum(d_v)
                dk_ref[k_cols, :] += sum(d_k)
        for q in range(n):
            q_cols = slice(q_at + q * SUB, q_at + (q + 1) * SUB)
            d_q = []
            for k in range(n):
                if (q, k) in made:
                    d_q.append(dot(x_ref[64:128, k_at + k * SUB : k_at + (k + 1) * SUB], made[q, k]))
            if k_at == 0:
                dq_ref[:, q_cols] = sum(d_q)
            else:
                dq_ref[:, q_cols] += sum(d_q)

    turned = []
    for b in range(N_BLOCKS):
        cols = slice(b * BLOCK, (b + 1) * BLOCK)
        turned.append(jnp.concatenate([dq_ref[:, cols] * 0.125, dk_ref[cols, :].T, dv_ref[cols, :].T], axis=0))
    turn_out(turned, turn, core, slot_ref, mine_ref, theirs_ref)


def prepare_kernel(
    q_in, k_in, v_in, u_in, cot_in, w_in, send_out, ut_out, dg_out,
    q_ref, k_ref, v_ref, u_ref, cot_ref, w_ref, send_ref, ut_ref, dg_ref, in_sems, w_sems, out_sems,
):
    pairs = (q_in, q_ref), (k_in, k_ref), (v_in, v_ref), (cot_in, cot_ref), (u_in, u_ref)
    copies = [pltpu.make_async_copy(a, b, in_sems.at[i]) for i, (a, b) in enumerate(pairs)]
    parts = [pl.ds(at, 256) for at in range(0, WIDTH, 256)]
    heads = [pl.ds(at, 4) for at in range(0, HEADS, 4)]
    w_copies = [pltpu.make_async_copy(w_in.at[part], w_ref.at[part], w_sems.at[i]) for i, part in enumerate(parts)]
    outs = [
        [
            pltpu.make_async_copy(send_ref.at[heads[i]], send_out.at[heads[i]], out_sems.at[0, i]),
            pltpu.make_async_copy(ut_ref.at[parts[i]], ut_out.at[parts[i]], out_sems.at[1, i]),
            pltpu.make_async_copy(dg_ref.at[parts[i]], dg_out.at[parts[i]], out_sems.at[2, i]),
        ]
        for i in range(4)
    ]
    for copy in copies + w_copies:
        copy.start()
    for i, ref in enumerate((q_ref, k_ref, v_ref)):
        copies[i].wait()
        for at in range(0, WIDTH, 256):
            rows = ref[:, at : at + 256].T
            for h in range(4):
                send_ref[at // 64 + h, i * 64 : (i + 1) * 64, :] = rows[h * 64 : (h + 1) * 64]
    copies[3].wait()
    copies[4].wait()
    for i in range(4):
        cols = slice(i * 256, (i + 1) * 256)
        u_t = u_ref[:, cols].T
        w_copies[i].wait()
        d_gated = dot_nt(w_ref[cols, :], cot_ref[...])
        dg_ref[cols, :] = d_gated
        ut_ref[cols, :] = u_t
        g_t = (d_gated * u_t.astype(F32)).astype(BF16)
        for h in range(4):
            send_ref[4 * i + h, 192:256, :] = g_t[h * 64 : (h + 1) * 64]
        for copy in outs[i]:
            copy.start()
    for out in outs:
        for copy in out:
            copy.wait()


def other_half_kernel(place_ref, got_ref, out_ref):
    core, begin = place_of(place_ref)[:2]
    for j in range(8):
        out_ref[j] = jnp.where(low_is_mine(j, core, begin), got_ref[8 + j], got_ref[j])


def to_owners_kernel(place_ref, mine_ref, theirs_ref, out_ref):
    core, begin = place_of(place_ref)[:2]
    for j in range(8):
        low_mine = low_is_mine(j, core, begin)
        mine, theirs = mine_ref[j], theirs_ref[j]
        out_ref[j] = jnp.where(low_mine, mine, theirs)
        out_ref[8 + j] = jnp.where(low_mine, theirs, mine)


def attn_to_owners_kernel(place_ref, mine_ref, theirs_ref, stat_ref, out_ref):
    to_owners_kernel(place_ref, mine_ref, theirs_ref, out_ref.at[:, 0:64, :])
    for j in range(HEADS):
        out_ref[j, 64:, :] = stat_ref[...]


def normalised(got_ref):
    attn = got_ref[:, 0:64, :].astype(F32).reshape(WIDTH, BLOCK)
    centre = attn - jnp.mean(attn, axis=0, keepdims=True)
    return centre * lax.rsqrt(jnp.mean(centre * centre, axis=0, keepdims=True) + 1e-05)


def gated_kernel(place_ref, got_ref, ut_ref, mine_ref, theirs_ref, zero_ref, one_ref):
    core = place_ref[4]
    gated = normalised(got_ref) * ut_ref[...].astype(F32)
    for z in (0, 1, 4, 5):
        for chip in range(HEADS):
            at = z * BLOCK + chip * 8
            one, two = gated[at : at + 8], gated[at + 2 * BLOCK : at + 2 * BLOCK + 8]
            row = (z % 2) * 256 + chip * 16 + (z // 2) * 4
            rows = slice(row, row + 8)
            zero_ref[rows, :] = jnp.concatenate([one[0:4], two[0:4]], axis=0)
            one_ref[rows, :] = jnp.concatenate([one[4:8], two[4:8]], axis=0)
    zero, one = zero_ref[...].astype(BF16), one_ref[...].astype(BF16)
    mine_ref[...] = jnp.where(core == 0, zero, one)
    theirs_ref[...] = jnp.where(core == 0, one, zero)


def d_gate_kernel(got_ref, dg_ref, after_ref, out_ref):
    d_gate = (dg_ref[...] * normalised(got_ref)).astype(BF16)
    for i in range(WIDTH // BLOCK):
        out_ref[:, i * BLOCK : (i + 1) * BLOCK] = d_gate[i * BLOCK : (i + 1) * BLOCK].T


def product_kernel(a_ref, b_ref, c_ref, d_ref, out_ref):
    for at in range(0, 512, 128):
        rows = slice(at, at + 128)
        out_ref[rows, :] = (dot(a_ref[rows, :], c_ref[...]) + dot(b_ref[rows, :], d_ref[...])).astype(BF16)


def finish_kernel(got_ref, dq_ref, dk_ref, dv_ref):
    for i, out_ref in enumerate((dq_ref, dk_ref, dv_ref)):
        for h in range(0, HEADS, 4):
            heads = got_ref[h : h + 4, i * 64 : (i + 1) * 64, :].reshape(256, BLOCK)
            out_ref[:, h * 64 : (h + 4) * 64] = heads.T


SMEM = pl.BlockSpec(memory_space=pltpu.SMEM)
VMEM = pl.BlockSpec(memory_space=pltpu.VMEM)
ANY = pl.BlockSpec(memory_space=pl.ANY)
DMA = pltpu.SemaphoreType.DMA


def call(kernel, name, out_shape, in_specs, args, scratch=(), out=VMEM, mib=8, flops=1 << 26, transcendentals=0):
    return pl.pallas_call(
        kernel,
        out_shape=out_shape,
        in_specs=in_specs,
        out_specs=jax.tree.map(lambda _: out, out_shape),
        scratch_shapes=list(scratch),
        compiler_params=pltpu.CompilerParams(vmem_limit_bytes=mib * 1024 * 1024),
        cost_estimate=pl.CostEstimate(flops=flops, bytes_accessed=1 << 21, transcendentals=transcendentals),
        name=name,
    )(*args)


def shape(dims, dtype=BF16):
    return jax.ShapeDtypeStruct(dims, dtype)


def prepare(*args):
    shapes = shape((HEADS, 256, BLOCK)), shape((WIDTH, BLOCK)), shape((WIDTH, BLOCK), F32)
    return call(
        prepare_kernel,
        "prepare",
        shapes,
        [ANY] * 6,
        args,
        [pltpu.VMEM((BLOCK, WIDTH), BF16)] * 5
        + [pltpu.VMEM((WIDTH, WIDTH), BF16)]
        + [pltpu.VMEM(s.shape, s.dtype) for s in shapes]
        + [DMA((5,)), DMA((4,)), DMA((3, 4))],
        out=ANY,
        mib=12,
    )


def attend_forward(place, got, other):
    return call(
        forward_kernel,
        "attend_forward",
        (
            shape((256, HALF)),
            shape((HEAD_DIM, HALF)),
            shape((8, HEAD_DIM, BLOCK)),
            shape((8, HEAD_DIM, BLOCK)),
            shape((STATS * N_BLOCKS, BLOCK)),
        ),
        [SMEM, VMEM, VMEM],
        (place, got, other),
        [
            pltpu.VMEM((HALF, HEAD_DIM), BF16),
            pltpu.VMEM((N_BLOCKS, 256, BLOCK), F32),
            pltpu.VMEM((STATS * N_BLOCKS, BLOCK), F32),
        ],
        mib=20,
        flops=1 << 30,
        transcendentals=1 << 22,
    )


def derive(place, x):
    tiles, rows = (len(PAIRS), SUB, SUB), (HALF, HEAD_DIM)
    return call(
        derive_kernel,
        "derive",
        (shape(tiles), shape(tiles), shape(rows), shape(rows)),
        [SMEM, VMEM],
        (place, x),
        [pltpu.VMEM(tiles, BF16)] * 2
        + [pltpu.VMEM(rows, BF16)] * 3
        + [DMA((len(GROUPS),)), DMA((len(GROUPS),)), DMA((2,))],
        out=ANY,
        mib=24,
        flops=1 << 31,
        transcendentals=1 << 22,
    )


def attend_backward(place, x, attn, got, derived):
    tiles, rows = (len(PAIRS), SUB, SUB), (HALF, HEAD_DIM)
    return call(
        backward_kernel,
        "attend_backward",
        (shape((8, 192, BLOCK)), shape((8, 192, BLOCK))),
        [SMEM] + [VMEM] * 3 + [ANY] * 4,
        (place, x, attn, got) + derived,
        [pltpu.VMEM(tiles, BF16)] * 2
        + [pltpu.VMEM(rows, BF16)] * 3
        + [
            pltpu.VMEM((HEAD_DIM, HALF), BF16),
            pltpu.VMEM((HEAD_DIM, HALF), F32),
            pltpu.VMEM(rows, F32),
            pltpu.VMEM(rows, F32),
            pltpu.VMEM((N_BLOCKS, 192, BLOCK), F32),
        ]
        + [DMA((len(GROUPS),)), DMA((len(GROUPS),)), DMA((2,))],
        mib=32,
        flops=1 << 33,
    )


def on_device(query, key, value, gate_u, out_weight, cotangent, hist_lengths):
    core = lax.axis_index("core")
    place = jnp.concatenate([hist_lengths[0], core[None]]).astype(jnp.int32)

    def swap(x):
        return lax.ppermute(x, "core", SWAP)

    def chips(x):
        return lax.all_to_all(x, CHIP, 0, 0, tiled=True)

    send, u_t, d_gated_t = prepare(query, key, value, gate_u, cotangent, out_weight)
    got = chips(send)
    theirs = call(other_half_kernel, "other_half", shape((8, 256, BLOCK)), [SMEM, VMEM], (place, got))
    x, attn, mine, theirs, stat = attend_forward(place, got, swap(theirs))

    rows = HEAD_DIM + STATS * N_BLOCKS
    send = call(
        attn_to_owners_kernel,
        "attn_to_owners",
        shape((HEADS, rows, BLOCK)),
        [SMEM] + [VMEM] * 3,
        (place, mine, swap(theirs), stat),
    )
    got_attn = chips(send)
    got_attn, derived = lax.optimization_barrier((got_attn, derive(place, x)))

    mine, theirs = call(
        gated_kernel,
        "gated",
        (shape((512, BLOCK)), shape((512, BLOCK))),
        [SMEM] + [VMEM] * 2,
        (place, got_attn, u_t),
        [pltpu.VMEM((512, BLOCK), F32)] * 2,
    )
    part = call(
        product_kernel,
        "product",
        shape((512, WIDTH)),
        [VMEM] * 4,
        (mine, swap(theirs), cotangent, swap(cotangent)),
    )
    parts = lax.all_to_all(part.reshape(32, 16, WIDTH), ("zl",) + CHIP, 0, 0, tiled=True)

    mine, theirs = attend_backward(place, x, attn, got_attn, derived)
    send = call(
        to_owners_kernel,
        "grads_to_owners",
        shape((HEADS, 192, BLOCK)),
        [SMEM] + [VMEM] * 2,
        (place, mine, swap(theirs)),
    )
    got = chips(send)
    d_gate = call(
        d_gate_kernel,
        "d_gate",
        shape((BLOCK, WIDTH)),
        [VMEM, VMEM, ANY],
        (got_attn, d_gated_t, send),
        flops=1 << 20,
    )

    parts, d_gate = lax.optimization_barrier((parts, d_gate))
    part = jnp.sum(parts.astype(F32), axis=0).reshape(4, 4, WIDTH)
    z = lax.axis_index("zh")
    for step in (2, 1):
        high = (z // step) % 2
        halves = part.reshape(2, step, 4, WIDTH)
        away = lax.dynamic_index_in_dim(halves, 1 - high, 0, keepdims=False)
        kept = lax.dynamic_index_in_dim(halves, high, 0, keepdims=False)
        part = kept + lax.ppermute(away, "zh", [(i, i ^ step) for i in range(4)])
    d_weight = part.reshape(4, WIDTH) * (1.0 / math.sqrt(32768))

    d_query, d_key, d_value = call(finish_kernel, "finish", (shape((BLOCK, WIDTH)),) * 3, [VMEM], (got,))
    return d_query, d_key, d_value, d_gate, d_weight


def solution(mesh):
    axes = ("zh", "zl", "x", "y", "core")
    inner = Mesh(mesh.devices.reshape(4, 2, 4, 4, 2), axes)
    rows = P(axes, None)
    return jax.shard_map(
        on_device,
        mesh=inner,
        in_specs=(rows, rows, rows, rows, P(), rows, P(("zh", "zl"), None)),
        out_specs=(rows, rows, rows, rows, rows),
        check_vma=False,
    )
```

```python
import math

import jax
import jax.numpy as jnp
from jax import lax
from jax.experimental import pallas as pl
from jax.experimental.pallas import tpu as pltpu
from jax.sharding import Mesh, PartitionSpec as P

HEADS = 16
HEAD_DIM = 64
WIDTH = HEADS * HEAD_DIM
N_BLOCKS = 16
BLOCK = 128
HALF = N_BLOCKS * BLOCK
SUB = 256
F_TILE = 2048
B_TILE = 1024
STATS = 5
TILES_MIB = 45
CHIP = ("x", "y")
SWAP = ((0, 1), (1, 0))
BF16 = jnp.bfloat16
F32 = jnp.float32


def dot(a, b):
    return lax.dot_general(a, b, (((1,), (0,)), ((), ())), preferred_element_type=F32)


def dot_nt(a, b):
    return lax.dot_general(a, b, (((1,), (1,)), ((), ())), preferred_element_type=F32)


def sigmoid(s):
    return pltpu.reciprocal(1.0 + jnp.exp(-s), approx=True)


def lanes():
    return lax.broadcasted_iota(jnp.int32, (1, BLOCK), 1)


def place_of(place_ref):
    first, second, third = (place_ref[i] for i in range(3))
    core = place_ref[4]
    is_first, is_second = first == HALF, second == HALF
    begin = jnp.where(is_first, 0, jnp.where(is_second, first, first + second + jnp.where(third == HALF, 0, third)))
    end1 = jnp.where(is_first, second, first)
    end2 = end1 + jnp.where(is_first | is_second, third, second)
    turn = jnp.where(core == 0, begin & (HALF - 1), 0)
    return core, begin, turn, jnp.where(core == 0, HALF, end1), jnp.where(core == 0, HALF, end2)


def low_is_mine(j, core, begin):
    return ((2 * j + core) * BLOCK + lanes() >= begin) == (core == 0)


def live_of(q_at, k_at, end1, end2, diagonal):
    q_place = q_at + lax.broadcasted_iota(jnp.int32, (1, SUB), 1)
    k_place = k_at + lax.broadcasted_iota(jnp.int32, (SUB, 1), 0)
    start = jnp.where(q_place < end1, 0, jnp.where(q_place < end2, end1, end2))
    live = k_place >= start
    return live & (k_place <= q_place) if diagonal else live


def below(n_tiles, tile):
    n_sub = tile // SUB
    for i in range(n_tiles):
        for j in range(i + 1):
            subs = [(q, k) for q in range(n_sub) for k in range(n_sub) if j < i or k <= q]
            yield i * tile, j * tile, subs


def forward_kernel(
    place_ref, got_ref, other_ref, x_ref, mine_ref, theirs_ref, stat_ref, k_ref, slot_ref, stats_ref
):
    core, begin, turn, end1, end2 = place_of(place_ref)
    whole, rest = turn // BLOCK, turn % BLOCK
    lane = lanes()
    for b in range(N_BLOCKS):
        j = b // 2
        mine = jnp.where(low_is_mine(j, core, begin), got_ref[j], got_ref[8 + j])
        here = jnp.where(core == b % 2, mine, other_ref[j])
        slot_ref[b] = pltpu.roll(here.astype(F32), lax.rem(BLOCK - rest, BLOCK), 1)
    for b in range(N_BLOCKS):
        first, second = slot_ref[lax.rem(b + whole, N_BLOCKS)], slot_ref[lax.rem(b + whole + 1, N_BLOCKS)]
        here = jnp.where(lane < BLOCK - rest, first, second)
        x_ref[0:64, b * BLOCK : (b + 1) * BLOCK] = (here[0:64] * 0.125).astype(BF16)
        x_ref[64:256, b * BLOCK : (b + 1) * BLOCK] = here[64:256].astype(BF16)
        k_ref[b * BLOCK : (b + 1) * BLOCK, :] = here[64:128].astype(BF16).T

    for q_at, k_at, subs in below(HALF // F_TILE, F_TILE):
        weights = {}
        for q, k in subs:
            q_sub, k_sub = q_at + q * SUB, k_at + k * SUB
            s = dot(k_ref[k_sub : k_sub + SUB, :], x_ref[0:64, q_sub : q_sub + SUB])
            live = live_of(q_sub, k_sub, end1, end2, q_sub == k_sub)
            weights[q, k] = jnp.where(live, s * sigmoid(s), 0.0).astype(BF16)
        for q in range(F_TILE // SUB):
            q_sub = q_at + q * SUB
            acc = jnp.zeros((HEAD_DIM, SUB), F32)
            for k in range(F_TILE // SUB):
                if (q, k) in weights:
                    k_sub = k_at + k * SUB
                    acc += dot(x_ref[128:192, k_sub : k_sub + SUB], weights[q, k])
            x_ref[256:320, q_sub : q_sub + SUB] = acc.astype(BF16)

    turned = []
    for b in range(N_BLOCKS):
        cols = slice(b * BLOCK, (b + 1) * BLOCK)
        attn = x_ref[256:320, cols].astype(F32)
        g = x_ref[192:256, cols].astype(F32)
        mean = jnp.mean(attn, axis=0, keepdims=True)
        centre = attn - mean
        both = jnp.sum(centre * g, axis=0, keepdims=True)
        mean_hi = mean.astype(BF16).astype(F32)
        square = jnp.sum(centre * centre, axis=0, keepdims=True)
        total = jnp.sum(g, axis=0, keepdims=True)
        for i, row in enumerate((mean_hi, mean - mean_hi, both, square, total)):
            stats_ref[i * N_BLOCKS + b : i * N_BLOCKS + b + 1, :] = row
        turned.append(attn)
    stat_ref[...] = stats_ref[...].astype(BF16)
    turn_out(turned, turn, core, slot_ref, mine_ref, theirs_ref)


def turn_out(blocks, turn, core, slot_ref, mine_ref, theirs_ref):
    whole, rest = turn // BLOCK, turn % BLOCK
    rows = blocks[0].shape[0]
    for b, block in enumerate(blocks):
        slot_ref[b, 0:rows, :] = pltpu.roll(block, rest, 1)
    from_this = lanes() >= rest
    for j in range(8):
        pair = []
        for b in (2 * j, 2 * j + 1):
            this = slot_ref[lax.rem(b - whole + N_BLOCKS, N_BLOCKS), 0:rows, :]
            last = slot_ref[lax.rem(b - whole + N_BLOCKS - 1, N_BLOCKS), 0:rows, :]
            pair.append(jnp.where(from_this, this, last).astype(BF16))
        mine_ref[j] = jnp.where(core == 0, pair[0], pair[1])
        theirs_ref[j] = jnp.where(core == 0, pair[1], pair[0])


GROUPS = [[(q_at // SUB + q, k_at // SUB + k) for q, k in subs] for q_at, k_at, subs in below(HALF // B_TILE, B_TILE)]
PAIRS = [pair for group in GROUPS for pair in group]
AT = {pair: i for i, pair in enumerate(PAIRS)}
ROWS_AT = 2 * len(PAIRS)
Q_LANES, V_LANES = slice(0, 64), slice(128, 192)


def group_copies(from_ref, to_ref, sems):
    silu, slope, at = [], [], 0
    for i, group in enumerate(GROUPS):
        for j, copies in enumerate((silu, slope)):
            part = pl.ds(j * len(PAIRS) + at, len(group))
            copies.append(pltpu.make_async_copy(from_ref.at[part], to_ref.at[part], sems.at[j, i]))
        at += len(group)
    part = pl.ds(ROWS_AT, HALF // SUB)
    return silu, slope, pltpu.make_async_copy(from_ref.at[part], to_ref.at[part], sems.at[0, len(GROUPS)])


def derive_kernel(
    place_ref, x_ref, tile_out, tile_ref, kn_ref, tile_sems
):
    end1, end2 = place_of(place_ref)[3:]
    for b in range(N_BLOCKS):
        cols = slice(b * BLOCK, (b + 1) * BLOCK)
        rows = slice((b % 2) * BLOCK, (b % 2 + 1) * BLOCK)
        tile_ref[ROWS_AT + b // 2, rows, Q_LANES] = x_ref[0:64, cols].T
        tile_ref[ROWS_AT + b // 2, rows, V_LANES] = x_ref[128:192, cols].T
        kn_ref[cols, :] = x_ref[64:128, cols].T
    silu_copies, slope_copies, rows_copy = group_copies(tile_ref, tile_out, tile_sems)
    rows_copy.start()
    for i, group in enumerate(GROUPS):
        for q, k in group:
            q_cols, k_cols = slice(q * SUB, (q + 1) * SUB), slice(k * SUB, (k + 1) * SUB)
            s = dot(kn_ref[k_cols, :], x_ref[0:64, q_cols])
            sigma = jnp.where(live_of(q * SUB, k * SUB, end1, end2, q == k), sigmoid(s), 0.0)
            silu = s * sigma
            tile_ref[AT[q, k]] = silu.astype(BF16)
            tile_ref[len(PAIRS) + AT[q, k]] = (sigma + silu * (1.0 - sigma)).astype(BF16)
        silu_copies[i].start()
        slope_copies[i].start()
    for copy in [rows_copy] + silu_copies + slope_copies:
        copy.wait()


def backward_kernel(
    place_ref, x_ref, got_ref, tile_in, mine_ref, theirs_ref,
    tile_ref, dn_ref, dt_ref, dq_ref, dk_ref, dv_ref, slot_ref,
    tile_sems,
):
    silu_copies, slope_copies, rows_copy = group_copies(tile_in, tile_ref, tile_sems)
    rows_copy.start()
    for i in range(len(GROUPS)):
        slope_copies[i].start()
        silu_copies[i].start()
    core, _, turn, end1, end2 = place_of(place_ref)
    stat = got_ref[:, 64 : 64 + STATS * N_BLOCKS, :].astype(F32).reshape(HEADS, STATS, N_BLOCKS, BLOCK)
    mean_h = stat[:, 0] + stat[:, 1]
    mean = jnp.mean(mean_h, axis=0)
    off = mean_h - mean[None]
    square = jnp.sum(stat[:, 3] + HEAD_DIM * off * off, axis=0)
    rstd = lax.rsqrt(square * (1.0 / WIDTH) + 1e-05)
    g_sum = stat[:, 4]
    g_mean = jnp.sum(g_sum, axis=0) * (1.0 / WIDTH)
    both = jnp.sum(stat[:, 2] + off * g_sum, axis=0) * rstd * (1.0 / WIDTH)
    for b in range(N_BLOCKS):
        cols = slice(b * BLOCK, (b + 1) * BLOCK)
        r = rstd[b : b + 1]
        normed = (x_ref[256:320, cols].astype(F32) - mean[b : b + 1]) * r
        d = (r * (x_ref[192:256, cols].astype(F32) - g_mean[b : b + 1] - normed * both[b : b + 1])).astype(BF16)
        dt_ref[:, cols] = d
        dn_ref[cols, :] = d.T

    rows_copy.wait()
    for i, (q_at, k_at, subs) in enumerate(below(HALF // B_TILE, B_TILE)):
        slope_copies[i].wait()
        n = B_TILE // SUB
        q_first, k_first = q_at // SUB, k_at // SUB
        made = {}
        for q, k in subs:
            q_cols = slice(q_at + q * SUB, q_at + (q + 1) * SUB)
            k_cols = slice(k_at + k * SUB, k_at + (k + 1) * SUB)
            d_p = dot(tile_ref[ROWS_AT + k_first + k, :, V_LANES], dt_ref[:, q_cols])
            made[q, k] = (d_p * tile_ref[len(PAIRS) + AT[q_first + q, k_first + k]].astype(F32)).astype(BF16)
        silu_copies[i].wait()
        for k in range(n):
            k_cols = slice(k_at + k * SUB, k_at + (k + 1) * SUB)
            d_v, d_k = [], []
            for q in range(n):
                if (q, k) in made:
                    q_cols = slice(q_at + q * SUB, q_at + (q + 1) * SUB)
                    d_v.append(dot(tile_ref[AT[q_first + q, k_first + k]], dn_ref[q_cols, :]))
                    d_k.append(dot(made[q, k], tile_ref[ROWS_AT + q_first + q, :, Q_LANES]))
            if q_at == k_at:
                dv_ref[k_cols, :], dk_ref[k_cols, :] = sum(d_v), sum(d_k)
            else:
                dv_ref[k_cols, :] += sum(d_v)
                dk_ref[k_cols, :] += sum(d_k)
        for q in range(n):
            q_cols = slice(q_at + q * SUB, q_at + (q + 1) * SUB)
            d_q = []
            for k in range(n):
                if (q, k) in made:
                    d_q.append(dot(x_ref[64:128, k_at + k * SUB : k_at + (k + 1) * SUB], made[q, k]))
            if k_at == 0:
                dq_ref[:, q_cols] = sum(d_q)
            else:
                dq_ref[:, q_cols] += sum(d_q)

    turned = []
    for b in range(N_BLOCKS):
        cols = slice(b * BLOCK, (b + 1) * BLOCK)
        turned.append(jnp.concatenate([dq_ref[:, cols] * 0.125, dk_ref[cols, :].T, dv_ref[cols, :].T], axis=0))
    turn_out(turned, turn, core, slot_ref, mine_ref, theirs_ref)


def prepare_kernel(
    q_in, k_in, v_in, u_in, cot_in, w_in, send_out, ut_out, dg_out,
    q_ref, k_ref, v_ref, u_ref, cot_ref, w_ref, send_ref, ut_ref, dg_ref, in_sems, w_sems, out_sems,
):
    pairs = (q_in, q_ref), (k_in, k_ref), (v_in, v_ref), (cot_in, cot_ref), (u_in, u_ref)
    copies = [pltpu.make_async_copy(a, b, in_sems.at[i]) for i, (a, b) in enumerate(pairs)]
    parts = [pl.ds(at, 256) for at in range(0, WIDTH, 256)]
    heads = [pl.ds(at, 4) for at in range(0, HEADS, 4)]
    w_copies = [pltpu.make_async_copy(w_in.at[part], w_ref.at[part], w_sems.at[i]) for i, part in enumerate(parts)]
    outs = [
        [
            pltpu.make_async_copy(send_ref.at[heads[i]], send_out.at[heads[i]], out_sems.at[0, i]),
            pltpu.make_async_copy(ut_ref.at[parts[i]], ut_out.at[parts[i]], out_sems.at[1, i]),
            pltpu.make_async_copy(dg_ref.at[parts[i]], dg_out.at[parts[i]], out_sems.at[2, i]),
        ]
        for i in range(4)
    ]
    for copy in copies + w_copies:
        copy.start()
    for i, ref in enumerate((q_ref, k_ref, v_ref)):
        copies[i].wait()
        for at in range(0, WIDTH, 256):
            rows = ref[:, at : at + 256].T
            for h in range(4):
                send_ref[at // 64 + h, i * 64 : (i + 1) * 64, :] = rows[h * 64 : (h + 1) * 64]
    copies[3].wait()
    copies[4].wait()
    for i in range(4):
        cols = slice(i * 256, (i + 1) * 256)
        u_t = u_ref[:, cols].T
        w_copies[i].wait()
        d_gated = dot_nt(w_ref[cols, :], cot_ref[...])
        dg_ref[cols, :] = d_gated
        ut_ref[cols, :] = u_t
        g_t = (d_gated * u_t.astype(F32)).astype(BF16)
        for h in range(4):
            send_ref[4 * i + h, 192:256, :] = g_t[h * 64 : (h + 1) * 64]
        for copy in outs[i]:
            copy.start()
    for out in outs:
        for copy in out:
            copy.wait()


def other_half_kernel(place_ref, got_ref, out_ref):
    core, begin = place_of(place_ref)[:2]
    for j in range(8):
        out_ref[j] = jnp.where(low_is_mine(j, core, begin), got_ref[8 + j], got_ref[j])


def to_owners_kernel(place_ref, mine_ref, theirs_ref, out_ref):
    core, begin = place_of(place_ref)[:2]
    for j in range(8):
        low_mine = low_is_mine(j, core, begin)
        mine, theirs = mine_ref[j], theirs_ref[j]
        out_ref[j] = jnp.where(low_mine, mine, theirs)
        out_ref[8 + j] = jnp.where(low_mine, theirs, mine)


def attn_to_owners_kernel(place_ref, mine_ref, theirs_ref, stat_ref, out_ref):
    to_owners_kernel(place_ref, mine_ref, theirs_ref, out_ref.at[:, 0:64, :])
    for j in range(HEADS):
        out_ref[j, 64:, :] = stat_ref[...]


def normalised(got_ref):
    attn = got_ref[:, 0:64, :].astype(F32).reshape(WIDTH, BLOCK)
    centre = attn - jnp.mean(attn, axis=0, keepdims=True)
    return centre * lax.rsqrt(jnp.mean(centre * centre, axis=0, keepdims=True) + 1e-05)


def gated_kernel(place_ref, got_ref, ut_ref, mine_ref, theirs_ref, zero_ref, one_ref):
    core = place_ref[4]
    gated = normalised(got_ref) * ut_ref[...].astype(F32)
    for z in (0, 1, 4, 5):
        for chip in range(HEADS):
            at = z * BLOCK + chip * 8
            one, two = gated[at : at + 8], gated[at + 2 * BLOCK : at + 2 * BLOCK + 8]
            row = (z % 2) * 256 + chip * 16 + (z // 2) * 4
            rows = slice(row, row + 8)
            zero_ref[rows, :] = jnp.concatenate([one[0:4], two[0:4]], axis=0)
            one_ref[rows, :] = jnp.concatenate([one[4:8], two[4:8]], axis=0)
    zero, one = zero_ref[...].astype(BF16), one_ref[...].astype(BF16)
    mine_ref[...] = jnp.where(core == 0, zero, one)
    theirs_ref[...] = jnp.where(core == 0, one, zero)


def d_gate_kernel(got_ref, dg_ref, after_ref, out_ref):
    d_gate = (dg_ref[...] * normalised(got_ref)).astype(BF16)
    for i in range(WIDTH // BLOCK):
        out_ref[:, i * BLOCK : (i + 1) * BLOCK] = d_gate[i * BLOCK : (i + 1) * BLOCK].T


def product_kernel(a_ref, b_ref, c_ref, d_ref, out_ref):
    for at in range(0, 512, 128):
        rows = slice(at, at + 128)
        out_ref[rows, :] = (dot(a_ref[rows, :], c_ref[...]) + dot(b_ref[rows, :], d_ref[...])).astype(BF16)


def finish_kernel(got_ref, dq_ref, dk_ref, dv_ref):
    for i, out_ref in enumerate((dq_ref, dk_ref, dv_ref)):
        for h in range(0, HEADS, 4):
            heads = got_ref[h : h + 4, i * 64 : (i + 1) * 64, :].reshape(256, BLOCK)
            out_ref[:, h * 64 : (h + 4) * 64] = heads.T


SMEM = pl.BlockSpec(memory_space=pltpu.SMEM)
VMEM = pl.BlockSpec(memory_space=pltpu.VMEM)
ANY = pl.BlockSpec(memory_space=pl.ANY)
DMA = pltpu.SemaphoreType.DMA


def call(kernel, name, out_shape, in_specs, args, scratch=(), out=VMEM, mib=8, flops=1 << 26, transcendentals=0):
    return pl.pallas_call(
        kernel,
        out_shape=out_shape,
        in_specs=in_specs,
        out_specs=jax.tree.map(lambda _: out, out_shape),
        scratch_shapes=list(scratch),
        compiler_params=pltpu.CompilerParams(vmem_limit_bytes=None if mib is None else mib * 1024 * 1024),
        cost_estimate=pl.CostEstimate(flops=flops, bytes_accessed=1 << 21, transcendentals=transcendentals),
        name=name,
    )(*args)


def shape(dims, dtype=BF16):
    return jax.ShapeDtypeStruct(dims, dtype)


def prepare(*args):
    shapes = shape((HEADS, 256, BLOCK)), shape((WIDTH, BLOCK)), shape((WIDTH, BLOCK), F32)
    return call(
        prepare_kernel,
        "prepare",
        shapes,
        [ANY] * 6,
        args,
        [pltpu.VMEM((BLOCK, WIDTH), BF16)] * 5
        + [pltpu.VMEM((WIDTH, WIDTH), BF16)]
        + [pltpu.VMEM(s.shape, s.dtype) for s in shapes]
        + [DMA((5,)), DMA((4,)), DMA((3, 4))],
        out=ANY,
        mib=None,
    )


def attend_forward(place, got, other):
    return call(
        forward_kernel,
        "attend_forward",
        (
            shape((320, HALF)),
            shape((8, HEAD_DIM, BLOCK)),
            shape((8, HEAD_DIM, BLOCK)),
            shape((STATS * N_BLOCKS, BLOCK)),
        ),
        [SMEM, VMEM, VMEM],
        (place, got, other),
        [
            pltpu.VMEM((HALF, HEAD_DIM), BF16),
            pltpu.VMEM((N_BLOCKS, 256, BLOCK), F32),
            pltpu.VMEM((STATS * N_BLOCKS, BLOCK), F32),
        ],
        mib=20,
        flops=1 << 30,
        transcendentals=1 << 22,
    )


def derive(place, x):
    tiles, rows = (ROWS_AT + HALF // SUB, SUB, SUB), (HALF, HEAD_DIM)
    return call(
        derive_kernel,
        "derive",
        shape(tiles),
        [SMEM, VMEM],
        (place, x),
        [pltpu.VMEM(tiles, BF16)]
        + [pltpu.VMEM(rows, BF16), DMA((2, len(GROUPS) + 1))],
        out=ANY,
        mib=TILES_MIB,
        flops=1 << 31,
        transcendentals=1 << 22,
    )


def attend_backward(place, x, got, derived):
    tiles, rows = (ROWS_AT + HALF // SUB, SUB, SUB), (HALF, HEAD_DIM)
    return call(
        backward_kernel,
        "attend_backward",
        (shape((8, 192, BLOCK)), shape((8, 192, BLOCK))),
        [SMEM, VMEM, VMEM, ANY],
        (place, x, got, derived),
        [pltpu.VMEM(tiles, BF16), pltpu.VMEM(rows, BF16)]
        + [
            pltpu.VMEM((HEAD_DIM, HALF), BF16),
            pltpu.VMEM((HEAD_DIM, HALF), F32),
            pltpu.VMEM(rows, F32),
            pltpu.VMEM(rows, F32),
            pltpu.VMEM((N_BLOCKS, 192, BLOCK), F32),
        ]
        + [DMA((2, len(GROUPS) + 1))],
        mib=TILES_MIB,
        flops=1 << 33,
    )


def on_device(query, key, value, gate_u, out_weight, cotangent, hist_lengths):
    core = lax.axis_index("core")
    place = jnp.concatenate([hist_lengths[0], core[None]]).astype(jnp.int32)

    def swap(x):
        return lax.ppermute(x, "core", SWAP)

    def chips(x):
        return lax.all_to_all(x, CHIP, 0, 0, tiled=True)

    send, u_t, d_gated_t = prepare(query, key, value, gate_u, cotangent, out_weight)
    got = chips(send)
    theirs = call(other_half_kernel, "other_half", shape((8, 256, BLOCK)), [SMEM, VMEM], (place, got))
    x, mine, theirs, stat = attend_forward(place, got, swap(theirs))

    rows = HEAD_DIM + STATS * N_BLOCKS
    send = call(
        attn_to_owners_kernel,
        "attn_to_owners",
        shape((HEADS, rows, BLOCK)),
        [SMEM] + [VMEM] * 3,
        (place, mine, swap(theirs), stat),
    )
    got_attn = chips(send)
    got_attn, derived = lax.optimization_barrier((got_attn, derive(place, x)))

    mine, theirs = call(
        gated_kernel,
        "gated",
        (shape((512, BLOCK)), shape((512, BLOCK))),
        [SMEM] + [VMEM] * 2,
        (place, got_attn, u_t),
        [pltpu.VMEM((512, BLOCK), F32)] * 2,
    )
    part = call(
        product_kernel,
        "product",
        shape((512, WIDTH)),
        [VMEM] * 4,
        (mine, swap(theirs), cotangent, swap(cotangent)),
    )
    parts = lax.all_to_all(part.reshape(32, 16, WIDTH), ("zl",) + CHIP, 0, 0, tiled=True)

    mine, theirs = attend_backward(place, x, got_attn, derived)
    send = call(
        to_owners_kernel,
        "grads_to_owners",
        shape((HEADS, 192, BLOCK)),
        [SMEM] + [VMEM] * 2,
        (place, mine, swap(theirs)),
    )
    got = chips(send)
    d_gate = call(
        d_gate_kernel,
        "d_gate",
        shape((BLOCK, WIDTH)),
        [VMEM, VMEM, ANY],
        (got_attn, d_gated_t, send),
        flops=1 << 20,
    )

    parts, d_gate = lax.optimization_barrier((parts, d_gate))
    part = jnp.sum(parts.astype(F32), axis=0).reshape(4, 4, WIDTH)
    z = lax.axis_index("zh")
    for step in (2, 1):
        high = (z // step) % 2
        halves = part.reshape(2, step, 4, WIDTH)
        away = lax.dynamic_index_in_dim(halves, 1 - high, 0, keepdims=False)
        kept = lax.dynamic_index_in_dim(halves, high, 0, keepdims=False)
        part = kept + lax.ppermute(away, "zh", [(i, i ^ step) for i in range(4)])
    d_weight = part.reshape(4, WIDTH) * (1.0 / math.sqrt(32768))

    d_query, d_key, d_value = call(finish_kernel, "finish", (shape((BLOCK, WIDTH)),) * 3, [VMEM], (got,))
    return d_query, d_key, d_value, d_gate, d_weight


def solution(mesh):
    axes = ("zh", "zl", "x", "y", "core")
    inner = Mesh(mesh.devices.reshape(4, 2, 4, 4, 2), axes)
    rows = P(axes, None)
    return jax.shard_map(
        on_device,
        mesh=inner,
        in_specs=(rows, rows, rows, rows, P(), rows, P(("zh", "zl"), None)),
        out_specs=(rows, rows, rows, rows, rows),
        check_vma=False,
    )
```

```python
import math

import jax
import jax.numpy as jnp
from jax import lax
from jax.experimental import pallas as pl
from jax.experimental.pallas import tpu as pltpu
from jax.sharding import Mesh, PartitionSpec as P

HEADS = 16
HEAD_DIM = 64
WIDTH = HEADS * HEAD_DIM
N_BLOCKS = 16
BLOCK = 128
HALF = N_BLOCKS * BLOCK
SUB = 256
F_TILE = 2048
B_TILE = 1024
STATS = 5
TILES_MIB = 45
CHIP = ("x", "y")
SWAP = ((0, 1), (1, 0))
BF16 = jnp.bfloat16
F32 = jnp.float32


def dot(a, b):
    return lax.dot_general(a, b, (((1,), (0,)), ((), ())), preferred_element_type=F32)


def dot_nt(a, b):
    return lax.dot_general(a, b, (((1,), (1,)), ((), ())), preferred_element_type=F32)


def sigmoid(s):
    return pltpu.reciprocal(1.0 + jnp.exp(-s), approx=True)


def lanes():
    return lax.broadcasted_iota(jnp.int32, (1, BLOCK), 1)


def place_of(place_ref):
    first, second, third = (place_ref[i] for i in range(3))
    core = place_ref[4]
    is_first, is_second = first == HALF, second == HALF
    begin = jnp.where(is_first, 0, jnp.where(is_second, first, first + second + jnp.where(third == HALF, 0, third)))
    end1 = jnp.where(is_first, second, first)
    end2 = end1 + jnp.where(is_first | is_second, third, second)
    turn = jnp.where(core == 0, begin & (HALF - 1), 0)
    return core, begin, turn, jnp.where(core == 0, HALF, end1), jnp.where(core == 0, HALF, end2)


def low_is_mine(j, core, begin):
    return ((2 * j + core) * BLOCK + lanes() >= begin) == (core == 0)


def live_of(q_at, k_at, end1, end2, diagonal):
    q_place = q_at + lax.broadcasted_iota(jnp.int32, (1, SUB), 1)
    k_place = k_at + lax.broadcasted_iota(jnp.int32, (SUB, 1), 0)
    start = jnp.where(q_place < end1, 0, jnp.where(q_place < end2, end1, end2))
    live = k_place >= start
    return live & (k_place <= q_place) if diagonal else live


def below(n_tiles, tile):
    n_sub = tile // SUB
    for i in range(n_tiles):
        for j in range(i + 1):
            subs = [(q, k) for q in range(n_sub) for k in range(n_sub) if j < i or k <= q]
            yield i * tile, j * tile, subs


def forward_kernel(
    place_ref, got_ref, other_ref, x_ref, mine_ref, theirs_ref, stat_ref, k_ref, slot_ref, stats_ref
):
    core, begin, turn, end1, end2 = place_of(place_ref)
    whole, rest = turn // BLOCK, turn % BLOCK
    lane = lanes()
    for b in range(N_BLOCKS):
        j = b // 2
        mine = jnp.where(low_is_mine(j, core, begin), got_ref[j], got_ref[8 + j])
        here = jnp.where(core == b % 2, mine, other_ref[j])
        slot_ref[b] = pltpu.roll(here.astype(F32), lax.rem(BLOCK - rest, BLOCK), 1)
    for b in range(N_BLOCKS):
        first, second = slot_ref[lax.rem(b + whole, N_BLOCKS)], slot_ref[lax.rem(b + whole + 1, N_BLOCKS)]
        here = jnp.where(lane < BLOCK - rest, first, second)
        x_ref[0:64, b * BLOCK : (b + 1) * BLOCK] = (here[0:64] * 0.125).astype(BF16)
        x_ref[64:256, b * BLOCK : (b + 1) * BLOCK] = here[64:256].astype(BF16)
        k_ref[b * BLOCK : (b + 1) * BLOCK, :] = here[64:128].astype(BF16).T

    for q_at, k_at, subs in below(HALF // F_TILE, F_TILE):
        weights = {}
        for q, k in subs:
            q_sub, k_sub = q_at + q * SUB, k_at + k * SUB
            s = dot(k_ref[k_sub : k_sub + SUB, :], x_ref[0:64, q_sub : q_sub + SUB])
            live = live_of(q_sub, k_sub, end1, end2, q_sub == k_sub)
            weights[q, k] = jnp.where(live, s * sigmoid(s), 0.0).astype(BF16)
        for q in range(F_TILE // SUB):
            q_sub = q_at + q * SUB
            acc = jnp.zeros((HEAD_DIM, SUB), F32)
            for k in range(F_TILE // SUB):
                if (q, k) in weights:
                    k_sub = k_at + k * SUB
                    acc += dot(x_ref[128:192, k_sub : k_sub + SUB], weights[q, k])
            x_ref[256:320, q_sub : q_sub + SUB] = acc.astype(BF16)

    turned = []
    for b in range(N_BLOCKS):
        cols = slice(b * BLOCK, (b + 1) * BLOCK)
        attn = x_ref[256:320, cols].astype(F32)
        g = x_ref[192:256, cols].astype(F32)
        mean = jnp.mean(attn, axis=0, keepdims=True)
        centre = attn - mean
        both = jnp.sum(centre * g, axis=0, keepdims=True)
        mean_hi = mean.astype(BF16).astype(F32)
        square = jnp.sum(centre * centre, axis=0, keepdims=True)
        total = jnp.sum(g, axis=0, keepdims=True)
        for i, row in enumerate((mean_hi, mean - mean_hi, both, square, total)):
            stats_ref[i * N_BLOCKS + b : i * N_BLOCKS + b + 1, :] = row
        turned.append(attn)
    stat_ref[...] = stats_ref[...].astype(BF16)
    turn_out(turned, turn, core, slot_ref, mine_ref, theirs_ref)


def turn_out(blocks, turn, core, slot_ref, mine_ref, theirs_ref):
    whole, rest = turn // BLOCK, turn % BLOCK
    rows = blocks[0].shape[0]
    for b, block in enumerate(blocks):
        slot_ref[b, 0:rows, :] = pltpu.roll(block, rest, 1)
    from_this = lanes() >= rest
    for j in range(8):
        pair = []
        for b in (2 * j, 2 * j + 1):
            this = slot_ref[lax.rem(b - whole + N_BLOCKS, N_BLOCKS), 0:rows, :]
            last = slot_ref[lax.rem(b - whole + N_BLOCKS - 1, N_BLOCKS), 0:rows, :]
            pair.append(jnp.where(from_this, this, last).astype(BF16))
        mine_ref[j] = jnp.where(core == 0, pair[0], pair[1])
        theirs_ref[j] = jnp.where(core == 0, pair[1], pair[0])


GROUPS = [[(q_at // SUB + q, k_at // SUB + k) for q, k in subs] for q_at, k_at, subs in below(HALF // B_TILE, B_TILE)]
PAIRS = [pair for group in GROUPS for pair in group]
AT = {pair: i for i, pair in enumerate(PAIRS)}
ROWS_AT = 2 * len(PAIRS)
Q_LANES, V_LANES = slice(0, 64), slice(128, 192)


def group_copies(from_ref, to_ref, sems):
    silu, slope, at = [], [], 0
    for i, group in enumerate(GROUPS):
        for j, copies in enumerate((silu, slope)):
            part = pl.ds(j * len(PAIRS) + at, len(group))
            copies.append(pltpu.make_async_copy(from_ref.at[part], to_ref.at[part], sems.at[j, i]))
        at += len(group)
    part = pl.ds(ROWS_AT, HALF // SUB)
    return silu, slope, pltpu.make_async_copy(from_ref.at[part], to_ref.at[part], sems.at[0, len(GROUPS)])


def derive_kernel(
    place_ref, x_ref, tile_out, tile_ref, kn_ref, tile_sems
):
    end1, end2 = place_of(place_ref)[3:]
    for b in range(N_BLOCKS):
        cols = slice(b * BLOCK, (b + 1) * BLOCK)
        rows = slice((b % 2) * BLOCK, (b % 2 + 1) * BLOCK)
        tile_ref[ROWS_AT + b // 2, rows, Q_LANES] = x_ref[0:64, cols].T
        tile_ref[ROWS_AT + b // 2, rows, V_LANES] = x_ref[128:192, cols].T
        kn_ref[cols, :] = x_ref[64:128, cols].T
    silu_copies, slope_copies, rows_copy = group_copies(tile_ref, tile_out, tile_sems)
    rows_copy.start()
    for i, group in enumerate(GROUPS):
        for q, k in group:
            q_cols, k_cols = slice(q * SUB, (q + 1) * SUB), slice(k * SUB, (k + 1) * SUB)
            s = dot(kn_ref[k_cols, :], x_ref[0:64, q_cols])
            sigma = jnp.where(live_of(q * SUB, k * SUB, end1, end2, q == k), sigmoid(s), 0.0)
            silu = s * sigma
            tile_ref[AT[q, k]] = silu.astype(BF16)
            tile_ref[len(PAIRS) + AT[q, k]] = (sigma + silu * (1.0 - sigma)).astype(BF16)
        silu_copies[i].start()
        slope_copies[i].start()
    for copy in [rows_copy] + silu_copies + slope_copies:
        copy.wait()


def backward_kernel(
    place_ref, x_ref, got_ref, tile_in, mine_ref, theirs_ref,
    tile_ref, dn_ref, dt_ref, dq_ref, dk_ref, dv_ref, slot_ref,
    tile_sems,
):
    silu_copies, slope_copies, rows_copy = group_copies(tile_in, tile_ref, tile_sems)
    rows_copy.start()
    for i in range(len(GROUPS)):
        slope_copies[i].start()
        silu_copies[i].start()
    core, _, turn, end1, end2 = place_of(place_ref)
    stat = got_ref[:, 64 : 64 + STATS * N_BLOCKS, :].astype(F32).reshape(HEADS, STATS, N_BLOCKS, BLOCK)
    mean_h = stat[:, 0] + stat[:, 1]
    mean = jnp.mean(mean_h, axis=0)
    off = mean_h - mean[None]
    square = jnp.sum(stat[:, 3] + HEAD_DIM * off * off, axis=0)
    rstd = lax.rsqrt(square * (1.0 / WIDTH) + 1e-05)
    g_sum = stat[:, 4]
    g_mean = jnp.sum(g_sum, axis=0) * (1.0 / WIDTH)
    both = jnp.sum(stat[:, 2] + off * g_sum, axis=0) * rstd * (1.0 / WIDTH)
    for b in range(N_BLOCKS):
        cols = slice(b * BLOCK, (b + 1) * BLOCK)
        r = rstd[b : b + 1]
        normed = (x_ref[256:320, cols].astype(F32) - mean[b : b + 1]) * r
        d = (r * (x_ref[192:256, cols].astype(F32) - g_mean[b : b + 1] - normed * both[b : b + 1])).astype(BF16)
        dt_ref[:, cols] = d
        dn_ref[cols, :] = d.T

    rows_copy.wait()
    for i, (q_at, k_at, subs) in enumerate(below(HALF // B_TILE, B_TILE)):
        slope_copies[i].wait()
        n = B_TILE // SUB
        q_first, k_first = q_at // SUB, k_at // SUB
        made = {}
        for q, k in subs:
            q_cols = slice(q_at + q * SUB, q_at + (q + 1) * SUB)
            k_cols = slice(k_at + k * SUB, k_at + (k + 1) * SUB)
            d_p = dot(tile_ref[ROWS_AT + k_first + k, :, V_LANES], dt_ref[:, q_cols])
            made[q, k] = (d_p * tile_ref[len(PAIRS) + AT[q_first + q, k_first + k]].astype(F32)).astype(BF16)
        silu_copies[i].wait()
        for k in range(n):
            k_cols = slice(k_at + k * SUB, k_at + (k + 1) * SUB)
            d_v, d_k = [], []
            for q in range(n):
                if (q, k) in made:
                    q_cols = slice(q_at + q * SUB, q_at + (q + 1) * SUB)
                    d_v.append(dot(tile_ref[AT[q_first + q, k_first + k]], dn_ref[q_cols, :]))
                    d_k.append(dot(made[q, k], tile_ref[ROWS_AT + q_first + q, :, Q_LANES]))
            if q_at == k_at:
                dv_ref[k_cols, :], dk_ref[k_cols, :] = sum(d_v), sum(d_k)
            else:
                dv_ref[k_cols, :] += sum(d_v)
                dk_ref[k_cols, :] += sum(d_k)
        for q in range(n):
            q_cols = slice(q_at + q * SUB, q_at + (q + 1) * SUB)
            d_q = []
            for k in range(n):
                if (q, k) in made:
                    d_q.append(dot(x_ref[64:128, k_at + k * SUB : k_at + (k + 1) * SUB], made[q, k]))
            if k_at == 0:
                dq_ref[:, q_cols] = sum(d_q)
            else:
                dq_ref[:, q_cols] += sum(d_q)

    turned = []
    for b in range(N_BLOCKS):
        cols = slice(b * BLOCK, (b + 1) * BLOCK)
        turned.append(jnp.concatenate([dq_ref[:, cols] * 0.125, dk_ref[cols, :].T, dv_ref[cols, :].T], axis=0))
    turn_out(turned, turn, core, slot_ref, mine_ref, theirs_ref)


def prepare_kernel(
    q_in, k_in, v_in, u_in, cot_in, w_in, send_out, ut_out, dg_out,
    q_ref, k_ref, v_ref, u_ref, cot_ref, w_ref, send_ref, ut_ref, dg_ref, in_sems, w_sems, out_sems,
):
    pairs = (q_in, q_ref), (k_in, k_ref), (v_in, v_ref), (cot_in, cot_ref), (u_in, u_ref)
    copies = [pltpu.make_async_copy(a, b, in_sems.at[i]) for i, (a, b) in enumerate(pairs)]
    parts = [pl.ds(at, 256) for at in range(0, WIDTH, 256)]
    heads = [pl.ds(at, 4) for at in range(0, HEADS, 4)]
    w_copies = [pltpu.make_async_copy(w_in.at[part], w_ref.at[part], w_sems.at[i]) for i, part in enumerate(parts)]
    outs = [
        [
            pltpu.make_async_copy(send_ref.at[heads[i]], send_out.at[heads[i]], out_sems.at[0, i]),
            pltpu.make_async_copy(ut_ref.at[parts[i]], ut_out.at[parts[i]], out_sems.at[1, i]),
            pltpu.make_async_copy(dg_ref.at[parts[i]], dg_out.at[parts[i]], out_sems.at[2, i]),
        ]
        for i in range(4)
    ]
    for copy in copies + w_copies:
        copy.start()
    for i, ref in enumerate((q_ref, k_ref, v_ref)):
        copies[i].wait()
        for at in range(0, WIDTH, 256):
            rows = ref[:, at : at + 256].T
            for h in range(4):
                send_ref[at // 64 + h, i * 64 : (i + 1) * 64, :] = rows[h * 64 : (h + 1) * 64]
    copies[3].wait()
    copies[4].wait()
    for i in range(4):
        cols = slice(i * 256, (i + 1) * 256)
        u_t = u_ref[:, cols].T
        w_copies[i].wait()
        d_gated = dot_nt(w_ref[cols, :], cot_ref[...])
        dg_ref[cols, :] = d_gated
        ut_ref[cols, :] = u_t
        g_t = (d_gated * u_t.astype(F32)).astype(BF16)
        for h in range(4):
            send_ref[4 * i + h, 192:256, :] = g_t[h * 64 : (h + 1) * 64]
        for copy in outs[i]:
            copy.start()
    for out in outs:
        for copy in out:
            copy.wait()


def other_half_kernel(place_ref, got_ref, out_ref):
    core, begin = place_of(place_ref)[:2]
    for j in range(8):
        out_ref[j] = jnp.where(low_is_mine(j, core, begin), got_ref[8 + j], got_ref[j])


def to_owners_kernel(place_ref, mine_ref, theirs_ref, out_ref):
    core, begin = place_of(place_ref)[:2]
    for j in range(8):
        low_mine = low_is_mine(j, core, begin)
        mine, theirs = mine_ref[j], theirs_ref[j]
        out_ref[j] = jnp.where(low_mine, mine, theirs)
        out_ref[8 + j] = jnp.where(low_mine, theirs, mine)


def attn_to_owners_kernel(place_ref, mine_ref, theirs_ref, stat_ref, out, out_ref, sems):
    core, begin = place_of(place_ref)[:2]
    copies = [pltpu.make_async_copy(out_ref.at[j], out.at[j], sems.at[j]) for j in range(HEADS)]
    for j in range(8):
        low_mine = low_is_mine(j, core, begin)
        mine, theirs = mine_ref[j], theirs_ref[j]
        out_ref[j, 0:64, :] = jnp.where(low_mine, mine, theirs)
        out_ref[8 + j, 0:64, :] = jnp.where(low_mine, theirs, mine)
        for i in (j, 8 + j):
            out_ref[i, 64:, :] = stat_ref[...]
            copies[i].start()
    for copy in copies:
        copy.wait()


def normalised(got_ref):
    attn = got_ref[:, 0:64, :].astype(F32).reshape(WIDTH, BLOCK)
    centre = attn - jnp.mean(attn, axis=0, keepdims=True)
    return centre * lax.rsqrt(jnp.mean(centre * centre, axis=0, keepdims=True) + 1e-05)


def gated_kernel(place_ref, got_ref, ut_ref, keep_ref, core_ref, z_ref, both_ref, half_ref):
    core, zl = place_ref[4], place_ref[5]
    gated = normalised(got_ref) * ut_ref[...].astype(F32)
    for z in (0, 1, 4, 5):
        for chip in range(HEADS):
            at = z * BLOCK + chip * 8
            one, two = gated[at : at + 8], gated[at + 2 * BLOCK : at + 2 * BLOCK + 8]
            row = (z % 2) * 256 + chip * 16 + (z // 2) * 4
            rows = slice(row, row + 8)
            half_ref[0, rows, :] = jnp.concatenate([one[0:4], two[0:4]], axis=0)
            half_ref[1, rows, :] = jnp.concatenate([one[4:8], two[4:8]], axis=0)
    for c, z, out_ref in ((core, zl, keep_ref), (1 - core, zl, core_ref), (core, 1 - zl, z_ref), (1 - core, 1 - zl, both_ref)):
        out_ref[...] = half_ref[c, pl.ds(pl.multiple_of(z * 256, 256), 256), :].astype(BF16)


def d_gate_kernel(got_ref, dg_ref, after_ref, out_ref):
    d_gate = (dg_ref[...] * normalised(got_ref)).astype(BF16)
    for i in range(WIDTH // BLOCK):
        out_ref[:, i * BLOCK : (i + 1) * BLOCK] = d_gate[i * BLOCK : (i + 1) * BLOCK].T


def product_kernel(*refs):
    gated, cotangent, (out, out_ref, sems) = refs[0:4], refs[4:8], refs[8:]
    copies = []
    for i in range(2):
        rows = slice(i * 128, (i + 1) * 128)
        out_ref[rows, :] = sum(dot(a[rows, :], b[...]) for a, b in zip(gated, cotangent)).astype(BF16)
        part = pl.ds(i * 128, 128)
        copies.append(pltpu.make_async_copy(out_ref.at[part], out.at[part], sems.at[i]))
        copies[i].start()
    for copy in copies:
        copy.wait()


def finish_kernel(got_ref, dq_ref, dk_ref, dv_ref):
    for i, out_ref in enumerate((dq_ref, dk_ref, dv_ref)):
        for h in range(0, HEADS, 4):
            heads = got_ref[h : h + 4, i * 64 : (i + 1) * 64, :].reshape(256, BLOCK)
            out_ref[:, h * 64 : (h + 4) * 64] = heads.T


SMEM = pl.BlockSpec(memory_space=pltpu.SMEM)
VMEM = pl.BlockSpec(memory_space=pltpu.VMEM)
ANY = pl.BlockSpec(memory_space=pl.ANY)
DMA = pltpu.SemaphoreType.DMA


def call(kernel, name, out_shape, in_specs, args, scratch=(), out=VMEM, mib=8, flops=1 << 26, transcendentals=0):
    return pl.pallas_call(
        kernel,
        out_shape=out_shape,
        in_specs=in_specs,
        out_specs=jax.tree.map(lambda _: out, out_shape),
        scratch_shapes=list(scratch),
        compiler_params=pltpu.CompilerParams(vmem_limit_bytes=None if mib is None else mib * 1024 * 1024),
        cost_estimate=pl.CostEstimate(flops=flops, bytes_accessed=1 << 21, transcendentals=transcendentals),
        name=name,
    )(*args)


def shape(dims, dtype=BF16):
    return jax.ShapeDtypeStruct(dims, dtype)


def prepare(*args):
    shapes = shape((HEADS, 256, BLOCK)), shape((WIDTH, BLOCK)), shape((WIDTH, BLOCK), F32)
    return call(
        prepare_kernel,
        "prepare",
        shapes,
        [ANY] * 6,
        args,
        [pltpu.VMEM((BLOCK, WIDTH), BF16)] * 5
        + [pltpu.VMEM((WIDTH, WIDTH), BF16)]
        + [pltpu.VMEM(s.shape, s.dtype) for s in shapes]
        + [DMA((5,)), DMA((4,)), DMA((3, 4))],
        out=ANY,
        mib=None,
    )


def attend_forward(place, got, other):
    return call(
        forward_kernel,
        "attend_forward",
        (
            shape((320, HALF)),
            shape((8, HEAD_DIM, BLOCK)),
            shape((8, HEAD_DIM, BLOCK)),
            shape((STATS * N_BLOCKS, BLOCK)),
        ),
        [SMEM, VMEM, VMEM],
        (place, got, other),
        [
            pltpu.VMEM((HALF, HEAD_DIM), BF16),
            pltpu.VMEM((N_BLOCKS, 256, BLOCK), F32),
            pltpu.VMEM((STATS * N_BLOCKS, BLOCK), F32),
        ],
        mib=20,
        flops=1 << 30,
        transcendentals=1 << 22,
    )


def derive(place, x):
    tiles, rows = (ROWS_AT + HALF // SUB, SUB, SUB), (HALF, HEAD_DIM)
    return call(
        derive_kernel,
        "derive",
        shape(tiles),
        [SMEM, VMEM],
        (place, x),
        [pltpu.VMEM(tiles, BF16)]
        + [pltpu.VMEM(rows, BF16), DMA((2, len(GROUPS) + 1))],
        out=ANY,
        mib=TILES_MIB,
        flops=1 << 31,
        transcendentals=1 << 22,
    )


def attend_backward(place, x, got, derived):
    tiles, rows = (ROWS_AT + HALF // SUB, SUB, SUB), (HALF, HEAD_DIM)
    return call(
        backward_kernel,
        "attend_backward",
        (shape((8, 192, BLOCK)), shape((8, 192, BLOCK))),
        [SMEM, VMEM, VMEM, ANY],
        (place, x, got, derived),
        [pltpu.VMEM(tiles, BF16), pltpu.VMEM(rows, BF16)]
        + [
            pltpu.VMEM((HEAD_DIM, HALF), BF16),
            pltpu.VMEM((HEAD_DIM, HALF), F32),
            pltpu.VMEM(rows, F32),
            pltpu.VMEM(rows, F32),
            pltpu.VMEM((N_BLOCKS, 192, BLOCK), F32),
        ]
        + [DMA((2, len(GROUPS) + 1))],
        mib=TILES_MIB,
        flops=1 << 33,
    )


def on_device(query, key, value, gate_u, out_weight, cotangent, hist_lengths):
    core = lax.axis_index("core")
    place = jnp.concatenate([hist_lengths[0], core[None], lax.axis_index("zl")[None]]).astype(jnp.int32)

    def swap(x):
        return lax.ppermute(x, "core", SWAP)

    def chips(x):
        return lax.all_to_all(x, CHIP, 0, 0, tiled=True)

    send, u_t, d_gated_t = prepare(query, key, value, gate_u, cotangent, out_weight)
    got = chips(send)
    theirs = call(other_half_kernel, "other_half", shape((8, 256, BLOCK)), [SMEM, VMEM], (place, got))
    x, mine, theirs, stat = attend_forward(place, got, swap(theirs))

    rows = HEAD_DIM + STATS * N_BLOCKS
    send = call(
        attn_to_owners_kernel,
        "attn_to_owners",
        shape((HEADS, rows, BLOCK)),
        [SMEM] + [VMEM] * 3,
        (place, mine, swap(theirs), stat),
        [pltpu.VMEM((HEADS, rows, BLOCK), BF16), DMA((HEADS,))],
        out=ANY,
    )
    got_attn = chips(send)
    got_attn, derived = lax.optimization_barrier((got_attn, derive(place, x)))

    def four(parts):
        return [parts[0]] + [
            lax.ppermute(part, ("zl", "core"), [(i, i ^ step) for i in range(4)])
            for step, part in zip((1, 2, 3), parts[1:])
        ]

    gated = call(
        gated_kernel,
        "gated",
        (shape((256, BLOCK)),) * 4,
        [SMEM] + [VMEM] * 2,
        (place, got_attn, u_t),
        [pltpu.VMEM((2, 512, BLOCK), F32)],
    )
    part = call(
        product_kernel,
        "product",
        shape((256, WIDTH)),
        [VMEM] * 8,
        four(gated) + four([cotangent] * 4),
        [pltpu.VMEM((256, WIDTH), BF16), DMA((2,))],
        out=ANY,
    )
    parts = chips(part.reshape(HEADS, 16, WIDTH))

    mine, theirs = attend_backward(place, x, got_attn, derived)
    send = call(
        to_owners_kernel,
        "grads_to_owners",
        shape((HEADS, 192, BLOCK)),
        [SMEM] + [VMEM] * 2,
        (place, mine, swap(theirs)),
    )
    got = chips(send)
    d_gate = call(
        d_gate_kernel,
        "d_gate",
        shape((BLOCK, WIDTH)),
        [VMEM, VMEM, ANY],
        (got_attn, d_gated_t, send),
        flops=1 << 20,
    )

    parts, _ = lax.optimization_barrier((parts, send))
    part = jnp.sum(parts.astype(F32), axis=0).reshape(4, 4, WIDTH)
    z = lax.axis_index("zh")
    for step in (2, 1):
        high = (z // step) % 2
        halves = part.reshape(2, step, 4, WIDTH)
        away = lax.dynamic_index_in_dim(halves, 1 - high, 0, keepdims=False)
        kept = lax.dynamic_index_in_dim(halves, high, 0, keepdims=False)
        part = kept + lax.ppermute(away, "zh", [(i, i ^ step) for i in range(4)])
    d_weight = part.reshape(4, WIDTH) * (1.0 / math.sqrt(32768))

    d_query, d_key, d_value = call(finish_kernel, "finish", (shape((BLOCK, WIDTH)),) * 3, [VMEM], (got,))
    return d_query, d_key, d_value, d_gate, d_weight


def solution(mesh):
    axes = ("zh", "zl", "x", "y", "core")
    inner = Mesh(mesh.devices.reshape(4, 2, 4, 4, 2), axes)
    rows = P(axes, None)
    return jax.shard_map(
        on_device,
        mesh=inner,
        in_specs=(rows, rows, rows, rows, P(), rows, P(("zh", "zl"), None)),
        out_specs=(rows, rows, rows, rows, rows),
        check_vma=False,
    )
```

```python
import math

import jax
import jax.numpy as jnp
from jax import lax
from jax.experimental import pallas as pl
from jax.experimental.pallas import tpu as pltpu
from jax.sharding import Mesh, PartitionSpec as P

HEADS = 16
HEAD_DIM = 64
WIDTH = HEADS * HEAD_DIM
N_BLOCKS = 16
BLOCK = 128
HALF = N_BLOCKS * BLOCK
SUB = 256
F_TILE = 2048
B_TILE = 1024
STATS = 5
TILES_MIB = 45
CHIP = ("x", "y")
SWAP = ((0, 1), (1, 0))
BF16 = jnp.bfloat16
F32 = jnp.float32


def dot(a, b):
    return lax.dot_general(a, b, (((1,), (0,)), ((), ())), preferred_element_type=F32)


def dot_nt(a, b):
    return lax.dot_general(a, b, (((1,), (1,)), ((), ())), preferred_element_type=F32)


def sigmoid(s):
    return pltpu.reciprocal(1.0 + jnp.exp(-s), approx=True)


def lanes():
    return lax.broadcasted_iota(jnp.int32, (1, BLOCK), 1)


def place_of(place_ref):
    first, second, third = (place_ref[i] for i in range(3))
    core = place_ref[4]
    is_first, is_second = first == HALF, second == HALF
    begin = jnp.where(is_first, 0, jnp.where(is_second, first, first + second + jnp.where(third == HALF, 0, third)))
    end1 = jnp.where(is_first, second, first)
    end2 = end1 + jnp.where(is_first | is_second, third, second)
    turn = jnp.where(core == 0, begin & (HALF - 1), 0)
    return core, begin, turn, jnp.where(core == 0, HALF, end1), jnp.where(core == 0, HALF, end2)


def low_is_mine(j, core, begin):
    return ((2 * j + core) * BLOCK + lanes() >= begin) == (core == 0)


def live_of(q_at, k_at, end1, end2, diagonal):
    q_place = q_at + lax.broadcasted_iota(jnp.int32, (1, SUB), 1)
    k_place = k_at + lax.broadcasted_iota(jnp.int32, (SUB, 1), 0)
    start = jnp.where(q_place < end1, 0, jnp.where(q_place < end2, end1, end2))
    live = k_place >= start
    return live & (k_place <= q_place) if diagonal else live


def below(n_tiles, tile):
    n_sub = tile // SUB
    for i in range(n_tiles):
        for j in range(i + 1):
            subs = [(q, k) for q in range(n_sub) for k in range(n_sub) if j < i or k <= q]
            yield i * tile, j * tile, subs


def forward_kernel(
    place_ref, got_ref, other_ref, x_ref, mine_ref, theirs_ref, stat_ref, k_ref, slot_ref, stats_ref
):
    core, begin, turn, end1, end2 = place_of(place_ref)
    whole, rest = turn // BLOCK, turn % BLOCK
    lane = lanes()
    for b in range(N_BLOCKS):
        j = b // 2
        mine = jnp.where(low_is_mine(j, core, begin), got_ref[j], got_ref[8 + j])
        here = jnp.where(core == b % 2, mine, other_ref[j])
        slot_ref[b] = pltpu.roll(here.astype(F32), lax.rem(BLOCK - rest, BLOCK), 1)
    for b in range(N_BLOCKS):
        first, second = slot_ref[lax.rem(b + whole, N_BLOCKS)], slot_ref[lax.rem(b + whole + 1, N_BLOCKS)]
        here = jnp.where(lane < BLOCK - rest, first, second)
        x_ref[0:64, b * BLOCK : (b + 1) * BLOCK] = (here[0:64] * 0.125).astype(BF16)
        x_ref[64:256, b * BLOCK : (b + 1) * BLOCK] = here[64:256].astype(BF16)
        k_ref[b * BLOCK : (b + 1) * BLOCK, :] = here[64:128].astype(BF16).T

    for q_at, k_at, subs in below(HALF // F_TILE, F_TILE):
        weights = {}
        for q, k in subs:
            q_sub, k_sub = q_at + q * SUB, k_at + k * SUB
            s = dot(k_ref[k_sub : k_sub + SUB, :], x_ref[0:64, q_sub : q_sub + SUB])
            live = live_of(q_sub, k_sub, end1, end2, q_sub == k_sub)
            weights[q, k] = jnp.where(live, s * sigmoid(s), 0.0).astype(BF16)
        for q in range(F_TILE // SUB):
            q_sub = q_at + q * SUB
            acc = jnp.zeros((HEAD_DIM, SUB), F32)
            for k in range(F_TILE // SUB):
                if (q, k) in weights:
                    k_sub = k_at + k * SUB
                    acc += dot(x_ref[128:192, k_sub : k_sub + SUB], weights[q, k])
            x_ref[256:320, q_sub : q_sub + SUB] = acc.astype(BF16)

    turned = []
    for b in range(N_BLOCKS):
        cols = slice(b * BLOCK, (b + 1) * BLOCK)
        attn = x_ref[256:320, cols].astype(F32)
        g = x_ref[192:256, cols].astype(F32)
        mean = jnp.mean(attn, axis=0, keepdims=True)
        centre = attn - mean
        both = jnp.sum(centre * g, axis=0, keepdims=True)
        mean_hi = mean.astype(BF16).astype(F32)
        square = jnp.sum(centre * centre, axis=0, keepdims=True)
        total = jnp.sum(g, axis=0, keepdims=True)
        for i, row in enumerate((mean_hi, mean - mean_hi, both, square, total)):
            stats_ref[i * N_BLOCKS + b : i * N_BLOCKS + b + 1, :] = row
        turned.append(attn)
    stat_ref[...] = stats_ref[...].astype(BF16)
    turn_out(turned, turn, core, slot_ref, mine_ref, theirs_ref)


def turn_out(blocks, turn, core, slot_ref, mine_ref, theirs_ref):
    whole, rest = turn // BLOCK, turn % BLOCK
    rows = blocks[0].shape[0]
    for b, block in enumerate(blocks):
        slot_ref[b, 0:rows, :] = pltpu.roll(block, rest, 1)
    from_this = lanes() >= rest
    for j in range(8):
        pair = []
        for b in (2 * j, 2 * j + 1):
            this = slot_ref[lax.rem(b - whole + N_BLOCKS, N_BLOCKS), 0:rows, :]
            last = slot_ref[lax.rem(b - whole + N_BLOCKS - 1, N_BLOCKS), 0:rows, :]
            pair.append(jnp.where(from_this, this, last).astype(BF16))
        mine_ref[j] = jnp.where(core == 0, pair[0], pair[1])
        theirs_ref[j] = jnp.where(core == 0, pair[1], pair[0])


GROUPS = [[(q_at // SUB + q, k_at // SUB + k) for q, k in subs] for q_at, k_at, subs in below(HALF // B_TILE, B_TILE)]
PAIRS = [pair for group in GROUPS for pair in group]
AT = {pair: i for i, pair in enumerate(PAIRS)}
ROWS_AT = 2 * len(PAIRS)
Q_LANES, V_LANES = slice(0, 64), slice(128, 192)


def group_copies(from_ref, to_ref, sems):
    silu, slope, at = [], [], 0
    for i, group in enumerate(GROUPS):
        for j, copies in enumerate((silu, slope)):
            part = pl.ds(j * len(PAIRS) + at, len(group))
            copies.append(pltpu.make_async_copy(from_ref.at[part], to_ref.at[part], sems.at[j, i]))
        at += len(group)
    part = pl.ds(ROWS_AT, HALF // SUB)
    return silu, slope, pltpu.make_async_copy(from_ref.at[part], to_ref.at[part], sems.at[0, len(GROUPS)])


def derive_kernel(
    place_ref, x_ref, tile_out, tile_ref, kn_ref, tile_sems
):
    end1, end2 = place_of(place_ref)[3:]
    for b in range(N_BLOCKS):
        cols = slice(b * BLOCK, (b + 1) * BLOCK)
        rows = slice((b % 2) * BLOCK, (b % 2 + 1) * BLOCK)
        tile_ref[ROWS_AT + b // 2, rows, Q_LANES] = x_ref[0:64, cols].T
        tile_ref[ROWS_AT + b // 2, rows, V_LANES] = x_ref[128:192, cols].T
        kn_ref[cols, :] = x_ref[64:128, cols].T
    silu_copies, slope_copies, rows_copy = group_copies(tile_ref, tile_out, tile_sems)
    rows_copy.start()
    for i, group in enumerate(GROUPS):
        for q, k in group:
            q_cols, k_cols = slice(q * SUB, (q + 1) * SUB), slice(k * SUB, (k + 1) * SUB)
            s = dot(kn_ref[k_cols, :], x_ref[0:64, q_cols])
            sigma = jnp.where(live_of(q * SUB, k * SUB, end1, end2, q == k), sigmoid(s), 0.0)
            silu = s * sigma
            tile_ref[AT[q, k]] = silu.astype(BF16)
            tile_ref[len(PAIRS) + AT[q, k]] = (sigma + silu * (1.0 - sigma)).astype(BF16)
        silu_copies[i].start()
        slope_copies[i].start()
    for copy in [rows_copy] + silu_copies + slope_copies:
        copy.wait()


def backward_kernel(
    place_ref, x_ref, got_ref, tile_in, mine_ref, theirs_ref,
    tile_ref, dn_ref, dt_ref, dq_ref, dk_ref, dv_ref, slot_ref,
    tile_sems,
):
    silu_copies, slope_copies, rows_copy = group_copies(tile_in, tile_ref, tile_sems)
    rows_copy.start()
    for i in range(len(GROUPS)):
        slope_copies[i].start()
        silu_copies[i].start()
    core, _, turn, end1, end2 = place_of(place_ref)
    stat = got_ref[:, 64 : 64 + STATS * N_BLOCKS, :].astype(F32).reshape(HEADS, STATS, N_BLOCKS, BLOCK)
    mean_h = stat[:, 0] + stat[:, 1]
    mean = jnp.mean(mean_h, axis=0)
    off = mean_h - mean[None]
    square = jnp.sum(stat[:, 3] + HEAD_DIM * off * off, axis=0)
    rstd = lax.rsqrt(square * (1.0 / WIDTH) + 1e-05)
    g_sum = stat[:, 4]
    g_mean = jnp.sum(g_sum, axis=0) * (1.0 / WIDTH)
    both = jnp.sum(stat[:, 2] + off * g_sum, axis=0) * rstd * (1.0 / WIDTH)
    for b in range(N_BLOCKS):
        cols = slice(b * BLOCK, (b + 1) * BLOCK)
        r = rstd[b : b + 1]
        normed = (x_ref[256:320, cols].astype(F32) - mean[b : b + 1]) * r
        d = (r * (x_ref[192:256, cols].astype(F32) - g_mean[b : b + 1] - normed * both[b : b + 1])).astype(BF16)
        dt_ref[:, cols] = d
        dn_ref[cols, :] = d.T

    rows_copy.wait()
    for i, (q_at, k_at, subs) in enumerate(below(HALF // B_TILE, B_TILE)):
        slope_copies[i].wait()
        n = B_TILE // SUB
        q_first, k_first = q_at // SUB, k_at // SUB
        made = {}
        for q, k in subs:
            q_cols = slice(q_at + q * SUB, q_at + (q + 1) * SUB)
            k_cols = slice(k_at + k * SUB, k_at + (k + 1) * SUB)
            d_p = dot(tile_ref[ROWS_AT + k_first + k, :, V_LANES], dt_ref[:, q_cols])
            made[q, k] = (d_p * tile_ref[len(PAIRS) + AT[q_first + q, k_first + k]].astype(F32)).astype(BF16)
        silu_copies[i].wait()
        for k in range(n):
            k_cols = slice(k_at + k * SUB, k_at + (k + 1) * SUB)
            d_v, d_k = [], []
            for q in range(n):
                if (q, k) in made:
                    q_cols = slice(q_at + q * SUB, q_at + (q + 1) * SUB)
                    d_v.append(dot(tile_ref[AT[q_first + q, k_first + k]], dn_ref[q_cols, :]))
                    d_k.append(dot(made[q, k], tile_ref[ROWS_AT + q_first + q, :, Q_LANES]))
            if q_at == k_at:
                dv_ref[k_cols, :], dk_ref[k_cols, :] = sum(d_v), sum(d_k)
            else:
                dv_ref[k_cols, :] += sum(d_v)
                dk_ref[k_cols, :] += sum(d_k)
        for q in range(n):
            q_cols = slice(q_at + q * SUB, q_at + (q + 1) * SUB)
            d_q = []
            for k in range(n):
                if (q, k) in made:
                    d_q.append(dot(x_ref[64:128, k_at + k * SUB : k_at + (k + 1) * SUB], made[q, k]))
            if k_at == 0:
                dq_ref[:, q_cols] = sum(d_q)
            else:
                dq_ref[:, q_cols] += sum(d_q)

    turned = []
    for b in range(N_BLOCKS):
        cols = slice(b * BLOCK, (b + 1) * BLOCK)
        turned.append(jnp.concatenate([dq_ref[:, cols] * 0.125, dk_ref[cols, :].T, dv_ref[cols, :].T], axis=0))
    turn_out(turned, turn, core, slot_ref, mine_ref, theirs_ref)


def prepare_kernel(
    q_in, k_in, v_in, u_in, cot_in, w_in, send_out, dg_out,
    q_ref, k_ref, v_ref, u_ref, cot_ref, w_ref, qkv_ref, g_ref, dg_ref, in_sems, w_sems, qkv_sems, g_sems, dg_sems,
):
    pairs = (q_in, q_ref), (k_in, k_ref), (v_in, v_ref), (cot_in, cot_ref), (u_in, u_ref)
    copies = [pltpu.make_async_copy(a, b, in_sems.at[i]) for i, (a, b) in enumerate(pairs)]
    parts = [pl.ds(at, 256) for at in range(0, WIDTH, 256)]
    w_copies = [pltpu.make_async_copy(w_in.at[part], w_ref.at[part], w_sems.at[i]) for i, part in enumerate(parts)]
    qkv_copies = [
        pltpu.make_async_copy(qkv_ref.at[i], send_out.at[:, pl.ds(i * 64, 64), :], qkv_sems.at[i]) for i in range(3)
    ]
    g_copies = [
        pltpu.make_async_copy(g_ref.at[pl.ds(i * 4, 4)], send_out.at[pl.ds(i * 4, 4), pl.ds(192, 64), :], g_sems.at[i])
        for i in range(4)
    ]
    dg_copies = [pltpu.make_async_copy(dg_ref.at[part], dg_out.at[part], dg_sems.at[i]) for i, part in enumerate(parts)]
    for copy in copies[3:] + w_copies + copies[:3]:
        copy.start()
    copies[3].wait()
    copies[4].wait()
    for i in range(4):
        cols = slice(i * 256, (i + 1) * 256)
        u_t = u_ref[:, cols].T
        w_copies[i].wait()
        d_gated = dot_nt(w_ref[cols, :], cot_ref[...])
        g_ref[i * 4 : (i + 1) * 4] = (d_gated * u_t.astype(F32)).astype(BF16).reshape(4, 64, BLOCK)
        g_copies[i].start()
        dg_ref[cols, :] = d_gated
        dg_copies[i].start()
    for i, ref in enumerate((q_ref, k_ref, v_ref)):
        copies[i].wait()
        for at in range(0, WIDTH, 256):
            qkv_ref[i, at // 64 : at // 64 + 4] = ref[:, at : at + 256].T.reshape(4, 64, BLOCK)
        qkv_copies[i].start()
    for copy in qkv_copies + g_copies + dg_copies:
        copy.wait()


def other_half_kernel(place_ref, got_ref, out_ref):
    core, begin = place_of(place_ref)[:2]
    for j in range(8):
        out_ref[j] = jnp.where(low_is_mine(j, core, begin), got_ref[8 + j], got_ref[j])


def to_owners_kernel(place_ref, mine_ref, theirs_ref, out_ref):
    core, begin = place_of(place_ref)[:2]
    for j in range(8):
        low_mine = low_is_mine(j, core, begin)
        mine, theirs = mine_ref[j], theirs_ref[j]
        out_ref[j] = jnp.where(low_mine, mine, theirs)
        out_ref[8 + j] = jnp.where(low_mine, theirs, mine)


def attn_to_owners_kernel(place_ref, mine_ref, theirs_ref, stat_ref, out, out_ref, sems):
    core, begin = place_of(place_ref)[:2]
    copies = [pltpu.make_async_copy(out_ref.at[j], out.at[j], sems.at[j]) for j in range(HEADS)]
    for j in range(8):
        low_mine = low_is_mine(j, core, begin)
        mine, theirs = mine_ref[j], theirs_ref[j]
        out_ref[j, 0:64, :] = jnp.where(low_mine, mine, theirs)
        out_ref[8 + j, 0:64, :] = jnp.where(low_mine, theirs, mine)
        for i in (j, 8 + j):
            out_ref[i, 64:, :] = stat_ref[...]
            copies[i].start()
    for copy in copies:
        copy.wait()


def normalised(got_ref):
    attn = got_ref[:, 0:64, :].astype(F32).reshape(WIDTH, BLOCK)
    centre = attn - jnp.mean(attn, axis=0, keepdims=True)
    return centre * lax.rsqrt(jnp.mean(centre * centre, axis=0, keepdims=True) + 1e-05)


def gated_kernel(place_ref, got_ref, u_ref, keep_ref, core_ref, z_ref, both_ref, half_ref):
    core, zl = place_ref[4], place_ref[5]
    gated = normalised(got_ref) * u_ref[...].T.astype(F32)
    for z in (0, 1, 4, 5):
        for chip in range(HEADS):
            at = z * BLOCK + chip * 8
            one, two = gated[at : at + 8], gated[at + 2 * BLOCK : at + 2 * BLOCK + 8]
            row = (z % 2) * 256 + chip * 16 + (z // 2) * 4
            rows = slice(row, row + 8)
            half_ref[0, rows, :] = jnp.concatenate([one[0:4], two[0:4]], axis=0)
            half_ref[1, rows, :] = jnp.concatenate([one[4:8], two[4:8]], axis=0)
    for c, z, out_ref in ((core, zl, keep_ref), (1 - core, zl, core_ref), (core, 1 - zl, z_ref), (1 - core, 1 - zl, both_ref)):
        out_ref[...] = half_ref[c, pl.ds(pl.multiple_of(z * 256, 256), 256), :].astype(BF16)


def d_gate_kernel(got_ref, dg_ref, after_ref, out_ref):
    d_gate = (dg_ref[...] * normalised(got_ref)).astype(BF16)
    for i in range(WIDTH // BLOCK):
        out_ref[:, i * BLOCK : (i + 1) * BLOCK] = d_gate[i * BLOCK : (i + 1) * BLOCK].T


def product_kernel(*refs):
    gated, cotangent, (out, out_ref, sems) = refs[0:4], refs[4:8], refs[8:]
    copies = []
    for i in range(2):
        rows = slice(i * 128, (i + 1) * 128)
        out_ref[rows, :] = sum(dot(a[rows, :], b[...]) for a, b in zip(gated, cotangent)).astype(BF16)
        part = pl.ds(i * 128, 128)
        copies.append(pltpu.make_async_copy(out_ref.at[part], out.at[part], sems.at[i]))
        copies[i].start()
    for copy in copies:
        copy.wait()


def finish_kernel(got_ref, dq_ref, dk_ref, dv_ref):
    for i, out_ref in enumerate((dq_ref, dk_ref, dv_ref)):
        for h in range(0, HEADS, 4):
            heads = got_ref[h : h + 4, i * 64 : (i + 1) * 64, :].reshape(256, BLOCK)
            out_ref[:, h * 64 : (h + 4) * 64] = heads.T


SMEM = pl.BlockSpec(memory_space=pltpu.SMEM)
VMEM = pl.BlockSpec(memory_space=pltpu.VMEM)
ANY = pl.BlockSpec(memory_space=pl.ANY)
DMA = pltpu.SemaphoreType.DMA


def call(kernel, name, out_shape, in_specs, args, scratch=(), out=VMEM, mib=8, flops=1 << 26, transcendentals=0):
    return pl.pallas_call(
        kernel,
        out_shape=out_shape,
        in_specs=in_specs,
        out_specs=jax.tree.map(lambda _: out, out_shape),
        scratch_shapes=list(scratch),
        compiler_params=pltpu.CompilerParams(vmem_limit_bytes=None if mib is None else mib * 1024 * 1024),
        cost_estimate=pl.CostEstimate(flops=flops, bytes_accessed=1 << 21, transcendentals=transcendentals),
        name=name,
    )(*args)


def shape(dims, dtype=BF16):
    return jax.ShapeDtypeStruct(dims, dtype)


def prepare(*args):
    return call(
        prepare_kernel,
        "prepare",
        (shape((HEADS, 256, BLOCK)), shape((WIDTH, BLOCK), F32)),
        [ANY] * 6,
        args,
        [pltpu.VMEM((BLOCK, WIDTH), BF16)] * 5
        + [
            pltpu.VMEM((WIDTH, WIDTH), BF16),
            pltpu.VMEM((3, HEADS, 64, BLOCK), BF16),
            pltpu.VMEM((HEADS, 64, BLOCK), BF16),
            pltpu.VMEM((WIDTH, BLOCK), F32),
        ]
        + [DMA((5,)), DMA((4,)), DMA((3,)), DMA((4,)), DMA((4,))],
        out=ANY,
        mib=None,
    )


def attend_forward(place, got, other):
    return call(
        forward_kernel,
        "attend_forward",
        (
            shape((320, HALF)),
            shape((8, HEAD_DIM, BLOCK)),
            shape((8, HEAD_DIM, BLOCK)),
            shape((STATS * N_BLOCKS, BLOCK)),
        ),
        [SMEM, VMEM, VMEM],
        (place, got, other),
        [
            pltpu.VMEM((HALF, HEAD_DIM), BF16),
            pltpu.VMEM((N_BLOCKS, 256, BLOCK), F32),
            pltpu.VMEM((STATS * N_BLOCKS, BLOCK), F32),
        ],
        mib=20,
        flops=1 << 30,
        transcendentals=1 << 22,
    )


def derive(place, x):
    tiles, rows = (ROWS_AT + HALF // SUB, SUB, SUB), (HALF, HEAD_DIM)
    return call(
        derive_kernel,
        "derive",
        shape(tiles),
        [SMEM, VMEM],
        (place, x),
        [pltpu.VMEM(tiles, BF16)]
        + [pltpu.VMEM(rows, BF16), DMA((2, len(GROUPS) + 1))],
        out=ANY,
        mib=TILES_MIB,
        flops=1 << 31,
        transcendentals=1 << 22,
    )


def attend_backward(place, x, got, derived):
    tiles, rows = (ROWS_AT + HALF // SUB, SUB, SUB), (HALF, HEAD_DIM)
    return call(
        backward_kernel,
        "attend_backward",
        (shape((8, 192, BLOCK)), shape((8, 192, BLOCK))),
        [SMEM, VMEM, VMEM, ANY],
        (place, x, got, derived),
        [pltpu.VMEM(tiles, BF16), pltpu.VMEM(rows, BF16)]
        + [
            pltpu.VMEM((HEAD_DIM, HALF), BF16),
            pltpu.VMEM((HEAD_DIM, HALF), F32),
            pltpu.VMEM(rows, F32),
            pltpu.VMEM(rows, F32),
            pltpu.VMEM((N_BLOCKS, 192, BLOCK), F32),
        ]
        + [DMA((2, len(GROUPS) + 1))],
        mib=TILES_MIB,
        flops=1 << 33,
    )


def on_device(query, key, value, gate_u, out_weight, cotangent, hist_lengths):
    core = lax.axis_index("core")
    place = jnp.concatenate([hist_lengths[0], core[None], lax.axis_index("zl")[None]]).astype(jnp.int32)

    def swap(x):
        return lax.ppermute(x, "core", SWAP)

    def chips(x):
        return lax.all_to_all(x, CHIP, 0, 0, tiled=True)

    send, d_gated_t = prepare(query, key, value, gate_u, cotangent, out_weight)
    got = chips(send)
    theirs = call(other_half_kernel, "other_half", shape((8, 256, BLOCK)), [SMEM, VMEM], (place, got))
    x, mine, theirs, stat = attend_forward(place, got, swap(theirs))

    rows = HEAD_DIM + STATS * N_BLOCKS
    send = call(
        attn_to_owners_kernel,
        "attn_to_owners",
        shape((HEADS, rows, BLOCK)),
        [SMEM] + [VMEM] * 3,
        (place, mine, swap(theirs), stat),
        [pltpu.VMEM((HEADS, rows, BLOCK), BF16), DMA((HEADS,))],
        out=ANY,
    )
    got_attn = chips(send)
    got_attn, derived = lax.optimization_barrier((got_attn, derive(place, x)))

    def four(parts):
        return [parts[0]] + [
            lax.ppermute(part, ("zl", "core"), [(i, i ^ step) for i in range(4)])
            for step, part in zip((1, 2, 3), parts[1:])
        ]

    gated = call(
        gated_kernel,
        "gated",
        (shape((256, BLOCK)),) * 4,
        [SMEM] + [VMEM] * 2,
        (place, got_attn, gate_u),
        [pltpu.VMEM((2, 512, BLOCK), F32)],
    )
    part = call(
        product_kernel,
        "product",
        shape((256, WIDTH)),
        [VMEM] * 8,
        four(gated) + four([cotangent] * 4),
        [pltpu.VMEM((256, WIDTH), BF16), DMA((2,))],
        out=ANY,
    )
    parts = chips(part.reshape(HEADS, 16, WIDTH))

    mine, theirs = attend_backward(place, x, got_attn, derived)
    send = call(
        to_owners_kernel,
        "grads_to_owners",
        shape((HEADS, 192, BLOCK)),
        [SMEM] + [VMEM] * 2,
        (place, mine, swap(theirs)),
    )
    got = chips(send)
    d_gate = call(
        d_gate_kernel,
        "d_gate",
        shape((BLOCK, WIDTH)),
        [VMEM, VMEM, ANY],
        (got_attn, d_gated_t, send),
        flops=1 << 20,
    )

    parts, _ = lax.optimization_barrier((parts, send))
    part = jnp.sum(parts.astype(F32), axis=0).reshape(4, 4, WIDTH)
    z = lax.axis_index("zh")
    for step in (2, 1):
        high = (z // step) % 2
        halves = part.reshape(2, step, 4, WIDTH)
        away = lax.dynamic_index_in_dim(halves, 1 - high, 0, keepdims=False)
        kept = lax.dynamic_index_in_dim(halves, high, 0, keepdims=False)
        part = kept + lax.ppermute(away, "zh", [(i, i ^ step) for i in range(4)])
    d_weight = part.reshape(4, WIDTH) * (1.0 / math.sqrt(32768))

    d_query, d_key, d_value = call(finish_kernel, "finish", (shape((BLOCK, WIDTH)),) * 3, [VMEM], (got,))
    return d_query, d_key, d_value, d_gate, d_weight


def solution(mesh):
    axes = ("zh", "zl", "x", "y", "core")
    inner = Mesh(mesh.devices.reshape(4, 2, 4, 4, 2), axes)
    rows = P(axes, None)
    return jax.shard_map(
        on_device,
        mesh=inner,
        in_specs=(rows, rows, rows, rows, P(), rows, P(("zh", "zl"), None)),
        out_specs=(rows, rows, rows, rows, rows),
        check_vma=False,
    )
```

```python
import math

import jax
import jax.numpy as jnp
from jax import lax
from jax.experimental import pallas as pl
from jax.experimental.pallas import tpu as pltpu
from jax.sharding import Mesh, PartitionSpec as P

HEADS = 16
HEAD_DIM = 64
WIDTH = HEADS * HEAD_DIM
N_BLOCKS = 16
BLOCK = 128
HALF = N_BLOCKS * BLOCK
SUB = 256
F_TILE = 2048
B_TILE = 1024
STATS = 5
TILES_MIB = 45
CHIP = ("x", "y")
SWAP = ((0, 1), (1, 0))
BF16 = jnp.bfloat16
F32 = jnp.float32


def dot(a, b):
    return lax.dot_general(a, b, (((1,), (0,)), ((), ())), preferred_element_type=F32)


def dot_nt(a, b):
    return lax.dot_general(a, b, (((1,), (1,)), ((), ())), preferred_element_type=F32)


def sigmoid(s):
    return pltpu.reciprocal(1.0 + jnp.exp(-s), approx=True)


def lanes():
    return lax.broadcasted_iota(jnp.int32, (1, BLOCK), 1)


def place_of(place_ref):
    first, second, third = (place_ref[i] for i in range(3))
    core = place_ref[4]
    is_first, is_second = first == HALF, second == HALF
    begin = jnp.where(is_first, 0, jnp.where(is_second, first, first + second + jnp.where(third == HALF, 0, third)))
    end1 = jnp.where(is_first, second, first)
    end2 = end1 + jnp.where(is_first | is_second, third, second)
    turn = jnp.where(core == 0, begin & (HALF - 1), 0)
    return core, begin, turn, jnp.where(core == 0, HALF, end1), jnp.where(core == 0, HALF, end2)


def low_is_mine(j, core, begin):
    return ((2 * j + core) * BLOCK + lanes() >= begin) == (core == 0)


def live_of(q_at, k_at, end1, end2, diagonal):
    q_place = q_at + lax.broadcasted_iota(jnp.int32, (1, SUB), 1)
    k_place = k_at + lax.broadcasted_iota(jnp.int32, (SUB, 1), 0)
    start = jnp.where(q_place < end1, 0, jnp.where(q_place < end2, end1, end2))
    live = k_place >= start
    return live & (k_place <= q_place) if diagonal else live


def below(n_tiles, tile):
    n_sub = tile // SUB
    for i in range(n_tiles):
        for j in range(i + 1):
            subs = [(q, k) for q in range(n_sub) for k in range(n_sub) if j < i or k <= q]
            yield i * tile, j * tile, subs


def forward_kernel(
    place_ref, got_ref, other_ref, x_ref, mine_ref, theirs_ref, stat_ref, k_ref, slot_ref, stats_ref
):
    core, begin, turn, end1, end2 = place_of(place_ref)
    whole, rest = turn // BLOCK, turn % BLOCK
    lane = lanes()
    for b in range(N_BLOCKS):
        j = b // 2
        mine = jnp.where(low_is_mine(j, core, begin), got_ref[j], got_ref[8 + j])
        here = jnp.where(core == b % 2, mine, other_ref[j])
        slot_ref[b] = pltpu.roll(here.astype(F32), lax.rem(BLOCK - rest, BLOCK), 1)
    for b in range(N_BLOCKS):
        first, second = slot_ref[lax.rem(b + whole, N_BLOCKS)], slot_ref[lax.rem(b + whole + 1, N_BLOCKS)]
        here = jnp.where(lane < BLOCK - rest, first, second)
        x_ref[0:64, b * BLOCK : (b + 1) * BLOCK] = (here[0:64] * 0.125).astype(BF16)
        x_ref[64:256, b * BLOCK : (b + 1) * BLOCK] = here[64:256].astype(BF16)
        k_ref[b * BLOCK : (b + 1) * BLOCK, :] = here[64:128].astype(BF16).T

    for q_at, k_at, subs in below(HALF // F_TILE, F_TILE):
        weights = {}
        for q, k in subs:
            q_sub, k_sub = q_at + q * SUB, k_at + k * SUB
            s = dot(k_ref[k_sub : k_sub + SUB, :], x_ref[0:64, q_sub : q_sub + SUB])
            live = live_of(q_sub, k_sub, end1, end2, q_sub == k_sub)
            weights[q, k] = jnp.where(live, s * sigmoid(s), 0.0).astype(BF16)
        for q in range(F_TILE // SUB):
            q_sub = q_at + q * SUB
            acc = jnp.zeros((HEAD_DIM, SUB), F32)
            for k in range(F_TILE // SUB):
                if (q, k) in weights:
                    k_sub = k_at + k * SUB
                    acc += dot(x_ref[128:192, k_sub : k_sub + SUB], weights[q, k])
            x_ref[256:320, q_sub : q_sub + SUB] = acc.astype(BF16)

    turned = []
    for b in range(N_BLOCKS):
        cols = slice(b * BLOCK, (b + 1) * BLOCK)
        attn = x_ref[256:320, cols].astype(F32)
        g = x_ref[192:256, cols].astype(F32)
        mean = jnp.mean(attn, axis=0, keepdims=True)
        centre = attn - mean
        both = jnp.sum(centre * g, axis=0, keepdims=True)
        mean_hi = mean.astype(BF16).astype(F32)
        square = jnp.sum(centre * centre, axis=0, keepdims=True)
        total = jnp.sum(g, axis=0, keepdims=True)
        for i, row in enumerate((mean_hi, mean - mean_hi, both, square, total)):
            stats_ref[i * N_BLOCKS + b : i * N_BLOCKS + b + 1, :] = row
        turned.append(attn)
    stat_ref[...] = stats_ref[...].astype(BF16)
    turn_out(turned, turn, core, slot_ref, mine_ref, theirs_ref)


def turn_out(blocks, turn, core, slot_ref, mine_ref, theirs_ref):
    whole, rest = turn // BLOCK, turn % BLOCK
    rows = blocks[0].shape[0]
    for b, block in enumerate(blocks):
        slot_ref[b, 0:rows, :] = pltpu.roll(block, rest, 1)
    from_this = lanes() >= rest
    for j in range(8):
        pair = []
        for b in (2 * j, 2 * j + 1):
            this = slot_ref[lax.rem(b - whole + N_BLOCKS, N_BLOCKS), 0:rows, :]
            last = slot_ref[lax.rem(b - whole + N_BLOCKS - 1, N_BLOCKS), 0:rows, :]
            pair.append(jnp.where(from_this, this, last).astype(BF16))
        mine_ref[j] = jnp.where(core == 0, pair[0], pair[1])
        theirs_ref[j] = jnp.where(core == 0, pair[1], pair[0])


GROUPS = [[(q_at // SUB + q, k_at // SUB + k) for q, k in subs] for q_at, k_at, subs in below(HALF // B_TILE, B_TILE)]
PAIRS = [pair for group in GROUPS for pair in group]
AT = {pair: i for i, pair in enumerate(PAIRS)}
ROWS_AT = 2 * len(PAIRS)
Q_LANES, V_LANES = slice(0, 64), slice(128, 192)


def group_copies(from_ref, to_ref, sems):
    silu, slope, at = [], [], 0
    for i, group in enumerate(GROUPS):
        for j, copies in enumerate((silu, slope)):
            part = pl.ds(j * len(PAIRS) + at, len(group))
            copies.append(pltpu.make_async_copy(from_ref.at[part], to_ref.at[part], sems.at[j, i]))
        at += len(group)
    part = pl.ds(ROWS_AT, HALF // SUB)
    return silu, slope, pltpu.make_async_copy(from_ref.at[part], to_ref.at[part], sems.at[0, len(GROUPS)])


def derive_kernel(
    place_ref, x_ref, tile_out, tile_ref, kn_ref, tile_sems
):
    end1, end2 = place_of(place_ref)[3:]
    for b in range(N_BLOCKS):
        cols = slice(b * BLOCK, (b + 1) * BLOCK)
        rows = slice((b % 2) * BLOCK, (b % 2 + 1) * BLOCK)
        tile_ref[ROWS_AT + b // 2, rows, Q_LANES] = x_ref[0:64, cols].T
        tile_ref[ROWS_AT + b // 2, rows, V_LANES] = x_ref[128:192, cols].T
        kn_ref[cols, :] = x_ref[64:128, cols].T
    silu_copies, slope_copies, rows_copy = group_copies(tile_ref, tile_out, tile_sems)
    rows_copy.start()
    for i, group in enumerate(GROUPS):
        for q, k in group:
            q_cols, k_cols = slice(q * SUB, (q + 1) * SUB), slice(k * SUB, (k + 1) * SUB)
            s = dot(kn_ref[k_cols, :], x_ref[0:64, q_cols])
            sigma = jnp.where(live_of(q * SUB, k * SUB, end1, end2, q == k), sigmoid(s), 0.0)
            silu = s * sigma
            tile_ref[AT[q, k]] = silu.astype(BF16)
            tile_ref[len(PAIRS) + AT[q, k]] = (sigma + silu * (1.0 - sigma)).astype(BF16)
        silu_copies[i].start()
        slope_copies[i].start()
    for copy in [rows_copy] + silu_copies + slope_copies:
        copy.wait()


def backward_kernel(
    place_ref, x_ref, got_ref, tile_in, mine_ref, theirs_ref,
    tile_ref, dn_ref, dt_ref, dq_ref, dk_ref, dv_ref, slot_ref,
    tile_sems,
):
    silu_copies, slope_copies, rows_copy = group_copies(tile_in, tile_ref, tile_sems)
    rows_copy.start()
    for i in range(len(GROUPS)):
        slope_copies[i].start()
        silu_copies[i].start()
    core, _, turn, end1, end2 = place_of(place_ref)
    stat = got_ref[:, 64 : 64 + STATS * N_BLOCKS, :].astype(F32).reshape(HEADS, STATS, N_BLOCKS, BLOCK)
    mean_h = stat[:, 0] + stat[:, 1]
    mean = jnp.mean(mean_h, axis=0)
    off = mean_h - mean[None]
    square = jnp.sum(stat[:, 3] + HEAD_DIM * off * off, axis=0)
    rstd = lax.rsqrt(square * (1.0 / WIDTH) + 1e-05)
    g_sum = stat[:, 4]
    g_mean = jnp.sum(g_sum, axis=0) * (1.0 / WIDTH)
    both = jnp.sum(stat[:, 2] + off * g_sum, axis=0) * rstd * (1.0 / WIDTH)
    for b in range(N_BLOCKS):
        cols = slice(b * BLOCK, (b + 1) * BLOCK)
        r = rstd[b : b + 1]
        normed = (x_ref[256:320, cols].astype(F32) - mean[b : b + 1]) * r
        d = (r * (x_ref[192:256, cols].astype(F32) - g_mean[b : b + 1] - normed * both[b : b + 1])).astype(BF16)
        dt_ref[:, cols] = d
        dn_ref[cols, :] = d.T

    rows_copy.wait()
    for i, (q_at, k_at, subs) in enumerate(below(HALF // B_TILE, B_TILE)):
        slope_copies[i].wait()
        n = B_TILE // SUB
        q_first, k_first = q_at // SUB, k_at // SUB
        made = {}
        for q, k in subs:
            q_cols = slice(q_at + q * SUB, q_at + (q + 1) * SUB)
            k_cols = slice(k_at + k * SUB, k_at + (k + 1) * SUB)
            d_p = dot(tile_ref[ROWS_AT + k_first + k, :, V_LANES], dt_ref[:, q_cols])
            made[q, k] = (d_p * tile_ref[len(PAIRS) + AT[q_first + q, k_first + k]].astype(F32)).astype(BF16)
        silu_copies[i].wait()
        for k in range(n):
            k_cols = slice(k_at + k * SUB, k_at + (k + 1) * SUB)
            d_v, d_k = [], []
            for q in range(n):
                if (q, k) in made:
                    q_cols = slice(q_at + q * SUB, q_at + (q + 1) * SUB)
                    d_v.append(dot(tile_ref[AT[q_first + q, k_first + k]], dn_ref[q_cols, :]))
                    d_k.append(dot(made[q, k], tile_ref[ROWS_AT + q_first + q, :, Q_LANES]))
            if q_at == k_at:
                dv_ref[k_cols, :], dk_ref[k_cols, :] = sum(d_v), sum(d_k)
            else:
                dv_ref[k_cols, :] += sum(d_v)
                dk_ref[k_cols, :] += sum(d_k)
        for q in range(n):
            q_cols = slice(q_at + q * SUB, q_at + (q + 1) * SUB)
            d_q = []
            for k in range(n):
                if (q, k) in made:
                    d_q.append(dot(x_ref[64:128, k_at + k * SUB : k_at + (k + 1) * SUB], made[q, k]))
            if k_at == 0:
                dq_ref[:, q_cols] = sum(d_q)
            else:
                dq_ref[:, q_cols] += sum(d_q)

    turned = []
    for b in range(N_BLOCKS):
        cols = slice(b * BLOCK, (b + 1) * BLOCK)
        turned.append(jnp.concatenate([dq_ref[:, cols] * 0.125, dk_ref[cols, :].T, dv_ref[cols, :].T], axis=0))
    turn_out(turned, turn, core, slot_ref, mine_ref, theirs_ref)


def prepare_kernel(
    q_in, k_in, v_in, u_in, cot_in, w_in, send_out, dg_out,
    q_ref, k_ref, v_ref, u_ref, cot_ref, w_ref, qkv_ref, g_ref, dg_ref, in_sems, w_sems, qkv_sems, g_sems, dg_sems,
):
    pairs = (q_in, q_ref), (k_in, k_ref), (v_in, v_ref), (cot_in, cot_ref), (u_in, u_ref)
    copies = [pltpu.make_async_copy(a, b, in_sems.at[i]) for i, (a, b) in enumerate(pairs)]
    parts = [pl.ds(at, 256) for at in range(0, WIDTH, 256)]
    w_copies = [pltpu.make_async_copy(w_in.at[part], w_ref.at[part], w_sems.at[i]) for i, part in enumerate(parts)]
    qkv_copies = [
        pltpu.make_async_copy(qkv_ref.at[i], send_out.at[:, pl.ds(i * 64, 64), :], qkv_sems.at[i]) for i in range(3)
    ]
    g_copies = [
        pltpu.make_async_copy(g_ref.at[pl.ds(i * 4, 4)], send_out.at[pl.ds(i * 4, 4), pl.ds(192, 64), :], g_sems.at[i])
        for i in range(4)
    ]
    dg_copies = [pltpu.make_async_copy(dg_ref.at[part], dg_out.at[part], dg_sems.at[i]) for i, part in enumerate(parts)]
    for copy in copies[3:] + w_copies + copies[:3]:
        copy.start()
    copies[3].wait()
    copies[4].wait()
    for i in range(4):
        cols = slice(i * 256, (i + 1) * 256)
        u_t = u_ref[:, cols].T
        w_copies[i].wait()
        d_gated = dot_nt(w_ref[cols, :], cot_ref[...])
        g_ref[i * 4 : (i + 1) * 4] = (d_gated * u_t.astype(F32)).astype(BF16).reshape(4, 64, BLOCK)
        g_copies[i].start()
        dg_ref[cols, :] = d_gated
        dg_copies[i].start()
    for i, ref in enumerate((q_ref, k_ref, v_ref)):
        copies[i].wait()
        for at in range(0, WIDTH, 256):
            qkv_ref[i, at // 64 : at // 64 + 4] = ref[:, at : at + 256].T.reshape(4, 64, BLOCK)
        qkv_copies[i].start()
    for copy in qkv_copies + g_copies + dg_copies:
        copy.wait()


def other_half_kernel(place_ref, got_ref, out_ref):
    core, begin = place_of(place_ref)[:2]
    for j in range(8):
        out_ref[j] = jnp.where(low_is_mine(j, core, begin), got_ref[8 + j], got_ref[j])


def to_owners_kernel(place_ref, mine_ref, theirs_ref, out_ref):
    core, begin = place_of(place_ref)[:2]
    for j in range(8):
        low_mine = low_is_mine(j, core, begin)
        mine, theirs = mine_ref[j], theirs_ref[j]
        out_ref[j] = jnp.where(low_mine, mine, theirs)
        out_ref[8 + j] = jnp.where(low_mine, theirs, mine)


def attn_to_owners_kernel(place_ref, mine_ref, theirs_ref, stat_ref, out, out_ref, sems):
    core, begin = place_of(place_ref)[:2]
    copies = [pltpu.make_async_copy(out_ref.at[j], out.at[j], sems.at[j]) for j in range(HEADS)]
    for j in range(8):
        low_mine = low_is_mine(j, core, begin)
        mine, theirs = mine_ref[j], theirs_ref[j]
        out_ref[j, 0:64, :] = jnp.where(low_mine, mine, theirs)
        out_ref[8 + j, 0:64, :] = jnp.where(low_mine, theirs, mine)
        for i in (j, 8 + j):
            out_ref[i, 64:, :] = stat_ref[...]
            copies[i].start()
    for copy in copies:
        copy.wait()


def normalised(got_ref):
    attn = got_ref[:, 0:64, :].astype(F32).reshape(WIDTH, BLOCK)
    centre = attn - jnp.mean(attn, axis=0, keepdims=True)
    return centre * lax.rsqrt(jnp.mean(centre * centre, axis=0, keepdims=True) + 1e-05)


def gated_kernel(place_ref, got_ref, u_ref, mine_ref, theirs_ref, half_ref):
    core = place_ref[4]
    gated = normalised(got_ref) * u_ref[...].T.astype(F32)
    for z in (0, 1, 4, 5):
        for chip in range(HEADS):
            at = z * BLOCK + chip * 8
            one, two = gated[at : at + 8], gated[at + 2 * BLOCK : at + 2 * BLOCK + 8]
            row = (z % 2) * 256 + chip * 16 + (z // 2) * 4
            rows = slice(row, row + 8)
            half_ref[0, rows, :] = jnp.concatenate([one[0:4], two[0:4]], axis=0)
            half_ref[1, rows, :] = jnp.concatenate([one[4:8], two[4:8]], axis=0)
    mine_ref[...] = half_ref[core].astype(BF16)
    theirs_ref[...] = half_ref[1 - core].astype(BF16)


def d_gate_kernel(got_ref, dg_ref, after_ref, out_ref):
    d_gate = (dg_ref[...] * normalised(got_ref)).astype(BF16)
    for i in range(WIDTH // BLOCK):
        out_ref[:, i * BLOCK : (i + 1) * BLOCK] = d_gate[i * BLOCK : (i + 1) * BLOCK].T


def product_kernel(*refs):
    gated, cotangent, (out, out_ref, sems) = refs[0:2], refs[2:4], refs[4:]
    copies = []
    for i in range(4):
        rows = slice(i * 128, (i + 1) * 128)
        out_ref[rows, :] = sum(dot(a[rows, :], b[...]) for a, b in zip(gated, cotangent)).astype(BF16)
        part = pl.ds(i * 128, 128)
        copies.append(pltpu.make_async_copy(out_ref.at[part], out.at[part], sems.at[i]))
        copies[i].start()
    for copy in copies:
        copy.wait()


def finish_kernel(got_ref, dq_ref, dk_ref, dv_ref):
    for i, out_ref in enumerate((dq_ref, dk_ref, dv_ref)):
        for h in range(0, HEADS, 4):
            heads = got_ref[h : h + 4, i * 64 : (i + 1) * 64, :].reshape(256, BLOCK)
            out_ref[:, h * 64 : (h + 4) * 64] = heads.T


SMEM = pl.BlockSpec(memory_space=pltpu.SMEM)
VMEM = pl.BlockSpec(memory_space=pltpu.VMEM)
ANY = pl.BlockSpec(memory_space=pl.ANY)
DMA = pltpu.SemaphoreType.DMA


def call(kernel, name, out_shape, in_specs, args, scratch=(), out=VMEM, mib=8, flops=1 << 26, transcendentals=0):
    return pl.pallas_call(
        kernel,
        out_shape=out_shape,
        in_specs=in_specs,
        out_specs=jax.tree.map(lambda _: out, out_shape),
        scratch_shapes=list(scratch),
        compiler_params=pltpu.CompilerParams(vmem_limit_bytes=None if mib is None else mib * 1024 * 1024),
        cost_estimate=pl.CostEstimate(flops=flops, bytes_accessed=1 << 21, transcendentals=transcendentals),
        name=name,
    )(*args)


def shape(dims, dtype=BF16):
    return jax.ShapeDtypeStruct(dims, dtype)


def prepare(*args):
    return call(
        prepare_kernel,
        "prepare",
        (shape((HEADS, 256, BLOCK)), shape((WIDTH, BLOCK), F32)),
        [ANY] * 6,
        args,
        [pltpu.VMEM((BLOCK, WIDTH), BF16)] * 5
        + [
            pltpu.VMEM((WIDTH, WIDTH), BF16),
            pltpu.VMEM((3, HEADS, 64, BLOCK), BF16),
            pltpu.VMEM((HEADS, 64, BLOCK), BF16),
            pltpu.VMEM((WIDTH, BLOCK), F32),
        ]
        + [DMA((5,)), DMA((4,)), DMA((3,)), DMA((4,)), DMA((4,))],
        out=ANY,
        mib=None,
    )


def attend_forward(place, got, other):
    return call(
        forward_kernel,
        "attend_forward",
        (
            shape((320, HALF)),
            shape((8, HEAD_DIM, BLOCK)),
            shape((8, HEAD_DIM, BLOCK)),
            shape((STATS * N_BLOCKS, BLOCK)),
        ),
        [SMEM, VMEM, VMEM],
        (place, got, other),
        [
            pltpu.VMEM((HALF, HEAD_DIM), BF16),
            pltpu.VMEM((N_BLOCKS, 256, BLOCK), F32),
            pltpu.VMEM((STATS * N_BLOCKS, BLOCK), F32),
        ],
        mib=20,
        flops=1 << 30,
        transcendentals=1 << 22,
    )


def derive(place, x):
    tiles, rows = (ROWS_AT + HALF // SUB, SUB, SUB), (HALF, HEAD_DIM)
    return call(
        derive_kernel,
        "derive",
        shape(tiles),
        [SMEM, VMEM],
        (place, x),
        [pltpu.VMEM(tiles, BF16)]
        + [pltpu.VMEM(rows, BF16), DMA((2, len(GROUPS) + 1))],
        out=ANY,
        mib=TILES_MIB,
        flops=1 << 31,
        transcendentals=1 << 22,
    )


def attend_backward(place, x, got, derived):
    tiles, rows = (ROWS_AT + HALF // SUB, SUB, SUB), (HALF, HEAD_DIM)
    return call(
        backward_kernel,
        "attend_backward",
        (shape((8, 192, BLOCK)), shape((8, 192, BLOCK))),
        [SMEM, VMEM, VMEM, ANY],
        (place, x, got, derived),
        [pltpu.VMEM(tiles, BF16), pltpu.VMEM(rows, BF16)]
        + [
            pltpu.VMEM((HEAD_DIM, HALF), BF16),
            pltpu.VMEM((HEAD_DIM, HALF), F32),
            pltpu.VMEM(rows, F32),
            pltpu.VMEM(rows, F32),
            pltpu.VMEM((N_BLOCKS, 192, BLOCK), F32),
        ]
        + [DMA((2, len(GROUPS) + 1))],
        mib=TILES_MIB,
        flops=1 << 33,
    )


def on_device(query, key, value, gate_u, out_weight, cotangent, hist_lengths):
    core = lax.axis_index("core")
    place = jnp.concatenate([hist_lengths[0], core[None]]).astype(jnp.int32)

    def swap(x):
        return lax.ppermute(x, "core", SWAP)

    def chips(x):
        return lax.all_to_all(x, CHIP, 0, 0, tiled=True)

    send, d_gated_t = prepare(query, key, value, gate_u, cotangent, out_weight)
    got = chips(send)
    theirs = call(other_half_kernel, "other_half", shape((8, 256, BLOCK)), [SMEM, VMEM], (place, got))
    x, mine, theirs, stat = attend_forward(place, got, swap(theirs))

    rows = HEAD_DIM + STATS * N_BLOCKS
    send = call(
        attn_to_owners_kernel,
        "attn_to_owners",
        shape((HEADS, rows, BLOCK)),
        [SMEM] + [VMEM] * 3,
        (place, mine, swap(theirs), stat),
        [pltpu.VMEM((HEADS, rows, BLOCK), BF16), DMA((HEADS,))],
        out=ANY,
    )
    got_attn = chips(send)
    got_attn, derived = lax.optimization_barrier((got_attn, derive(place, x)))

    mine, theirs = call(
        gated_kernel,
        "gated",
        (shape((512, BLOCK)),) * 2,
        [SMEM] + [VMEM] * 2,
        (place, got_attn, gate_u),
        [pltpu.VMEM((2, 512, BLOCK), F32)],
    )
    part = call(
        product_kernel,
        "product",
        shape((512, WIDTH)),
        [VMEM] * 4,
        (mine, swap(theirs), cotangent, swap(cotangent)),
        [pltpu.VMEM((512, WIDTH), BF16), DMA((4,))],
        out=ANY,
    )
    parts = lax.all_to_all(part.reshape(32, 16, WIDTH), ("zl",) + CHIP, 0, 0, tiled=True)

    mine, theirs = attend_backward(place, x, got_attn, derived)
    send = call(
        to_owners_kernel,
        "grads_to_owners",
        shape((HEADS, 192, BLOCK)),
        [SMEM] + [VMEM] * 2,
        (place, mine, swap(theirs)),
    )
    got = chips(send)
    d_gate = call(
        d_gate_kernel,
        "d_gate",
        shape((BLOCK, WIDTH)),
        [VMEM, VMEM, ANY],
        (got_attn, d_gated_t, send),
        flops=1 << 20,
    )

    parts, _ = lax.optimization_barrier((parts, send))
    part = jnp.sum(parts.astype(F32), axis=0).reshape(4, 4, WIDTH)
    z = lax.axis_index("zh")
    for step in (2, 1):
        high = (z // step) % 2
        halves = part.reshape(2, step, 4, WIDTH)
        away = lax.dynamic_index_in_dim(halves, 1 - high, 0, keepdims=False)
        kept = lax.dynamic_index_in_dim(halves, high, 0, keepdims=False)
        part = kept + lax.ppermute(away, "zh", [(i, i ^ step) for i in range(4)])
    d_weight = part.reshape(4, WIDTH) * (1.0 / math.sqrt(32768))

    d_query, d_key, d_value = call(finish_kernel, "finish", (shape((BLOCK, WIDTH)),) * 3, [VMEM], (got,))
    return d_query, d_key, d_value, d_gate, d_weight


def solution(mesh):
    axes = ("zh", "zl", "x", "y", "core")
    inner = Mesh(mesh.devices.reshape(4, 2, 4, 4, 2), axes)
    rows = P(axes, None)
    return jax.shard_map(
        on_device,
        mesh=inner,
        in_specs=(rows, rows, rows, rows, P(), rows, P(("zh", "zl"), None)),
        out_specs=(rows, rows, rows, rows, rows),
        check_vma=False,
    )
```

```python
import math

import jax
import jax.numpy as jnp
from jax import lax
from jax.experimental import pallas as pl
from jax.experimental.pallas import tpu as pltpu
from jax.sharding import Mesh, PartitionSpec as P

HEADS = 16
HEAD_DIM = 64
WIDTH = HEADS * HEAD_DIM
N_BLOCKS = 16
BLOCK = 128
HALF = N_BLOCKS * BLOCK
SUB = 256
F_TILE = 2048
B_TILE = 1024
STATS = 5
TILES_MIB = 45
CHIP = ("x", "y")
SWAP = ((0, 1), (1, 0))
BF16 = jnp.bfloat16
F32 = jnp.float32


def dot(a, b):
    return lax.dot_general(a, b, (((1,), (0,)), ((), ())), preferred_element_type=F32)


def dot_nt(a, b):
    return lax.dot_general(a, b, (((1,), (1,)), ((), ())), preferred_element_type=F32)


def sigmoid(s):
    return pltpu.reciprocal(1.0 + jnp.exp(-s), approx=True)


def lanes():
    return lax.broadcasted_iota(jnp.int32, (1, BLOCK), 1)


def place_of(place_ref):
    first, second, third = (place_ref[i] for i in range(3))
    core = place_ref[4]
    is_first, is_second = first == HALF, second == HALF
    begin = jnp.where(is_first, 0, jnp.where(is_second, first, first + second + jnp.where(third == HALF, 0, third)))
    end1 = jnp.where(is_first, second, first)
    end2 = end1 + jnp.where(is_first | is_second, third, second)
    turn = jnp.where(core == 0, begin & (HALF - 1), 0)
    return core, begin, turn, jnp.where(core == 0, HALF, end1), jnp.where(core == 0, HALF, end2)


def low_is_mine(j, core, begin):
    return ((2 * j + core) * BLOCK + lanes() >= begin) == (core == 0)


def live_of(q_at, k_at, end1, end2, diagonal):
    q_place = q_at + lax.broadcasted_iota(jnp.int32, (1, SUB), 1)
    k_place = k_at + lax.broadcasted_iota(jnp.int32, (SUB, 1), 0)
    start = jnp.where(q_place < end1, 0, jnp.where(q_place < end2, end1, end2))
    live = k_place >= start
    return live & (k_place <= q_place) if diagonal else live


def below(n_tiles, tile):
    n_sub = tile // SUB
    for i in range(n_tiles):
        for j in range(i + 1):
            subs = [(q, k) for q in range(n_sub) for k in range(n_sub) if j < i or k <= q]
            yield i * tile, j * tile, subs


def forward_kernel(
    place_ref, got_ref, other_ref, x_ref, mine_ref, theirs_ref, stat_ref, k_ref, slot_ref, stats_ref
):
    core, begin, turn, end1, end2 = place_of(place_ref)
    whole, rest = turn // BLOCK, turn % BLOCK
    lane = lanes()
    for b in range(N_BLOCKS):
        j = b // 2
        mine = jnp.where(low_is_mine(j, core, begin), got_ref[j], got_ref[8 + j])
        here = jnp.where(core == b % 2, mine, other_ref[j])
        slot_ref[b] = pltpu.roll(here.astype(F32), lax.rem(BLOCK - rest, BLOCK), 1)
    for b in range(N_BLOCKS):
        first, second = slot_ref[lax.rem(b + whole, N_BLOCKS)], slot_ref[lax.rem(b + whole + 1, N_BLOCKS)]
        here = jnp.where(lane < BLOCK - rest, first, second)
        x_ref[0:64, b * BLOCK : (b + 1) * BLOCK] = (here[0:64] * 0.125).astype(BF16)
        x_ref[64:256, b * BLOCK : (b + 1) * BLOCK] = here[64:256].astype(BF16)
        k_ref[b * BLOCK : (b + 1) * BLOCK, :] = here[64:128].astype(BF16).T

    for q_at, k_at, subs in below(HALF // F_TILE, F_TILE):
        weights = {}
        for q, k in subs:
            q_sub, k_sub = q_at + q * SUB, k_at + k * SUB
            s = dot(k_ref[k_sub : k_sub + SUB, :], x_ref[0:64, q_sub : q_sub + SUB])
            live = live_of(q_sub, k_sub, end1, end2, q_sub == k_sub)
            weights[q, k] = jnp.where(live, s * sigmoid(s), 0.0).astype(BF16)
        for q in range(F_TILE // SUB):
            q_sub = q_at + q * SUB
            acc = jnp.zeros((HEAD_DIM, SUB), F32)
            for k in range(F_TILE // SUB):
                if (q, k) in weights:
                    k_sub = k_at + k * SUB
                    acc += dot(x_ref[128:192, k_sub : k_sub + SUB], weights[q, k])
            x_ref[256:320, q_sub : q_sub + SUB] = acc.astype(BF16)

    turned = []
    for b in range(N_BLOCKS):
        cols = slice(b * BLOCK, (b + 1) * BLOCK)
        attn = x_ref[256:320, cols].astype(F32)
        g = x_ref[192:256, cols].astype(F32)
        mean = jnp.mean(attn, axis=0, keepdims=True)
        centre = attn - mean
        both = jnp.sum(centre * g, axis=0, keepdims=True)
        mean_hi = mean.astype(BF16).astype(F32)
        square = jnp.sum(centre * centre, axis=0, keepdims=True)
        total = jnp.sum(g, axis=0, keepdims=True)
        for i, row in enumerate((mean_hi, mean - mean_hi, both, square, total)):
            stats_ref[i * N_BLOCKS + b : i * N_BLOCKS + b + 1, :] = row
        turned.append(attn)
    stat_ref[...] = stats_ref[...].astype(BF16)
    turn_out(turned, turn, core, slot_ref, mine_ref, theirs_ref)


def turn_out(blocks, turn, core, slot_ref, mine_ref, theirs_ref):
    whole, rest = turn // BLOCK, turn % BLOCK
    rows = blocks[0].shape[0]
    for b, block in enumerate(blocks):
        slot_ref[b, 0:rows, :] = pltpu.roll(block, rest, 1)
    from_this = lanes() >= rest
    for j in range(8):
        pair = []
        for b in (2 * j, 2 * j + 1):
            this = slot_ref[lax.rem(b - whole + N_BLOCKS, N_BLOCKS), 0:rows, :]
            last = slot_ref[lax.rem(b - whole + N_BLOCKS - 1, N_BLOCKS), 0:rows, :]
            pair.append(jnp.where(from_this, this, last).astype(BF16))
        mine_ref[j] = jnp.where(core == 0, pair[0], pair[1])
        theirs_ref[j] = jnp.where(core == 0, pair[1], pair[0])


GROUPS = [[(q_at // SUB + q, k_at // SUB + k) for q, k in subs] for q_at, k_at, subs in below(HALF // B_TILE, B_TILE)]
PAIRS = [pair for group in GROUPS for pair in group]
AT = {pair: i for i, pair in enumerate(PAIRS)}
ROWS_AT = 2 * len(PAIRS)
Q_LANES, V_LANES = slice(0, 64), slice(128, 192)


def group_copies(from_ref, to_ref, sems):
    silu, slope, at = [], [], 0
    for i, group in enumerate(GROUPS):
        for j, copies in enumerate((silu, slope)):
            part = pl.ds(j * len(PAIRS) + at, len(group))
            copies.append(pltpu.make_async_copy(from_ref.at[part], to_ref.at[part], sems.at[j, i]))
        at += len(group)
    part = pl.ds(ROWS_AT, HALF // SUB)
    return silu, slope, pltpu.make_async_copy(from_ref.at[part], to_ref.at[part], sems.at[0, len(GROUPS)])


def derive_kernel(
    place_ref, x_ref, tile_out, tile_ref, kn_ref, tile_sems
):
    end1, end2 = place_of(place_ref)[3:]
    for b in range(N_BLOCKS):
        cols = slice(b * BLOCK, (b + 1) * BLOCK)
        rows = slice((b % 2) * BLOCK, (b % 2 + 1) * BLOCK)
        tile_ref[ROWS_AT + b // 2, rows, Q_LANES] = x_ref[0:64, cols].T
        tile_ref[ROWS_AT + b // 2, rows, V_LANES] = x_ref[128:192, cols].T
        kn_ref[cols, :] = x_ref[64:128, cols].T
    silu_copies, slope_copies, rows_copy = group_copies(tile_ref, tile_out, tile_sems)
    rows_copy.start()
    for i, group in enumerate(GROUPS):
        for q, k in group:
            q_cols, k_cols = slice(q * SUB, (q + 1) * SUB), slice(k * SUB, (k + 1) * SUB)
            s = dot(kn_ref[k_cols, :], x_ref[0:64, q_cols])
            sigma = jnp.where(live_of(q * SUB, k * SUB, end1, end2, q == k), sigmoid(s), 0.0)
            silu = s * sigma
            tile_ref[AT[q, k]] = silu.astype(BF16)
            tile_ref[len(PAIRS) + AT[q, k]] = (sigma + silu * (1.0 - sigma)).astype(BF16)
        silu_copies[i].start()
        slope_copies[i].start()
    for copy in [rows_copy] + silu_copies + slope_copies:
        copy.wait()


def backward_kernel(
    place_ref, x_ref, got_ref, tile_in, mine_ref, theirs_ref,
    tile_ref, dn_ref, dt_ref, dq_ref, dk_ref, dv_ref, slot_ref,
    tile_sems,
):
    silu_copies, slope_copies, rows_copy = group_copies(tile_in, tile_ref, tile_sems)
    rows_copy.start()
    for i in range(len(GROUPS)):
        slope_copies[i].start()
        silu_copies[i].start()
    core, _, turn, end1, end2 = place_of(place_ref)
    stat = got_ref[:, 64 : 64 + STATS * N_BLOCKS, :].astype(F32).reshape(HEADS, STATS, N_BLOCKS, BLOCK)
    mean_h = stat[:, 0] + stat[:, 1]
    mean = jnp.mean(mean_h, axis=0)
    off = mean_h - mean[None]
    square = jnp.sum(stat[:, 3] + HEAD_DIM * off * off, axis=0)
    rstd = lax.rsqrt(square * (1.0 / WIDTH) + 1e-05)
    g_sum = stat[:, 4]
    g_mean = jnp.sum(g_sum, axis=0) * (1.0 / WIDTH)
    both = jnp.sum(stat[:, 2] + off * g_sum, axis=0) * rstd * (1.0 / WIDTH)
    for b in range(N_BLOCKS):
        cols = slice(b * BLOCK, (b + 1) * BLOCK)
        r = rstd[b : b + 1]
        normed = (x_ref[256:320, cols].astype(F32) - mean[b : b + 1]) * r
        d = (r * (x_ref[192:256, cols].astype(F32) - g_mean[b : b + 1] - normed * both[b : b + 1])).astype(BF16)
        dt_ref[:, cols] = d
        dn_ref[cols, :] = d.T

    rows_copy.wait()
    for i, (q_at, k_at, subs) in enumerate(below(HALF // B_TILE, B_TILE)):
        slope_copies[i].wait()
        n = B_TILE // SUB
        q_first, k_first = q_at // SUB, k_at // SUB
        made = {}
        for q, k in subs:
            q_cols = slice(q_at + q * SUB, q_at + (q + 1) * SUB)
            k_cols = slice(k_at + k * SUB, k_at + (k + 1) * SUB)
            d_p = dot(tile_ref[ROWS_AT + k_first + k, :, V_LANES], dt_ref[:, q_cols])
            made[q, k] = (d_p * tile_ref[len(PAIRS) + AT[q_first + q, k_first + k]].astype(F32)).astype(BF16)
        silu_copies[i].wait()
        for k in range(n):
            k_cols = slice(k_at + k * SUB, k_at + (k + 1) * SUB)
            d_v, d_k = [], []
            for q in range(n):
                if (q, k) in made:
                    q_cols = slice(q_at + q * SUB, q_at + (q + 1) * SUB)
                    d_v.append(dot(tile_ref[AT[q_first + q, k_first + k]], dn_ref[q_cols, :]))
                    d_k.append(dot(made[q, k], tile_ref[ROWS_AT + q_first + q, :, Q_LANES]))
            if q_at == k_at:
                dv_ref[k_cols, :], dk_ref[k_cols, :] = sum(d_v), sum(d_k)
            else:
                dv_ref[k_cols, :] += sum(d_v)
                dk_ref[k_cols, :] += sum(d_k)
        for q in range(n):
            q_cols = slice(q_at + q * SUB, q_at + (q + 1) * SUB)
            d_q = []
            for k in range(n):
                if (q, k) in made:
                    d_q.append(dot(x_ref[64:128, k_at + k * SUB : k_at + (k + 1) * SUB], made[q, k]))
            if k_at == 0:
                dq_ref[:, q_cols] = sum(d_q)
            else:
                dq_ref[:, q_cols] += sum(d_q)

    turned = []
    for b in range(N_BLOCKS):
        cols = slice(b * BLOCK, (b + 1) * BLOCK)
        turned.append(jnp.concatenate([dq_ref[:, cols] * 0.125, dk_ref[cols, :].T, dv_ref[cols, :].T], axis=0))
    turn_out(turned, turn, core, slot_ref, mine_ref, theirs_ref)


def prepare_kernel(
    q_in, k_in, v_in, u_in, cot_in, w_in, send_out, dg_out,
    q_ref, k_ref, v_ref, u_ref, cot_ref, w_ref, qkv_ref, g_ref, dg_ref, in_sems, w_sems, qkv_sems, g_sems, dg_sems,
):
    pairs = (q_in, q_ref), (k_in, k_ref), (v_in, v_ref), (cot_in, cot_ref), (u_in, u_ref)
    copies = [pltpu.make_async_copy(a, b, in_sems.at[i]) for i, (a, b) in enumerate(pairs)]
    parts = [pl.ds(at, 256) for at in range(0, WIDTH, 256)]
    w_copies = [pltpu.make_async_copy(w_in.at[part], w_ref.at[part], w_sems.at[i]) for i, part in enumerate(parts)]
    qkv_copies = [
        pltpu.make_async_copy(qkv_ref.at[i], send_out.at[:, pl.ds(i * 64, 64), :], qkv_sems.at[i]) for i in range(3)
    ]
    g_copies = [
        pltpu.make_async_copy(g_ref.at[pl.ds(i * 4, 4)], send_out.at[pl.ds(i * 4, 4), pl.ds(192, 64), :], g_sems.at[i])
        for i in range(4)
    ]
    dg_copies = [pltpu.make_async_copy(dg_ref.at[part], dg_out.at[part], dg_sems.at[i]) for i, part in enumerate(parts)]
    for copy in copies[3:] + w_copies + copies[:3]:
        copy.start()
    copies[3].wait()
    copies[4].wait()
    for i in range(4):
        cols = slice(i * 256, (i + 1) * 256)
        u_t = u_ref[:, cols].T
        w_copies[i].wait()
        d_gated = dot_nt(w_ref[cols, :], cot_ref[...])
        g_ref[i * 4 : (i + 1) * 4] = (d_gated * u_t.astype(F32)).astype(BF16).reshape(4, 64, BLOCK)
        g_copies[i].start()
        dg_ref[cols, :] = d_gated
        dg_copies[i].start()
    for i, ref in enumerate((q_ref, k_ref, v_ref)):
        copies[i].wait()
        for at in range(0, WIDTH, 256):
            qkv_ref[i, at // 64 : at // 64 + 4] = ref[:, at : at + 256].T.reshape(4, 64, BLOCK)
        qkv_copies[i].start()
    for copy in qkv_copies + g_copies + dg_copies:
        copy.wait()


def other_half_kernel(place_ref, got_ref, out_ref):
    core, begin = place_of(place_ref)[:2]
    for j in range(8):
        out_ref[j] = jnp.where(low_is_mine(j, core, begin), got_ref[8 + j], got_ref[j])


def to_owners_kernel(place_ref, mine_ref, theirs_ref, out_ref):
    core, begin = place_of(place_ref)[:2]
    for j in range(8):
        low_mine = low_is_mine(j, core, begin)
        mine, theirs = mine_ref[j], theirs_ref[j]
        out_ref[j] = jnp.where(low_mine, mine, theirs)
        out_ref[8 + j] = jnp.where(low_mine, theirs, mine)


def attn_to_owners_kernel(place_ref, mine_ref, theirs_ref, stat_ref, out, out_ref, sems):
    core, begin = place_of(place_ref)[:2]
    copies = [pltpu.make_async_copy(out_ref.at[j], out.at[j], sems.at[j]) for j in range(HEADS)]
    for j in range(8):
        low_mine = low_is_mine(j, core, begin)
        mine, theirs = mine_ref[j], theirs_ref[j]
        out_ref[j, 0:64, :] = jnp.where(low_mine, mine, theirs)
        out_ref[8 + j, 0:64, :] = jnp.where(low_mine, theirs, mine)
        for i in (j, 8 + j):
            out_ref[i, 64:, :] = stat_ref[...]
            copies[i].start()
    for copy in copies:
        copy.wait()


def normalised(got_ref):
    attn = got_ref[:, 0:64, :].astype(F32).reshape(WIDTH, BLOCK)
    centre = attn - jnp.mean(attn, axis=0, keepdims=True)
    return centre * lax.rsqrt(jnp.mean(centre * centre, axis=0, keepdims=True) + 1e-05)


def gated_kernel(place_ref, got_ref, u_ref, mine_ref, theirs_ref, half_ref):
    core = place_ref[4]
    gated = normalised(got_ref) * u_ref[...].T.astype(F32)
    for z in (0, 1, 4, 5):
        for chip in range(HEADS):
            at = z * BLOCK + chip * 8
            one, two = gated[at : at + 8], gated[at + 2 * BLOCK : at + 2 * BLOCK + 8]
            row = (z % 2) * 256 + chip * 16 + (z // 2) * 4
            rows = slice(row, row + 8)
            half_ref[0, rows, :] = jnp.concatenate([one[0:4], two[0:4]], axis=0)
            half_ref[1, rows, :] = jnp.concatenate([one[4:8], two[4:8]], axis=0)
    mine_ref[...] = half_ref[core].astype(BF16)
    theirs_ref[...] = half_ref[1 - core].astype(BF16)


def d_gate_kernel(got_ref, dg_ref, after_ref, out_ref):
    d_gate = (dg_ref[...] * normalised(got_ref)).astype(BF16)
    for i in range(WIDTH // BLOCK):
        out_ref[:, i * BLOCK : (i + 1) * BLOCK] = d_gate[i * BLOCK : (i + 1) * BLOCK].T


def product_kernel(*refs):
    gated, cotangent, (out, out_ref, sems) = refs[0:2], refs[2:4], refs[4:]
    copies = []
    for i in range(4):
        rows = slice(i * 128, (i + 1) * 128)
        out_ref[rows, :] = sum(dot(a[rows, :], b[...]) for a, b in zip(gated, cotangent)).astype(BF16)
        part = pl.ds(i * 128, 128)
        copies.append(pltpu.make_async_copy(out_ref.at[part], out.at[part], sems.at[i]))
        copies[i].start()
    for copy in copies:
        copy.wait()


def finish_kernel(got_ref, dq_ref, dk_ref, dv_ref):
    for i, out_ref in enumerate((dq_ref, dk_ref, dv_ref)):
        for h in range(0, HEADS, 4):
            heads = got_ref[h : h + 4, i * 64 : (i + 1) * 64, :].reshape(256, BLOCK)
            out_ref[:, h * 64 : (h + 4) * 64] = heads.T


SMEM = pl.BlockSpec(memory_space=pltpu.SMEM)
VMEM = pl.BlockSpec(memory_space=pltpu.VMEM)
ANY = pl.BlockSpec(memory_space=pl.ANY)
DMA = pltpu.SemaphoreType.DMA


def call(kernel, name, out_shape, in_specs, args, scratch=(), out=VMEM, mib=8, flops=1 << 26, transcendentals=0):
    return pl.pallas_call(
        kernel,
        out_shape=out_shape,
        in_specs=in_specs,
        out_specs=jax.tree.map(lambda _: out, out_shape),
        scratch_shapes=list(scratch),
        compiler_params=pltpu.CompilerParams(vmem_limit_bytes=None if mib is None else mib * 1024 * 1024),
        cost_estimate=pl.CostEstimate(flops=flops, bytes_accessed=1 << 21, transcendentals=transcendentals),
        name=name,
    )(*args)


def shape(dims, dtype=BF16):
    return jax.ShapeDtypeStruct(dims, dtype)


def prepare(*args):
    return call(
        prepare_kernel,
        "prepare",
        (shape((HEADS, 256, BLOCK)), shape((WIDTH, BLOCK), F32)),
        [ANY] * 6,
        args,
        [pltpu.VMEM((BLOCK, WIDTH), BF16)] * 5
        + [
            pltpu.VMEM((WIDTH, WIDTH), BF16),
            pltpu.VMEM((3, HEADS, 64, BLOCK), BF16),
            pltpu.VMEM((HEADS, 64, BLOCK), BF16),
            pltpu.VMEM((WIDTH, BLOCK), F32),
        ]
        + [DMA((5,)), DMA((4,)), DMA((3,)), DMA((4,)), DMA((4,))],
        out=ANY,
        mib=None,
    )


def attend_forward(place, got, other):
    return call(
        forward_kernel,
        "attend_forward",
        (
            shape((320, HALF)),
            shape((8, HEAD_DIM, BLOCK)),
            shape((8, HEAD_DIM, BLOCK)),
            shape((STATS * N_BLOCKS, BLOCK)),
        ),
        [SMEM, VMEM, VMEM],
        (place, got, other),
        [
            pltpu.VMEM((HALF, HEAD_DIM), BF16),
            pltpu.VMEM((N_BLOCKS, 256, BLOCK), F32),
            pltpu.VMEM((STATS * N_BLOCKS, BLOCK), F32),
        ],
        mib=20,
        flops=1 << 30,
        transcendentals=1 << 22,
    )


def derive(place, x):
    tiles, rows = (ROWS_AT + HALF // SUB, SUB, SUB), (HALF, HEAD_DIM)
    return call(
        derive_kernel,
        "derive",
        shape(tiles),
        [SMEM, VMEM],
        (place, x),
        [pltpu.VMEM(tiles, BF16)]
        + [pltpu.VMEM(rows, BF16), DMA((2, len(GROUPS) + 1))],
        out=ANY,
        mib=TILES_MIB,
        flops=1 << 31,
        transcendentals=1 << 22,
    )


def attend_backward(place, x, got, derived):
    tiles, rows = (ROWS_AT + HALF // SUB, SUB, SUB), (HALF, HEAD_DIM)
    return call(
        backward_kernel,
        "attend_backward",
        (shape((8, 192, BLOCK)), shape((8, 192, BLOCK))),
        [SMEM, VMEM, VMEM, ANY],
        (place, x, got, derived),
        [pltpu.VMEM(tiles, BF16), pltpu.VMEM(rows, BF16)]
        + [
            pltpu.VMEM((HEAD_DIM, HALF), BF16),
            pltpu.VMEM((HEAD_DIM, HALF), F32),
            pltpu.VMEM(rows, F32),
            pltpu.VMEM(rows, F32),
            pltpu.VMEM((N_BLOCKS, 192, BLOCK), F32),
        ]
        + [DMA((2, len(GROUPS) + 1))],
        mib=TILES_MIB,
        flops=1 << 33,
    )


def on_device(query, key, value, gate_u, out_weight, cotangent, hist_lengths):
    core = lax.axis_index("core")
    place = jnp.concatenate([hist_lengths[0], core[None]]).astype(jnp.int32)

    def swap(x):
        return lax.ppermute(x, "core", SWAP)

    def chips(x):
        return lax.all_to_all(x, CHIP, 0, 0, tiled=True)

    send, d_gated_t = prepare(query, key, value, gate_u, cotangent, out_weight)
    got = chips(send)
    theirs = call(other_half_kernel, "other_half", shape((8, 256, BLOCK)), [SMEM, VMEM], (place, got))
    x, mine, theirs, stat = attend_forward(place, got, swap(theirs))

    rows = HEAD_DIM + STATS * N_BLOCKS
    send = call(
        attn_to_owners_kernel,
        "attn_to_owners",
        shape((HEADS, rows, BLOCK)),
        [SMEM] + [VMEM] * 3,
        (place, mine, swap(theirs), stat),
        [pltpu.VMEM((HEADS, rows, BLOCK), BF16), DMA((HEADS,))],
        out=ANY,
    )
    got_attn = chips(send)
    got_attn, derived = lax.optimization_barrier((got_attn, derive(place, x)))

    mine, theirs = call(
        gated_kernel,
        "gated",
        (shape((512, BLOCK)),) * 2,
        [SMEM] + [VMEM] * 2,
        (place, got_attn, gate_u),
        [pltpu.VMEM((2, 512, BLOCK), F32)],
    )
    part = call(
        product_kernel,
        "product",
        shape((512, WIDTH)),
        [VMEM] * 4,
        (mine, swap(theirs), cotangent, swap(cotangent)),
        [pltpu.VMEM((512, WIDTH), BF16), DMA((4,))],
        out=ANY,
    )
    parts = lax.all_to_all(part.reshape(32, 16, WIDTH), ("zl",) + CHIP, 0, 0, tiled=True)

    mine, theirs = attend_backward(place, x, got_attn, derived)
    send = call(
        to_owners_kernel,
        "grads_to_owners",
        shape((HEADS, 192, BLOCK)),
        [SMEM] + [VMEM] * 2,
        (place, mine, swap(theirs)),
    )
    d_gate = call(
        d_gate_kernel,
        "d_gate",
        shape((BLOCK, WIDTH)),
        [VMEM, VMEM, ANY],
        (got_attn, d_gated_t, send),
        flops=1 << 20,
    )
    send, d_gate = lax.optimization_barrier((send, d_gate))
    got = chips(send)

    parts, _ = lax.optimization_barrier((parts, send))
    part = jnp.sum(parts.astype(F32), axis=0).reshape(4, 4, WIDTH)
    z = lax.axis_index("zh")
    for step in (2, 1):
        high = (z // step) % 2
        halves = part.reshape(2, step, 4, WIDTH)
        away = lax.dynamic_index_in_dim(halves, 1 - high, 0, keepdims=False)
        kept = lax.dynamic_index_in_dim(halves, high, 0, keepdims=False)
        part = kept + lax.ppermute(away, "zh", [(i, i ^ step) for i in range(4)])
    d_weight = part.reshape(4, WIDTH) * (1.0 / math.sqrt(32768))

    d_query, d_key, d_value = call(finish_kernel, "finish", (shape((BLOCK, WIDTH)),) * 3, [VMEM], (got,))
    return d_query, d_key, d_value, d_gate, d_weight


def solution(mesh):
    axes = ("zh", "zl", "x", "y", "core")
    inner = Mesh(mesh.devices.reshape(4, 2, 4, 4, 2), axes)
    rows = P(axes, None)
    return jax.shard_map(
        on_device,
        mesh=inner,
        in_specs=(rows, rows, rows, rows, P(), rows, P(("zh", "zl"), None)),
        out_specs=(rows, rows, rows, rows, rows),
        check_vma=False,
    )
```
